512 devices in a mesh: sy: 32 (over x_lo, z), sx: 16 (over y, x_hi, core).
Axes of the slice: x: 4 (x_hi: 2, x_lo: 2; x = x_hi * 2 + x_lo), y: 4, z: 16, core: 2. Of those that a mesh axis runs over, the one named last changes fastest.
Arguments:
- object_field: float32 [2, 2, 4096, 2048], P(None, None, 'sy', 'sx'), may hold values from -6 to 6
- probe_modes: float32 [2, 4, 128, 128], replicated, may hold values from -5 to 5
- prop_taps: float32 [2, 2, 31], replicated, may hold values from -2 to 2
- measured: float32 [32, 16, 2, 128, 128], P('sy', 'sx'), may hold values from 0 to 2
- offsets: int32 [32, 16, 2, 2], P('sy', 'sx'), may hold values from 0 to 127
- counts: int32 [32, 16], P('sy', 'sx'), may hold values from 1 to 2, as said below
Outputs:
- object_grad: float32 [2, 2, 4096, 2048], P(None, None, 'sy', 'sx')
- probe_grad: float32 [2, 4, 128, 128], replicated
The draws below stay inside these ranges and needn't reach their ends.
Inputs may be any that keep to these rules, and one draw needn't show every extreme that they name: Slots j < counts of a tile are live, the others unused; in every draw some tile has all 2 slots live.
All inputs are finite; a program needn't handle non-finite values.
Results may differ from the reference program's by a relative error of at most 0.0003.
Values sent between devices are 32-bit elements; how exact they have to be, the bound alone decides.
No kernel may reach another device: no remote copies, remote signals or barrier semaphores. Data moves between devices by JAX's collectives and lax.ppermute only.
A program may use at most 64 MiB of HBM per device.

```python
import math
import jax
import jax.numpy as jnp
from jax import lax

WINDOW = 128
MODES = 4
SLICES = 2
TAPS = 31
TILE = 128
SLOTS = 2
TILES_Y = 32
TILES_X = 16
TILES = 512
NY = 4096
NX = 2048


def draw_counts(key, part):
    key = jax.random.fold_in(key, 7)
    first_key, second_key, third_key = jax.random.split(key, 3)
    base_counts = jax.random.randint(first_key, (TILES_Y, TILES_X), 1, 3)
    heavy_tiles = jax.random.randint(second_key, (TILES_Y, TILES_X), 0, 8) == 0
    chosen = jax.random.randint(third_key, (), 0, TILES_Y * TILES_X)
    flat_index = jnp.arange(TILES_Y * TILES_X, dtype=jnp.int32).reshape(TILES_Y, TILES_X)
    heavy_tiles = heavy_tiles | (flat_index == chosen)
    return jnp.where(heavy_tiles, SLOTS, jnp.minimum(base_counts, SLOTS)).astype(jnp.int32)


def place_ends(result, rng, least, high):
    spot = [jax.random.randint(jax.random.fold_in(rng, axis), (), 0, length) for axis, length in enumerate(result.shape)]
    main_axis = result.shape.index(max(result.shape))
    beside = spot[:main_axis] + [(spot[main_axis] + 1) % result.shape[main_axis]] + spot[main_axis + 1:]
    return result.at[tuple(spot)].set(least).at[tuple(beside)].set(high)


def shard_levels(key, shape, cuts, least, largest):
    def one(dim, blocks):
        heights = jax.random.uniform(jax.random.fold_in(jax.random.fold_in(key, 6), dim), (blocks,), jnp.float32, least / len(cuts), largest / len(cuts))
        return jnp.repeat(jnp.exp(heights), shape[dim] // blocks).reshape((-1,) + (1,) * (len(shape) - dim - 1))

    level = one(*cuts[0])
    for cut in cuts[1:]:
        level = level * one(*cut)
    return level


def centred(own_key, shape, width, reach, cuts=(), held_as=jnp.bfloat16):
    array = width * jax.random.normal(own_key, shape, jnp.float32)
    if cuts:
        array = array * shard_levels(own_key, shape, cuts, -0.22, 0.18)
    return jnp.clip(array, -reach, reach).astype(held_as)


def setup_inputs(seed: int = 0) -> dict:
    arg_keys = jax.random.split(jax.random.key(seed), 7)
    return {
        "object_field": centred(arg_keys[0], (2, SLICES, NY, NX), 0.7, 6.0, ((2, 32), (3, 16)), jnp.float32),
        "probe_modes": centred(arg_keys[1], (2, MODES, WINDOW, WINDOW), 0.35, 5.0, (), jnp.float32),
        "prop_taps": centred(arg_keys[2], (2, 2, TAPS), ((2 * TAPS) ** -0.5), 2.0, (), jnp.float32),
        "measured": jnp.clip(2.0 * jax.random.uniform(arg_keys[3], (TILES_Y, TILES_X, SLOTS, WINDOW, WINDOW), jnp.float32) ** shard_levels(arg_keys[3], (TILES_Y, TILES_X, SLOTS, WINDOW, WINDOW), ((0, 32), (1, 16)), -0.2, 0.2), 0.0, 2.0),
        "offsets": place_ends(jax.random.randint(arg_keys[4], (TILES_Y, TILES_X, SLOTS, 2), 0, TILE), jax.random.fold_in(arg_keys[4], 1), 0, TILE - 1).astype(jnp.int32),
        "counts": draw_counts(jax.random.fold_in(arg_keys[6], 71), 0),
    }


HIGHEST_PRECISION = lax.Precision.HIGHEST

def band_matrix(taps_pair, extent):
    count_taps = taps_pair.shape[-1]
    tap_reach = count_taps // 2
    tap_index = lax.broadcasted_iota(jnp.int32, (count_taps, extent, extent), 0)
    row_index = lax.broadcasted_iota(jnp.int32, (count_taps, extent, extent), 1)
    col_index = lax.broadcasted_iota(jnp.int32, (count_taps, extent, extent), 2)
    select = col_index - row_index + tap_reach == tap_index
    real_part = lax.optimization_barrier(jnp.sum(jnp.where(select, taps_pair[0][:, None, None], 0.0), axis=0))
    imag_part = lax.optimization_barrier(jnp.sum(jnp.where(select, taps_pair[1][:, None, None], 0.0), axis=0))
    return (real_part, imag_part)

def operators(prop_taps, extent):
    row_real, row_imag = band_matrix(prop_taps[0], extent)
    col_real, col_imag = band_matrix(prop_taps[1], extent)
    left_op = jnp.stack([jnp.stack([row_real, -row_imag]), jnp.stack([row_imag, row_real])])
    right_op = jnp.stack([jnp.stack([col_real, col_imag]), jnp.stack([-col_imag, col_real])])
    return (left_op, right_op)

def propagate(wavefield, left_op, right_op):
    rows_done = jnp.einsum('abrk,bmkq->amrq', left_op, wavefield, precision=HIGHEST_PRECISION)
    return jnp.einsum('amrk,abqk->bmrq', rows_done, right_op, precision=HIGHEST_PRECISION)

def slot_loss(window, probe_modes, target, left_op, right_op):
    wavefield = probe_modes
    for layer_index in range(window.shape[1]):
        object_real = window[0, layer_index]
        object_imag = window[1, layer_index]
        modulated = jnp.stack([wavefield[0] * object_real - wavefield[1] * object_imag, wavefield[0] * object_imag + wavefield[1] * object_real])
        wavefield = propagate(modulated, left_op, right_op)
    intensity = lax.optimization_barrier(jnp.sum(wavefield[0] * wavefield[0] + wavefield[1] * wavefield[1], axis=0))
    return 0.5 * jnp.sum((intensity - target) ** 2)

def slot_gradients(window, probe_modes, target, weight, left_op, right_op):
    loss_value, pullback = jax.vjp(lambda window_in, probe_in: slot_loss(window_in, probe_in, target, left_op, right_op), window, probe_modes)
    return pullback(weight.astype(loss_value.dtype))

def reference(object_field, probe_modes, prop_taps, measured, offsets, counts):
    half_width = WINDOW // 2
    layers = object_field.shape[1]
    padded = jnp.pad(object_field, ((0, 0), (0, 0), (half_width, half_width), (half_width, half_width)))
    left_op, right_op = operators(prop_taps, WINDOW)
    flat_index = jnp.arange(TILES_Y * TILES_X * SLOTS, dtype=jnp.int32)
    tile_rows = flat_index // (TILES_X * SLOTS)
    tile_cols = flat_index // SLOTS % TILES_X
    slot_ids = flat_index % SLOTS
    row_starts = (tile_rows * TILE + offsets[..., 0].reshape(-1)).astype(jnp.int32)
    col_starts = (tile_cols * TILE + offsets[..., 1].reshape(-1)).astype(jnp.int32)
    live = slot_ids < counts.reshape(-1)[flat_index // SLOTS]
    targets = measured.reshape(-1, WINDOW, WINDOW)
    anchor = jnp.zeros((), jnp.int32)

    def advance(carry_state, inputs):
        grad_padded, probe_accum = carry_state
        row_start, col_start, target, is_live = inputs
        corner = (anchor, anchor, row_start, col_start)
        window = lax.dynamic_slice(padded, corner, (2, layers, WINDOW, WINDOW))

        def active(unused):
            return slot_gradients(window, probe_modes, target, jnp.ones((), padded.dtype), left_op, right_op)

        def inactive(unused):
            return (jnp.zeros_like(window), jnp.zeros_like(probe_modes))
        window_grad, probe_part = lax.cond(is_live, active, inactive, 0)
        current = lax.dynamic_slice(grad_padded, corner, window.shape)
        grad_padded = lax.dynamic_update_slice(grad_padded, current + window_grad, corner)
        return ((grad_padded, probe_accum + probe_part), None)
    start_state = (jnp.zeros_like(padded), jnp.zeros_like(probe_modes))
    final_state, unused = lax.scan(advance, start_state, (row_starts, col_starts, targets, live))
    grad_padded, probe_accum = final_state
    object_grad = grad_padded[:, :, half_width:half_width + NY, half_width:half_width + NX]
    probe_grad = probe_accum / math.sqrt(TILES)
    return (object_grad, probe_grad)
```

```python
import functools
import math

import jax
import jax.numpy as jnp
from jax import lax
from jax.experimental import pallas as pl
from jax.experimental.pallas import tpu as pltpu
from jax.sharding import Mesh
from jax.sharding import PartitionSpec as P

F32 = jnp.float32
BF16 = jnp.bfloat16
ROW_AXES = ("xl", "za", "zb")
COL_AXES = ("y", "xh", "core")
NEAR_AXES = ("xl", "zb", "y", "xh", "core")
FAR_AXES = ("za",)
VMEM_LIMIT = 40 * 1024 * 1024
TILE = 128
HALF = 64
VM = pl.BlockSpec(memory_space=pltpu.VMEM)
SM = pl.BlockSpec(memory_space=pltpu.SMEM)
FAR = pl.BlockSpec(memory_space=pltpu.HBM)


def call(kernel, out_shape, in_specs, *args, scratch=(), out_specs=None, flops=0, moved=0):
    out_shape = tuple(out_shape)
    return pl.pallas_call(
        kernel,
        out_shape=out_shape,
        in_specs=in_specs,
        out_specs=tuple(out_specs or [VM] * len(out_shape)),
        scratch_shapes=list(scratch),
        compiler_params=pltpu.CompilerParams(vmem_limit_bytes=VMEM_LIMIT),
        cost_estimate=pl.CostEstimate(flops=flops, bytes_accessed=moved, transcendentals=0),
    )(*args)


def low_lanes(shape):
    return lax.broadcasted_iota(jnp.int32, shape, len(shape) - 1) < HALF


def split(value):
    high = value.astype(BF16)
    return high, (value - high.astype(F32)).astype(BF16)


def pack_columns(real, imag):
    low = low_lanes(real.shape)
    turned = pltpu.roll(imag, HALF, 1)
    return jnp.where(low, turned, real), jnp.where(low, real, turned)


def unpack_columns(from_left, from_right):
    low = low_lanes(from_left.shape)
    real = jnp.where(low, from_right, from_left)
    imag = pltpu.roll(jnp.where(low, from_left, from_right), HALF, 1)
    return real, imag


def pack_kernel(tile, to_right, to_left, to_down, to_up):
    for s in range(2):
        to_right[s], to_left[s] = pack_columns(tile[s], tile[2 + s])
    for p in range(4):
        to_up[p] = tile[p, :HALF]
        to_down[p] = tile[p, HALF:]


def corners_kernel(from_left, from_right, beside, to_down, to_up):
    for s in range(2):
        for p, plane in zip((s, 2 + s), unpack_columns(from_left[s], from_right[s])):
            beside[p] = plane
            to_up[p] = plane[:HALF]
            to_down[p] = plane[HALF:]


def operator_kernel(taps, probe, measured, high, low, probe_near, measured_near):
    probe_near[...] = probe[...]
    measured_near[...] = measured[...]
    rows = lax.broadcasted_iota(jnp.int32, (TILE, TILE), 0)
    cols = lax.broadcasted_iota(jnp.int32, (TILE, TILE), 1)
    forward = cols - rows + 15
    backward = rows - cols + 15

    def band(axis, part, place):
        total = jnp.zeros((TILE, TILE), F32)
        for t in range(31):
            total = jnp.where(place == t, taps[axis * 62 + part * 31 + t], total)
        return total

    def put(index, blocks):
        for i in range(2):
            for j in range(2):
                h, l = split(blocks[i][j])
                where = (index, pl.ds(i * TILE, TILE), pl.ds(j * TILE, TILE))
                high[where] = h
                low[where] = l

    yr, yi = band(0, 0, forward), band(0, 1, forward)
    put(0, ((yr, -yi), (yi, yr)))
    yr, yi = band(0, 0, backward), band(0, 1, backward)
    put(2, ((yr, yi), (-yi, yr)))
    xr, xi = band(1, 0, backward), band(1, 1, backward)
    put(1, ((xr, xi), (-xi, xr)))
    xr, xi = band(1, 0, forward), band(1, 1, forward)
    put(3, ((xr, -xi), (xi, xr)))


def dot(a, b):
    return jnp.dot(a, b, preferred_element_type=F32)


def main_kernel(
    offsets, counts, tile, beside, above, below, above_beside, below_beside,
    probe, measured, op_high, op_low,
    grad_tile, grad_beside, grad_above, grad_below, probe_grad,
    object_ext, grad_ext, field_high, field_low, mid_high, mid_low, wave_one, wave_two,
):
    for p in range(4):
        for b, parts in enumerate(((above, tile, below), (above_beside, beside, below_beside))):
            object_ext[b, p, :HALF] = parts[0][p]
            object_ext[b, p, HALF:HALF + TILE] = parts[1][p]
            object_ext[b, p, HALF + TILE:] = parts[2][p]
    grad_ext[...] = jnp.zeros_like(grad_ext)

    def block(m):
        return slice(m * TILE, (m + 1) * TILE)

    def put_field(slot, m, real, imag):
        for c, value in enumerate((real, imag)):
            h, l = split(value)
            field_high[slot, block(c), block(m)] = h
            field_low[slot, block(c), block(m)] = l

    def propagate(slot, which, take):
        for n in range(2):
            cols = slice(n * 256, (n + 1) * 256)
            fh, fl = field_high[slot, :, cols], field_low[slot, :, cols]
            mid = dot(op_high[which], fh) + (dot(op_high[which], fl) + dot(op_low[which], fh))
            for k in range(2):
                for c in range(2):
                    h, l = split(mid[block(c), block(k)])
                    mid_high[slot, block(2 * n + k), block(c)] = h
                    mid_low[slot, block(2 * n + k), block(c)] = l
        for m in range(4):
            gh, gl = mid_high[slot, block(m)], mid_low[slot, block(m)]
            done = dot(gh, op_high[which + 1]) + (dot(gl, op_high[which + 1]) + dot(gh, op_low[which + 1]))
            take(m, done[:, :TILE], done[:, TILE:])

    for slot in range(2):
        u = offsets[2 * slot]
        v = offsets[2 * slot + 1]
        weight = jnp.where(slot < counts[0], 1.0, 0.0).astype(F32)

        def window(p):
            rows = [object_ext[b, p, pl.ds(u, TILE), :] for b in range(2)]
            return pltpu.roll(jnp.concatenate(rows, axis=1), lax.rem(320 - v, 256), 1)[:, :TILE]

        def spread(p, value):
            wide = jnp.concatenate([value, jnp.zeros_like(value)], axis=1)
            wide = pltpu.roll(wide, lax.rem(v + 192, 256), 1)
            for b in range(2):
                grad_ext[b, p, pl.ds(u, TILE), :] += wide[:, block(b)]

        o0r, o0i, o1r, o1i = window(0), window(2), window(1), window(3)
        for m in range(4):
            pr, pi = probe[m], probe[4 + m]
            put_field(slot, m, pr * o0r - pi * o0i, pr * o0i + pi * o0r)

        def after_first(m, wr, wi):
            wave_one[slot, m, 0] = wr
            wave_one[slot, m, 1] = wi
            put_field(slot, m, wr * o1r - wi * o1i, wr * o1i + wi * o1r)

        propagate(slot, 0, after_first)
        intensity = [None]

        def after_second(m, wr, wi):
            wave_two[slot, m, 0] = wr
            wave_two[slot, m, 1] = wi
            term = wr * wr + wi * wi
            intensity[0] = term if m == 0 else intensity[0] + term

        propagate(slot, 0, after_second)
        residual = (intensity[0] - measured[slot]) * (2.0 * weight)
        for m in range(4):
            put_field(slot, m, residual * wave_two[slot, m, 0], residual * wave_two[slot, m, 1])
        sums = [None, None]

        def add(index, value, m):
            sums[index] = value if m == 0 else sums[index] + value

        def after_third(m, hr, hi):
            wr, wi = wave_one[slot, m, 0], wave_one[slot, m, 1]
            add(0, wr * hr + wi * hi, m)
            add(1, wr * hi - wi * hr, m)
            put_field(slot, m, hr * o1r + hi * o1i, hi * o1r - hr * o1i)

        propagate(slot, 2, after_third)
        spread(1, sums[0])
        spread(3, sums[1])

        def after_fourth(m, hr, hi):
            pr, pi = probe[m], probe[4 + m]
            add(0, pr * hr + pi * hi, m)
            add(1, pr * hi - pi * hr, m)
            dr = hr * o0r + hi * o0i
            di = hi * o0r - hr * o0i
            if slot == 0:
                probe_grad[m] = dr
                probe_grad[4 + m] = di
            else:
                probe_grad[m] += dr
                probe_grad[4 + m] += di

        propagate(slot, 2, after_fourth)
        spread(0, sums[0])
        spread(2, sums[1])

    for p in range(4):
        grad_tile[p] = grad_ext[0, p, HALF:HALF + TILE]
        grad_beside[p] = grad_ext[1, p, HALF:HALF + TILE]
        for b in range(2):
            grad_above[b, p] = grad_ext[b, p, :HALF]
            grad_below[b, p] = grad_ext[b, p, HALF + TILE:]


def fold_rows_kernel(
    shares, grad_tile, grad_beside, from_up, from_down, spread_share, result, to_right, to_left
):
    share = jnp.sum(shares[...], axis=0)
    for i in range(spread_share.shape[0]):
        spread_share[i] = share
    low = low_lanes((TILE, TILE))
    for s in range(2):
        planes = []
        for p in (s, 2 + s):
            result[p, :HALF] = grad_tile[p, :HALF] + from_up[0, p]
            result[p, HALF:] = grad_tile[p, HALF:] + from_down[0, p]
            planes.append(
                jnp.concatenate(
                    [grad_beside[p, :HALF] + from_up[1, p], grad_beside[p, HALF:] + from_down[1, p]], axis=0
                )
            )
        real, imag = planes
        turned = pltpu.roll(imag, HALF, 1)
        to_right[s] = jnp.where(low, real, turned)
        to_left[s] = jnp.where(low, turned, real)


def fold_cols_kernel(scale, shares, part, from_left, from_right, spread_share, result):
    share = jnp.sum(shares[...], axis=0) * scale
    for i in range(spread_share.shape[0]):
        spread_share[i] = share
    low = low_lanes((TILE, TILE))
    for s in range(2):
        result[s] = part[s] + jnp.where(low, from_left[s], from_right[s])
        turned = pltpu.roll(jnp.where(low, from_right[s], from_left[s]), HALF, 1)
        result[2 + s] = part[2 + s] + turned


def finish_kernel(result, gathered, result_far, probe_far, sems):
    moves = [pltpu.make_async_copy(result.at[p], result_far.at[p], sems.at[p]) for p in range(4)]
    for i in range(4):
        part = pl.ds(256 * i, 256)
        moves.append(pltpu.make_async_copy(gathered.at[part], probe_far.at[part], sems.at[4 + i]))
    for move in moves:
        move.start()
    for move in moves:
        move.wait()


def shift_pairs(count):
    forward = [(i, i + 1) for i in range(count - 1)]
    return forward, [(b, a) for a, b in forward]


def f32(*shape):
    return jax.ShapeDtypeStruct(shape, F32)


def body(object_field, probe_modes, prop_taps, measured, offsets, counts):
    down, up = shift_pairs(lax.axis_size(ROW_AXES))
    right, left = shift_pairs(lax.axis_size(COL_AXES))
    tile = object_field.reshape(4, TILE, TILE)
    strip = f32(2, TILE, TILE)
    rim = f32(2, 4, HALF, TILE)
    planes = f32(4, TILE, TILE)

    half = f32(4, HALF, TILE)
    to_right, to_left, to_down, to_up = call(pack_kernel, (strip, strip, half, half), [VM], tile)
    from_left = lax.ppermute(to_right, COL_AXES, right)
    from_right = lax.ppermute(to_left, COL_AXES, left)
    above = lax.ppermute(to_down, ROW_AXES, down)
    below = lax.ppermute(to_up, ROW_AXES, up)
    ops = jax.ShapeDtypeStruct((4, 2 * TILE, 2 * TILE), BF16)
    op_high, op_low, probe, targets = call(
        operator_kernel, (ops, ops, f32(8, TILE, TILE), strip), [SM, VM, VM],
        prop_taps.reshape(-1), probe_modes.reshape(8, TILE, TILE), measured.reshape(2, TILE, TILE),
    )
    beside, to_down, to_up = call(
        corners_kernel, (planes, half, half), [VM] * 2, from_left, from_right
    )
    above_beside = lax.ppermute(to_down, ROW_AXES, down)
    below_beside = lax.ppermute(to_up, ROW_AXES, up)

    grad_tile, grad_beside, grad_above, grad_below, probe_part = call(
        main_kernel,
        (planes, planes, rim, rim, f32(8, TILE, TILE)),
        [SM, SM] + [VM] * 10,
        offsets.reshape(-1), counts.reshape(-1), tile, beside, above, below, above_beside, below_beside,
        probe, targets, op_high, op_low,
        scratch=[
            pltpu.VMEM((2, 4, 256, TILE), F32),
            pltpu.VMEM((2, 4, 256, TILE), F32),
            pltpu.VMEM((2, 256, 512), BF16),
            pltpu.VMEM((2, 256, 512), BF16),
            pltpu.VMEM((2, 512, 256), BF16),
            pltpu.VMEM((2, 512, 256), BF16),
            pltpu.VMEM((2, 4, 2, TILE, TILE), F32),
            pltpu.VMEM((2, 4, 2, TILE, TILE), F32),
        ],
        flops=3_200_000_000, moved=4_000_000,
    )

    near = lax.axis_size(NEAR_AXES)
    far = lax.axis_size(FAR_AXES)
    rows = 8 * TILE // near
    shares = lax.all_to_all(probe_part.reshape(near, rows, TILE), NEAR_AXES, 0, 0, tiled=True)
    from_down = lax.ppermute(grad_above, ROW_AXES, up)
    from_up = lax.ppermute(grad_below, ROW_AXES, down)
    spread_share, part, to_right, to_left = call(
        fold_rows_kernel, (f32(far, rows, TILE), planes, strip, strip), [VM] * 5,
        shares, grad_tile, grad_beside, from_up, from_down,
    )
    from_left = lax.ppermute(to_right, COL_AXES, right)
    from_right = lax.ppermute(to_left, COL_AXES, left)
    shares = lax.all_to_all(spread_share, FAR_AXES, 0, 0, tiled=True)
    spread_share, result = call(
        functools.partial(fold_cols_kernel, 1.0 / math.sqrt(near * far)),
        (f32(near, rows, TILE), planes), [VM] * 4, shares, part, from_left, from_right,
    )
    gathered = lax.all_to_all(spread_share, NEAR_AXES, 0, 0, tiled=True)
    result, probe_grad = call(
        finish_kernel, (planes, f32(8 * TILE, TILE)), [VM] * 2,
        result, gathered.reshape(8 * TILE, TILE),
        scratch=[pltpu.SemaphoreType.DMA((8,))], out_specs=[FAR, FAR],
    )
    return result.reshape(object_field.shape), probe_grad.reshape(probe_modes.shape)


def solution(mesh):
    fine = Mesh(mesh.devices.reshape(2, 8, 2, 4, 2, 2), ROW_AXES + COL_AXES)
    return jax.shard_map(
        body,
        mesh=fine,
        in_specs=(
            P(None, None, ROW_AXES, COL_AXES),
            P(),
            P(),
            P(ROW_AXES, COL_AXES, None, None, None),
            P(ROW_AXES, COL_AXES, None, None),
            P(ROW_AXES, COL_AXES),
        ),
        out_specs=(P(None, None, ROW_AXES, COL_AXES), P()),
        check_vma=False,
    )
```

```python
import functools
import math

import jax
import jax.numpy as jnp
from jax import lax
from jax.experimental import pallas as pl
from jax.experimental.pallas import tpu as pltpu
from jax.sharding import Mesh
from jax.sharding import PartitionSpec as P

F32 = jnp.float32
BF16 = jnp.bfloat16
ROW_AXES = ("xl", "za", "zb")
COL_AXES = ("y", "xh", "core")
NEAR_AXES = ("xl", "zb", "y", "xh", "core")
FAR_AXES = ("za",)
VMEM_LIMIT = 40 * 1024 * 1024
TILE = 128
HALF = 64
VM = pl.BlockSpec(memory_space=pltpu.VMEM)
SM = pl.BlockSpec(memory_space=pltpu.SMEM)
FAR = pl.BlockSpec(memory_space=pltpu.HBM)


def call(kernel, out_shape, in_specs, *args, scratch=(), out_specs=None, flops=0, moved=0):
    out_shape = tuple(out_shape)
    return pl.pallas_call(
        kernel,
        out_shape=out_shape,
        in_specs=in_specs,
        out_specs=tuple(out_specs or [VM] * len(out_shape)),
        scratch_shapes=list(scratch),
        compiler_params=pltpu.CompilerParams(vmem_limit_bytes=VMEM_LIMIT),
        cost_estimate=pl.CostEstimate(flops=flops, bytes_accessed=moved, transcendentals=0),
    )(*args)


def low_lanes(shape):
    return lax.broadcasted_iota(jnp.int32, shape, len(shape) - 1) < HALF


def split(value):
    high = value.astype(BF16)
    return high, (value - high.astype(F32)).astype(BF16)


def pack_kernel(tile, to_right, to_left, to_down, to_up, down_right, down_left, up_right, up_left):
    low = low_lanes((TILE, TILE))
    for s in range(2):
        real, imag = tile[s], tile[2 + s]
        turned = pltpu.roll(imag, HALF, 1)
        right = jnp.where(low, turned, real)
        left = jnp.where(low, real, turned)
        to_right[s], to_left[s] = right, left
        down_right[s], down_left[s] = right[HALF:], left[HALF:]
        up_right[s], up_left[s] = right[:HALF], left[:HALF]
    for p in range(4):
        to_up[p] = tile[p, :HALF]
        to_down[p] = tile[p, HALF:]


def operator_kernel(taps, probe, measured, ops, probe_near, measured_near, padded):
    probe_near[...] = probe[...]
    measured_near[...] = measured[...]
    padded[...] = jnp.zeros_like(padded)
    for axis in range(2):
        padded[2 * axis:2 * axis + 2, :31] = taps[axis]

    def band(index):
        line = jnp.broadcast_to(padded[index:index + 1, :], (TILE, 2 * TILE))
        return pltpu.roll(line, 2 * TILE - 15, 1, stride=1, stride_axis=0)[:, :TILE]

    def put(index, blocks):
        for i in range(2):
            for j in range(2):
                high, low = split(blocks[i][j])
                cols = slice(j * TILE, (j + 1) * TILE)
                ops[index, i * TILE:(i + 1) * TILE, cols] = high
                ops[index, (2 + i) * TILE:(3 + i) * TILE, cols] = low

    yr, yi = band(0), band(1)
    put(0, ((yr, -yi), (yi, yr)))
    yr, yi = yr.T, yi.T
    put(2, ((yr, yi), (-yi, yr)))
    xr, xi = band(2), band(3)
    put(3, ((xr, -xi), (xi, xr)))
    xr, xi = xr.T, xi.T
    put(1, ((xr, xi), (-xi, xr)))


def dot(a, b):
    return jnp.dot(a, b, preferred_element_type=F32)


def block(m):
    return slice(m * TILE, (m + 1) * TILE)


def main_kernel(
    offsets, counts, tile, above, below, from_left, from_right,
    above_left, above_right, below_left, below_right, probe, measured, ops,
    probe_grad, grad_tile, to_up, to_down, to_right, to_left, up_right, up_left, down_right, down_left,
    object_ext, grad_ext, field_high, field_low, mid_high, mid_low, wave_one, wave_two,
):
    for p in range(4):
        object_ext[0, p, :HALF] = above[p]
        object_ext[0, p, HALF:HALF + TILE] = tile[p]
        object_ext[0, p, HALF + TILE:] = below[p]
    for start, end, left, right in (
        (0, HALF, above_left, above_right),
        (HALF, HALF + TILE, from_left, from_right),
        (HALF + TILE, 2 * TILE, below_left, below_right),
    ):
        low = low_lanes((end - start, TILE))
        for s in range(2):
            object_ext[1, s, start:end] = jnp.where(low, right[s], left[s])
            object_ext[1, 2 + s, start:end] = pltpu.roll(jnp.where(low, left[s], right[s]), HALF, 1)
    grad_ext[...] = jnp.zeros_like(grad_ext)

    def put_field(slot, m, real, imag):
        for c, value in enumerate((real, imag)):
            high, low = split(value)
            field_high[slot, block(c), block(m)] = high
            field_low[slot, block(c), block(m)] = low

    def rows_done(slot, which):
        for n in range(2):
            cols = slice(n * 256, (n + 1) * 256)
            both = dot(ops[which], field_high[slot, :, cols])
            mid = both[:256] + (both[256:] + dot(ops[which, :256], field_low[slot, :, cols]))
            for k in range(2):
                for c in range(2):
                    high, low = split(mid[block(c), block(k)])
                    mid_high[slot, block(2 * n + k), block(c)] = high
                    mid_low[slot, block(2 * n + k), block(c)] = low

    def cols_done(slot, which, take):
        high, low = ops[which, :256], ops[which, 256:]
        done = dot(mid_high[slot], high) + (dot(mid_low[slot], high) + dot(mid_high[slot], low))
        for m in range(4):
            take(slot, m, done[block(m), :TILE], done[block(m), TILE:])

    def propagate(which, take):
        for slot in range(2):
            rows_done(slot, which)
        for slot in range(2):
            cols_done(slot, which + 1, take)

    def window(slot, p):
        rows = [object_ext[b, p, pl.ds(offsets[2 * slot], TILE), :] for b in range(2)]
        shift = lax.rem(320 - offsets[2 * slot + 1], 256)
        return pltpu.roll(jnp.concatenate(rows, axis=1), shift, 1)[:, :TILE]

    def spread(slot, p, value):
        wide = jnp.concatenate([value, jnp.zeros_like(value)], axis=1)
        wide = pltpu.roll(wide, lax.rem(offsets[2 * slot + 1] + 192, 256), 1)
        for b in range(2):
            grad_ext[b, p, pl.ds(offsets[2 * slot], TILE), :] += wide[:, block(b)]

    views = [[window(slot, p) for p in range(4)] for slot in range(2)]
    for slot in range(2):
        o0r, o0i = views[slot][0], views[slot][2]
        for m in range(4):
            pr, pi = probe[m], probe[4 + m]
            put_field(slot, m, pr * o0r - pi * o0i, pr * o0i + pi * o0r)

    def after_first(slot, m, wr, wi):
        o1r, o1i = views[slot][1], views[slot][3]
        wave_one[slot, m, 0] = wr
        wave_one[slot, m, 1] = wi
        put_field(slot, m, wr * o1r - wi * o1i, wr * o1i + wi * o1r)

    propagate(0, after_first)
    intensity = [None, None]

    def after_second(slot, m, wr, wi):
        wave_two[slot, m, 0] = wr
        wave_two[slot, m, 1] = wi
        term = wr * wr + wi * wi
        intensity[slot] = term if m == 0 else intensity[slot] + term
        if m == 3:
            weight = jnp.where(slot < counts[0], 2.0, 0.0).astype(F32)
            residual = (intensity[slot] - measured[slot]) * weight
            for k in range(4):
                put_field(slot, k, residual * wave_two[slot, k, 0], residual * wave_two[slot, k, 1])

    propagate(0, after_second)
    sums = [[None, None], [None, None]]

    def add(slot, m, real, imag):
        pair = (real, imag) if m == 0 else (sums[slot][0] + real, sums[slot][1] + imag)
        sums[slot] = pair

    def after_third(slot, m, hr, hi):
        o1r, o1i = views[slot][1], views[slot][3]
        wr, wi = wave_one[slot, m, 0], wave_one[slot, m, 1]
        add(slot, m, wr * hr + wi * hi, wr * hi - wi * hr)
        put_field(slot, m, hr * o1r + hi * o1i, hi * o1r - hr * o1i)
        if m == 3:
            spread(slot, 1, sums[slot][0])
            spread(slot, 3, sums[slot][1])

    propagate(2, after_third)

    def after_fourth(slot, m, hr, hi):
        o0r, o0i = views[slot][0], views[slot][2]
        pr, pi = probe[m], probe[4 + m]
        add(slot, m, pr * hr + pi * hi, pr * hi - pi * hr)
        dr = hr * o0r + hi * o0i
        di = hi * o0r - hr * o0i
        if slot == 0:
            probe_grad[m] = dr
            probe_grad[4 + m] = di
        else:
            probe_grad[m] += dr
            probe_grad[4 + m] += di
        if m == 3:
            spread(slot, 0, sums[slot][0])
            spread(slot, 2, sums[slot][1])

    propagate(2, after_fourth)
    for p in range(4):
        to_up[p] = grad_ext[0, p, :HALF]
        grad_tile[p] = grad_ext[0, p, HALF:HALF + TILE]
        to_down[p] = grad_ext[0, p, HALF + TILE:]
    for start, end, left, right in (
        (0, HALF, up_left, up_right),
        (HALF, HALF + TILE, to_left, to_right),
        (HALF + TILE, 2 * TILE, down_left, down_right),
    ):
        low = low_lanes((end - start, TILE))
        for s in range(2):
            real = grad_ext[1, s, start:end]
            turned = pltpu.roll(grad_ext[1, 2 + s, start:end], HALF, 1)
            right[s] = jnp.where(low, real, turned)
            left[s] = jnp.where(low, turned, real)


def share_kernel(scale, shares, spread_share):
    share = jnp.sum(shares[...], axis=0) * scale
    for i in range(spread_share.shape[0]):
        spread_share[i] = share


def fold_sides(tile, from_up, from_down, from_left, from_right, result):
    low = low_lanes((TILE, TILE))
    for s in range(2):
        left, right = from_left[s], from_right[s]
        sides = (jnp.where(low, left, right), pltpu.roll(jnp.where(low, right, left), HALF, 1))
        for p, side in zip((s, 2 + s), sides):
            result[p, :HALF] = tile[p, :HALF] + from_up[p] + side[:HALF]
            result[p, HALF:] = tile[p, HALF:] + from_down[p] + side[HALF:]


def fold_corners(tile, up_left, up_right, down_left, down_right, result):
    low = low_lanes((HALF, TILE))
    for s in range(2):
        for rows, left, right in (
            (slice(0, HALF), up_left[s], up_right[s]),
            (slice(HALF, TILE), down_left[s], down_right[s]),
        ):
            result[s, rows] = tile[s, rows] + jnp.where(low, left, right)
            turned = pltpu.roll(jnp.where(low, right, left), HALF, 1)
            result[2 + s, rows] = tile[2 + s, rows] + turned


def near_kernel(shares, tile, from_up, from_down, from_left, from_right, spread_share, result):
    share_kernel(1.0, shares, spread_share)
    fold_sides(tile, from_up, from_down, from_left, from_right, result)


def far_kernel(scale, shares, tile, up_left, up_right, down_left, down_right, spread_share, result):
    share_kernel(scale, shares, spread_share)
    fold_corners(tile, up_left, up_right, down_left, down_right, result)


def finish_kernel(result, gathered, result_far, probe_far, sems):
    moves = [pltpu.make_async_copy(result.at[p], result_far.at[p], sems.at[p]) for p in range(4)]
    for i in range(4):
        part = pl.ds(256 * i, 256)
        moves.append(pltpu.make_async_copy(gathered.at[part], probe_far.at[part], sems.at[4 + i]))
    for move in moves:
        move.start()
    for move in moves:
        move.wait()


def shift(value, down, right):
    height, width = lax.axis_size(ROW_AXES), lax.axis_size(COL_AXES)
    if right == 0:
        return lax.ppermute(value, ROW_AXES, [(i, i + down) for i in range(height) if 0 <= i + down < height])
    if down == 0:
        return lax.ppermute(value, COL_AXES, [(j, j + right) for j in range(width) if 0 <= j + right < width])
    pairs = [
        (i * width + j, (i + down) * width + j + right)
        for i in range(height)
        for j in range(width)
        if 0 <= i + down < height and 0 <= j + right < width
    ]
    return lax.ppermute(value, ROW_AXES + COL_AXES, pairs)


def f32(*shape):
    return jax.ShapeDtypeStruct(shape, F32)


def body(object_field, probe_modes, prop_taps, measured, offsets, counts):
    tile = object_field.reshape(4, TILE, TILE)
    planes, half = f32(4, TILE, TILE), f32(4, HALF, TILE)
    strip, corner = f32(2, TILE, TILE), f32(2, HALF, TILE)

    to_right, to_left, to_down, to_up, down_right, down_left, up_right, up_left = call(
        pack_kernel, (strip, strip, half, half) + (corner,) * 4, [VM], tile
    )
    from_left = shift(to_right, 0, 1)
    from_right = shift(to_left, 0, -1)
    above = shift(to_down, 1, 0)
    below = shift(to_up, -1, 0)
    above_left = shift(down_right, 1, 1)
    above_right = shift(down_left, 1, -1)
    below_left = shift(up_right, -1, 1)
    below_right = shift(up_left, -1, -1)
    ops, probe, targets = call(
        operator_kernel,
        (jax.ShapeDtypeStruct((4, 512, 256), BF16), f32(8, TILE, TILE), strip), [VM, VM, VM],
        prop_taps, probe_modes.reshape(8, TILE, TILE), measured.reshape(2, TILE, TILE),
        scratch=[pltpu.VMEM((8, 2 * TILE), F32)],
    )
    (
        probe_part, grad_tile, to_up, to_down, to_right, to_left,
        up_right, up_left, down_right, down_left,
    ) = call(
        main_kernel,
        (f32(8, TILE, TILE), planes, half, half, strip, strip) + (corner,) * 4,
        [SM, SM] + [VM] * 12,
        offsets.reshape(-1), counts.reshape(-1), tile, above, below, from_left, from_right,
        above_left, above_right, below_left, below_right, probe, targets, ops,
        scratch=[
            pltpu.VMEM((2, 4, 256, TILE), F32),
            pltpu.VMEM((2, 4, 256, TILE), F32),
            pltpu.VMEM((2, 256, 512), BF16),
            pltpu.VMEM((2, 256, 512), BF16),
            pltpu.VMEM((2, 512, 256), BF16),
            pltpu.VMEM((2, 512, 256), BF16),
            pltpu.VMEM((2, 4, 2, TILE, TILE), F32),
            pltpu.VMEM((2, 4, 2, TILE, TILE), F32),
        ],
        flops=3_200_000_000, moved=4_000_000,
    )

    near = lax.axis_size(NEAR_AXES)
    far = lax.axis_size(FAR_AXES)
    rows = 8 * TILE // near
    sides = (shift(to_down, 1, 0), shift(to_up, -1, 0), shift(to_right, 0, 1), shift(to_left, 0, -1))
    shares = lax.all_to_all(probe_part.reshape(near, rows, TILE), NEAR_AXES, 0, 0, tiled=True)
    spread_share, part = call(
        near_kernel, (f32(far, rows, TILE), planes), [VM] * 6, shares, grad_tile, *sides
    )
    shares = lax.all_to_all(spread_share, FAR_AXES, 0, 0, tiled=True)
    corners = (
        shift(down_right, 1, 1), shift(down_left, 1, -1), shift(up_right, -1, 1), shift(up_left, -1, -1)
    )
    spread_share, result = call(
        functools.partial(far_kernel, 1.0 / math.sqrt(near * far)),
        (f32(near, rows, TILE), planes), [VM] * 6, shares, part, *corners,
    )
    gathered = lax.all_to_all(spread_share, NEAR_AXES, 0, 0, tiled=True)
    result, probe_grad = call(
        finish_kernel, (planes, f32(8 * TILE, TILE)), [VM] * 2,
        result, gathered.reshape(8 * TILE, TILE),
        scratch=[pltpu.SemaphoreType.DMA((8,))], out_specs=[FAR, FAR],
    )
    return result.reshape(object_field.shape), probe_grad.reshape(probe_modes.shape)


def solution(mesh):
    fine = Mesh(mesh.devices.reshape(2, 8, 2, 4, 2, 2), ROW_AXES + COL_AXES)
    return jax.shard_map(
        body,
        mesh=fine,
        in_specs=(
            P(None, None, ROW_AXES, COL_AXES),
            P(),
            P(),
            P(ROW_AXES, COL_AXES, None, None, None),
            P(ROW_AXES, COL_AXES, None, None),
            P(ROW_AXES, COL_AXES),
        ),
        out_specs=(P(None, None, ROW_AXES, COL_AXES), P()),
        check_vma=False,
    )
```

```python
import functools
import math

import jax
import jax.numpy as jnp
from jax import lax
from jax.experimental import pallas as pl
from jax.experimental.pallas import tpu as pltpu
from jax.sharding import Mesh
from jax.sharding import PartitionSpec as P

F32 = jnp.float32
BF16 = jnp.bfloat16
ROW_AXES = ("xl", "za", "zb")
COL_AXES = ("y", "xh", "core")
NEAR_AXES = ("xl", "zb", "y", "xh", "core")
FAR_AXES = ("za",)
VMEM_LIMIT = 40 * 1024 * 1024
TILE = 128
HALF = 64
VM = pl.BlockSpec(memory_space=pltpu.VMEM)
SM = pl.BlockSpec(memory_space=pltpu.SMEM)
FAR = pl.BlockSpec(memory_space=pltpu.HBM)


def call(kernel, out_shape, in_specs, *args, scratch=(), out_specs=None, flops=0, moved=0):
    out_shape = tuple(out_shape)
    return pl.pallas_call(
        kernel,
        out_shape=out_shape,
        in_specs=in_specs,
        out_specs=tuple(out_specs or [VM] * len(out_shape)),
        scratch_shapes=list(scratch),
        compiler_params=pltpu.CompilerParams(vmem_limit_bytes=VMEM_LIMIT),
        cost_estimate=pl.CostEstimate(flops=flops, bytes_accessed=moved, transcendentals=0),
    )(*args)


def low_lanes(shape):
    return lax.broadcasted_iota(jnp.int32, shape, len(shape) - 1) < HALF


def split(value):
    high = value.astype(BF16)
    return high, (value - high.astype(F32)).astype(BF16)


def even_column():
    return lax.axis_index("core") == 0


def even_row():
    return lax.axis_index("zb") == 0


def by_parity(even, first, second):
    return jnp.where(even, first, second), jnp.where(even, second, first)


def pack_kernel(tile, cross, mate):
    low = low_lanes((TILE, TILE))
    even = even_column()
    for s in range(2):
        turned = pltpu.roll(tile[2 + s], HALF, 1)
        to_right = jnp.where(low, turned, tile[s])
        to_left = jnp.where(low, tile[s], turned)
        mate[s], cross[s] = by_parity(even, to_right, to_left)


def rows_kernel(tile, from_cross, from_mate, beside, cross, mate):
    low = low_lanes((TILE, TILE))
    even = even_column()
    for s in range(2):
        from_right, from_left = by_parity(even, from_mate[s], from_cross[s])
        beside[s] = jnp.where(low, from_right, from_left)
        beside[2 + s] = pltpu.roll(jnp.where(low, from_left, from_right), HALF, 1)
    even = even_row()
    for b, plane in enumerate((tile, beside)):
        for p in range(4):
            mate[b, p], cross[b, p] = by_parity(even, plane[p, HALF:], plane[p, :HALF])


def operator_kernel(taps, probe, measured, ops, probe_near, measured_near, padded):
    probe_near[...] = probe[...]
    measured_near[...] = measured[...]
    padded[...] = jnp.zeros_like(padded)
    for axis in range(2):
        padded[2 * axis:2 * axis + 2, :31] = taps[axis]

    def band(index):
        line = jnp.broadcast_to(padded[index:index + 1, :], (TILE, 2 * TILE))
        return pltpu.roll(line, 2 * TILE - 15, 1, stride=1, stride_axis=0)[:, :TILE]

    def put(index, blocks):
        for i in range(2):
            for j in range(2):
                high, low = split(blocks[i][j])
                cols = slice(j * TILE, (j + 1) * TILE)
                ops[index, i * TILE:(i + 1) * TILE, cols] = high
                ops[index, (2 + i) * TILE:(3 + i) * TILE, cols] = low

    yr, yi = band(0), band(1)
    put(0, ((yr, -yi), (yi, yr)))
    yr, yi = yr.T, yi.T
    put(2, ((yr, yi), (-yi, yr)))
    xr, xi = band(2), band(3)
    put(3, ((xr, -xi), (xi, xr)))
    xr, xi = xr.T, xi.T
    put(1, ((xr, xi), (-xi, xr)))


def dot(a, b):
    return jnp.dot(a, b, preferred_element_type=F32)


def block(m):
    return slice(m * TILE, (m + 1) * TILE)


def main_kernel(
    offsets, counts, tile, beside, from_cross, from_mate, probe, measured, ops,
    probe_grad, grad_tile, grad_beside, cross, mate,
    object_ext, grad_ext, field_high, field_low, mid_high, mid_low, wave_one, wave_two,
):
    even = even_row()
    mate_rows = pl.ds(pl.multiple_of(jnp.where(even, HALF + TILE, 0), HALF), HALF)
    cross_rows = pl.ds(pl.multiple_of(jnp.where(even, 0, HALF + TILE), HALF), HALF)
    for b, plane in enumerate((tile, beside)):
        for p in range(4):
            object_ext[b, p, HALF:HALF + TILE] = plane[p]
            object_ext[b, p, mate_rows] = from_mate[b, p]
            object_ext[b, p, cross_rows] = from_cross[b, p]
    grad_ext[...] = jnp.zeros_like(grad_ext)

    def put_field(slot, m, real, imag):
        for c, value in enumerate((real, imag)):
            high, low = split(value)
            field_high[slot, block(c), block(m)] = high
            field_low[slot, block(c), block(m)] = low

    def rows_done(slot, which):
        for n in range(2):
            cols = slice(n * 256, (n + 1) * 256)
            both = dot(ops[which], field_high[slot, :, cols])
            mid = both[:256] + (both[256:] + dot(ops[which, :256], field_low[slot, :, cols]))
            for k in range(2):
                for c in range(2):
                    high, low = split(mid[block(c), block(k)])
                    mid_high[slot, block(2 * n + k), block(c)] = high
                    mid_low[slot, block(2 * n + k), block(c)] = low

    def cols_done(slot, which, take):
        high, low = ops[which, :256], ops[which, 256:]
        done = dot(mid_high[slot], high) + (dot(mid_low[slot], high) + dot(mid_high[slot], low))
        for m in range(4):
            take(slot, m, done[block(m), :TILE], done[block(m), TILE:])

    def propagate(which, take):
        for slot in range(2):
            rows_done(slot, which)
        for slot in range(2):
            cols_done(slot, which + 1, take)

    def window(slot, p):
        rows = [object_ext[b, p, pl.ds(offsets[2 * slot], TILE), :] for b in range(2)]
        shift = lax.rem(320 - offsets[2 * slot + 1], 256)
        return pltpu.roll(jnp.concatenate(rows, axis=1), shift, 1)[:, :TILE]

    def spread(slot, p, value):
        wide = jnp.concatenate([value, jnp.zeros_like(value)], axis=1)
        wide = pltpu.roll(wide, lax.rem(offsets[2 * slot + 1] + 192, 256), 1)
        for b in range(2):
            grad_ext[b, p, pl.ds(offsets[2 * slot], TILE), :] += wide[:, block(b)]

    views = [[window(slot, p) for p in range(4)] for slot in range(2)]
    for slot in range(2):
        o0r, o0i = views[slot][0], views[slot][2]
        for m in range(4):
            pr, pi = probe[m], probe[4 + m]
            put_field(slot, m, pr * o0r - pi * o0i, pr * o0i + pi * o0r)

    def after_first(slot, m, wr, wi):
        o1r, o1i = views[slot][1], views[slot][3]
        wave_one[slot, m, 0] = wr
        wave_one[slot, m, 1] = wi
        put_field(slot, m, wr * o1r - wi * o1i, wr * o1i + wi * o1r)

    propagate(0, after_first)
    intensity = [None, None]

    def after_second(slot, m, wr, wi):
        wave_two[slot, m, 0] = wr
        wave_two[slot, m, 1] = wi
        term = wr * wr + wi * wi
        intensity[slot] = term if m == 0 else intensity[slot] + term
        if m == 3:
            weight = jnp.where(slot < counts[0, 0], 2.0, 0.0).astype(F32)
            residual = (intensity[slot] - measured[slot]) * weight
            for k in range(4):
                put_field(slot, k, residual * wave_two[slot, k, 0], residual * wave_two[slot, k, 1])

    propagate(0, after_second)
    sums = [[None, None], [None, None]]

    def add(slot, m, real, imag):
        pair = (real, imag) if m == 0 else (sums[slot][0] + real, sums[slot][1] + imag)
        sums[slot] = pair

    def after_third(slot, m, hr, hi):
        o1r, o1i = views[slot][1], views[slot][3]
        wr, wi = wave_one[slot, m, 0], wave_one[slot, m, 1]
        add(slot, m, wr * hr + wi * hi, wr * hi - wi * hr)
        put_field(slot, m, hr * o1r + hi * o1i, hi * o1r - hr * o1i)
        if m == 3:
            spread(slot, 1, sums[slot][0])
            spread(slot, 3, sums[slot][1])

    propagate(2, after_third)

    def after_fourth(slot, m, hr, hi):
        o0r, o0i = views[slot][0], views[slot][2]
        pr, pi = probe[m], probe[4 + m]
        add(slot, m, pr * hr + pi * hi, pr * hi - pi * hr)
        dr = hr * o0r + hi * o0i
        di = hi * o0r - hr * o0i
        if slot == 0:
            probe_grad[m] = dr
            probe_grad[4 + m] = di
        else:
            probe_grad[m] += dr
            probe_grad[4 + m] += di
        if m == 3:
            spread(slot, 0, sums[slot][0])
            spread(slot, 2, sums[slot][1])

    propagate(2, after_fourth)
    for b, plane in enumerate((grad_tile, grad_beside)):
        for p in range(4):
            plane[p] = grad_ext[b, p, HALF:HALF + TILE]
            mate[b, p] = grad_ext[b, p, mate_rows]
            cross[b, p] = grad_ext[b, p, cross_rows]


def spread_sum(scale, shares, spread_share):
    share = jnp.sum(shares[...], axis=0) * scale
    for i in range(spread_share.shape[0]):
        spread_share[i] = share


def near_kernel(
    shares, grad_tile, grad_beside, from_cross, from_mate, spread_share, part, cross, mate, beside
):
    spread_sum(1.0, shares, spread_share)
    even = even_row()
    mate_rows = pl.ds(pl.multiple_of(jnp.where(even, HALF, 0), HALF), HALF)
    cross_rows = pl.ds(pl.multiple_of(jnp.where(even, 0, HALF), HALF), HALF)
    for b, (plane, total) in enumerate(((grad_tile, part), (grad_beside, beside))):
        for p in range(4):
            total[p, mate_rows] = plane[p, mate_rows] + from_mate[b, p]
            total[p, cross_rows] = plane[p, cross_rows] + from_cross[b, p]
    low = low_lanes((TILE, TILE))
    even = even_column()
    for s in range(2):
        turned = pltpu.roll(beside[2 + s], HALF, 1)
        to_right = jnp.where(low, beside[s], turned)
        to_left = jnp.where(low, turned, beside[s])
        mate[s], cross[s] = by_parity(even, to_right, to_left)


def far_kernel(scale, shares, part, from_cross, from_mate, spread_share, result):
    spread_sum(scale, shares, spread_share)
    low = low_lanes((TILE, TILE))
    even = even_column()
    for s in range(2):
        from_right, from_left = by_parity(even, from_mate[s], from_cross[s])
        result[s] = part[s] + jnp.where(low, from_left, from_right)
        result[2 + s] = part[2 + s] + pltpu.roll(jnp.where(low, from_right, from_left), HALF, 1)


def finish_kernel(result, gathered, result_far, probe_far, sems):
    moves = [pltpu.make_async_copy(result.at[p], result_far.at[p], sems.at[p]) for p in range(4)]
    for i in range(4):
        part = pl.ds(256 * i, 256)
        moves.append(pltpu.make_async_copy(gathered.at[part], probe_far.at[part], sems.at[4 + i]))
    for move in moves:
        move.start()
    for move in moves:
        move.wait()


def exchange(cross, mate, axes):
    count = lax.axis_size(axes)
    pairs = [(i, i + 1) for i in range(1, count - 1, 2)]
    from_cross = lax.ppermute(cross, axes, pairs + [(b, a) for a, b in pairs])
    pairs = [(i, i + 1) for i in range(0, count, 2)]
    from_mate = lax.ppermute(mate, axes, pairs + [(b, a) for a, b in pairs])
    return from_cross, from_mate


def f32(*shape):
    return jax.ShapeDtypeStruct(shape, F32)


def body(object_field, probe_modes, prop_taps, measured, offsets, counts):
    tile = object_field.reshape(4, TILE, TILE)
    planes, strip, rim = f32(4, TILE, TILE), f32(2, TILE, TILE), f32(2, 4, HALF, TILE)

    strips = exchange(*call(pack_kernel, (strip, strip), [VM], tile), COL_AXES)
    beside, cross, mate = call(rows_kernel, (planes, rim, rim), [VM] * 3, tile, *strips)
    rims = exchange(cross, mate, ROW_AXES)
    ops, probe, targets = call(
        operator_kernel,
        (jax.ShapeDtypeStruct((4, 512, 256), BF16), f32(8, TILE, TILE), strip), [VM, VM, VM],
        prop_taps, probe_modes.reshape(8, TILE, TILE), measured.reshape(2, TILE, TILE),
        scratch=[pltpu.VMEM((8, 2 * TILE), F32)],
    )
    probe_part, grad_tile, grad_beside, cross, mate = call(
        main_kernel,
        (f32(8, TILE, TILE), planes, planes, rim, rim), [SM, SM] + [VM] * 7,
        offsets.reshape(-1), counts.reshape(1, 1), tile, beside, *rims, probe, targets, ops,
        scratch=[
            pltpu.VMEM((2, 4, 256, TILE), F32),
            pltpu.VMEM((2, 4, 256, TILE), F32),
            pltpu.VMEM((2, 256, 512), BF16),
            pltpu.VMEM((2, 256, 512), BF16),
            pltpu.VMEM((2, 512, 256), BF16),
            pltpu.VMEM((2, 512, 256), BF16),
            pltpu.VMEM((2, 4, 2, TILE, TILE), F32),
            pltpu.VMEM((2, 4, 2, TILE, TILE), F32),
        ],
        flops=3_200_000_000, moved=4_000_000,
    )

    near = lax.axis_size(NEAR_AXES)
    far = lax.axis_size(FAR_AXES)
    rows = 8 * TILE // near
    shares = lax.all_to_all(probe_part.reshape(near, rows, TILE), NEAR_AXES, 0, 0, tiled=True)
    rims = exchange(cross, mate, ROW_AXES)
    spread_share, part, cross, mate = call(
        near_kernel, (f32(far, rows, TILE), planes, strip, strip), [VM] * 5,
        shares, grad_tile, grad_beside, *rims, scratch=[pltpu.VMEM((4, TILE, TILE), F32)],
    )
    strips = exchange(cross, mate, COL_AXES)
    shares = lax.all_to_all(spread_share, FAR_AXES, 0, 0, tiled=True)
    spread_share, result = call(
        functools.partial(far_kernel, 1.0 / math.sqrt(near * far)),
        (f32(near, rows, TILE), planes), [VM] * 4, shares, part, *strips,
    )
    gathered = lax.all_to_all(spread_share, NEAR_AXES, 0, 0, tiled=True)
    result, probe_grad = call(
        finish_kernel, (planes, f32(8 * TILE, TILE)), [VM] * 2,
        result, gathered.reshape(8 * TILE, TILE),
        scratch=[pltpu.SemaphoreType.DMA((8,))], out_specs=[FAR, FAR],
    )
    return result.reshape(object_field.shape), probe_grad.reshape(probe_modes.shape)


def solution(mesh):
    fine = Mesh(mesh.devices.reshape(2, 8, 2, 4, 2, 2), ROW_AXES + COL_AXES)
    return jax.shard_map(
        body,
        mesh=fine,
        in_specs=(
            P(None, None, ROW_AXES, COL_AXES),
            P(),
            P(),
            P(ROW_AXES, COL_AXES, None, None, None),
            P(ROW_AXES, COL_AXES, None, None),
            P(ROW_AXES, COL_AXES),
        ),
        out_specs=(P(None, None, ROW_AXES, COL_AXES), P()),
        check_vma=False,
    )
```

```python
import functools
import math

import jax
import jax.numpy as jnp
from jax import lax
from jax.experimental import pallas as pl
from jax.experimental.pallas import tpu as pltpu
from jax.sharding import Mesh
from jax.sharding import PartitionSpec as P

F32 = jnp.float32
BF16 = jnp.bfloat16
ROW_AXES = ("xl", "za", "zb")
COL_AXES = ("y", "xh", "core")
NEAR_AXES = ("xl", "zb", "y", "xh", "core")
FAR_AXES = ("za",)
VMEM_LIMIT = 40 * 1024 * 1024
TILE = 128
HALF = 64
VM = pl.BlockSpec(memory_space=pltpu.VMEM)
SM = pl.BlockSpec(memory_space=pltpu.SMEM)
FAR = pl.BlockSpec(memory_space=pltpu.HBM)


def call(kernel, out_shape, in_specs, *args, scratch=(), out_specs=None, flops=0, moved=0):
    out_shape = tuple(out_shape)
    return pl.pallas_call(
        kernel,
        out_shape=out_shape,
        in_specs=in_specs,
        out_specs=tuple(out_specs or [VM] * len(out_shape)),
        scratch_shapes=list(scratch),
        compiler_params=pltpu.CompilerParams(vmem_limit_bytes=VMEM_LIMIT),
        cost_estimate=pl.CostEstimate(flops=flops, bytes_accessed=moved, transcendentals=0),
    )(*args)


def low_lanes(shape):
    return lax.broadcasted_iota(jnp.int32, shape, len(shape) - 1) < HALF


def split(value):
    high = value.astype(BF16)
    return high, (value - high.astype(F32)).astype(BF16)


def even_column():
    return lax.axis_index("core") == 0


def even_row():
    return lax.axis_index("zb") == 0


def by_parity(even, first, second):
    return jnp.where(even, first, second), jnp.where(even, second, first)


def pack_columns(real, imag):
    low = low_lanes(real.shape)
    turned = pltpu.roll(imag, HALF, 1)
    return jnp.where(low, turned, real), jnp.where(low, real, turned)


def unpack_columns(from_left, from_right):
    low = low_lanes(from_left.shape)
    real = jnp.where(low, from_right, from_left)
    return real, pltpu.roll(jnp.where(low, from_left, from_right), HALF, 1)


def rows_kernel(tile, cross, mate):
    even = even_row()
    for p in range(4):
        mate[p], cross[p] = by_parity(even, tile[p, HALF:], tile[p, :HALF])


def columns_kernel(tile, from_cross, from_mate, tall, cross, mate):
    even = even_row()
    for p in range(4):
        below, above = by_parity(even, from_mate[p], from_cross[p])
        tall[p, :HALF] = above
        tall[p, HALF:HALF + TILE] = tile[p]
        tall[p, HALF + TILE:] = below
    even = even_column()
    for s in range(2):
        to_right, to_left = pack_columns(tall[s], tall[2 + s])
        mate[s], cross[s] = by_parity(even, to_right, to_left)


def operator_kernel(taps, probe, measured, ops, probe_near, measured_near, padded):
    probe_near[...] = probe[...]
    measured_near[...] = measured[...]
    padded[...] = jnp.zeros_like(padded)
    for axis in range(2):
        padded[2 * axis:2 * axis + 2, :31] = taps[axis]

    def band(index):
        line = jnp.broadcast_to(padded[index:index + 1, :], (TILE, 2 * TILE))
        return pltpu.roll(line, 2 * TILE - 15, 1, stride=1, stride_axis=0)[:, :TILE]

    def put(index, blocks):
        for i in range(2):
            for j in range(2):
                high, low = split(blocks[i][j])
                cols = slice(j * TILE, (j + 1) * TILE)
                ops[index, i * TILE:(i + 1) * TILE, cols] = high
                ops[index, (2 + i) * TILE:(3 + i) * TILE, cols] = low

    yr, yi = band(0), band(1)
    put(0, ((yr, -yi), (yi, yr)))
    yr, yi = yr.T, yi.T
    put(2, ((yr, yi), (-yi, yr)))
    xr, xi = band(2), band(3)
    put(3, ((xr, -xi), (xi, xr)))
    xr, xi = xr.T, xi.T
    put(1, ((xr, xi), (-xi, xr)))


def dot(a, b):
    return jnp.dot(a, b, preferred_element_type=F32)


def block(m):
    return slice(m * TILE, (m + 1) * TILE)


def main_kernel(
    offsets, counts, tall, from_cross, from_mate, probe, measured, ops,
    probe_grad, grad_tall, cross, mate,
    beside, grad_beside, field_high, field_low, mid_high, mid_low, wave_one, wave_two,
):
    even = even_column()
    for s in range(2):
        from_right, from_left = by_parity(even, from_mate[s], from_cross[s])
        beside[s], beside[2 + s] = unpack_columns(from_left, from_right)
    object_ext, grad_ext = (tall, beside), (grad_tall, grad_beside)
    for total in grad_ext:
        total[...] = jnp.zeros_like(total)

    def put_field(slot, m, real, imag):
        for c, value in enumerate((real, imag)):
            high, low = split(value)
            field_high[slot, block(c), block(m)] = high
            field_low[slot, block(c), block(m)] = low

    def rows_done(slot, which):
        for n in range(2):
            cols = slice(n * 256, (n + 1) * 256)
            both = dot(ops[which], field_high[slot, :, cols])
            mid = both[:256] + (both[256:] + dot(ops[which, :256], field_low[slot, :, cols]))
            for k in range(2):
                for c in range(2):
                    high, low = split(mid[block(c), block(k)])
                    mid_high[slot, block(2 * n + k), block(c)] = high
                    mid_low[slot, block(2 * n + k), block(c)] = low

    def cols_done(slot, which, take):
        high, low = ops[which, :256], ops[which, 256:]
        done = dot(mid_high[slot], high) + (dot(mid_low[slot], high) + dot(mid_high[slot], low))
        for m in range(4):
            take(slot, m, done[block(m), :TILE], done[block(m), TILE:])

    def propagate(which, take):
        for slot in range(2):
            rows_done(slot, which)
        for slot in range(2):
            cols_done(slot, which + 1, take)

    def window(slot, p):
        rows = [object_ext[b][p, pl.ds(offsets[2 * slot], TILE), :] for b in range(2)]
        shift = lax.rem(320 - offsets[2 * slot + 1], 256)
        return pltpu.roll(jnp.concatenate(rows, axis=1), shift, 1)[:, :TILE]

    def spread(slot, p, value):
        wide = jnp.concatenate([value, jnp.zeros_like(value)], axis=1)
        wide = pltpu.roll(wide, lax.rem(offsets[2 * slot + 1] + 192, 256), 1)
        for b in range(2):
            grad_ext[b][p, pl.ds(offsets[2 * slot], TILE), :] += wide[:, block(b)]

    views = [[window(slot, p) for p in range(4)] for slot in range(2)]
    for slot in range(2):
        o0r, o0i = views[slot][0], views[slot][2]
        for m in range(4):
            pr, pi = probe[m], probe[4 + m]
            put_field(slot, m, pr * o0r - pi * o0i, pr * o0i + pi * o0r)

    def after_first(slot, m, wr, wi):
        o1r, o1i = views[slot][1], views[slot][3]
        wave_one[slot, m, 0] = wr
        wave_one[slot, m, 1] = wi
        put_field(slot, m, wr * o1r - wi * o1i, wr * o1i + wi * o1r)

    propagate(0, after_first)
    intensity = [None, None]

    def after_second(slot, m, wr, wi):
        wave_two[slot, m, 0] = wr
        wave_two[slot, m, 1] = wi
        term = wr * wr + wi * wi
        intensity[slot] = term if m == 0 else intensity[slot] + term
        if m == 3:
            weight = jnp.where(slot < counts[0, 0], 2.0, 0.0).astype(F32)
            residual = (intensity[slot] - measured[slot]) * weight
            for k in range(4):
                put_field(slot, k, residual * wave_two[slot, k, 0], residual * wave_two[slot, k, 1])

    propagate(0, after_second)
    sums = [[None, None], [None, None]]

    def add(slot, m, real, imag):
        pair = (real, imag) if m == 0 else (sums[slot][0] + real, sums[slot][1] + imag)
        sums[slot] = pair

    def after_third(slot, m, hr, hi):
        o1r, o1i = views[slot][1], views[slot][3]
        wr, wi = wave_one[slot, m, 0], wave_one[slot, m, 1]
        add(slot, m, wr * hr + wi * hi, wr * hi - wi * hr)
        put_field(slot, m, hr * o1r + hi * o1i, hi * o1r - hr * o1i)
        if m == 3:
            spread(slot, 1, sums[slot][0])
            spread(slot, 3, sums[slot][1])

    propagate(2, after_third)

    def after_fourth(slot, m, hr, hi):
        o0r, o0i = views[slot][0], views[slot][2]
        pr, pi = probe[m], probe[4 + m]
        add(slot, m, pr * hr + pi * hi, pr * hi - pi * hr)
        dr = hr * o0r + hi * o0i
        di = hi * o0r - hr * o0i
        if slot == 0:
            probe_grad[m] = dr
            probe_grad[4 + m] = di
        else:
            probe_grad[m] += dr
            probe_grad[4 + m] += di
        if m == 3:
            spread(slot, 0, sums[slot][0])
            spread(slot, 2, sums[slot][1])

    propagate(2, after_fourth)
    for s in range(2):
        to_left, to_right = pack_columns(grad_beside[s], grad_beside[2 + s])
        mate[s], cross[s] = by_parity(even, to_right, to_left)


def spread_sum(scale, shares, spread_share):
    share = jnp.sum(shares[...], axis=0) * scale
    for i in range(spread_share.shape[0]):
        spread_share[i] = share


def near_kernel(shares, grad_tall, from_cross, from_mate, spread_share, part, cross, mate):
    spread_sum(1.0, shares, spread_share)
    even, even_down = even_column(), even_row()
    for s in range(2):
        from_right, from_left = by_parity(even, from_mate[s], from_cross[s])
        for p, sides in zip((s, 2 + s), unpack_columns(from_right, from_left)):
            total = grad_tall[p] + sides
            part[p] = total[HALF:HALF + TILE]
            mate[p], cross[p] = by_parity(even_down, total[HALF + TILE:], total[:HALF])


def far_kernel(scale, shares, part, from_cross, from_mate, spread_share, result):
    spread_sum(scale, shares, spread_share)
    even = even_row()
    for p in range(4):
        below, above = by_parity(even, from_mate[p], from_cross[p])
        result[p, :HALF] = part[p, :HALF] + above
        result[p, HALF:] = part[p, HALF:] + below


def finish_kernel(result, gathered, result_far, probe_far, sems):
    moves = [pltpu.make_async_copy(result.at[p], result_far.at[p], sems.at[p]) for p in range(4)]
    for i in range(4):
        part = pl.ds(256 * i, 256)
        moves.append(pltpu.make_async_copy(gathered.at[part], probe_far.at[part], sems.at[4 + i]))
    for move in moves:
        move.start()
    for move in moves:
        move.wait()


def exchange(cross, mate, axes):
    count = lax.axis_size(axes)
    pairs = [(i, i + 1) for i in range(1, count - 1, 2)]
    from_cross = lax.ppermute(cross, axes, pairs + [(b, a) for a, b in pairs])
    pairs = [(i, i + 1) for i in range(0, count, 2)]
    from_mate = lax.ppermute(mate, axes, pairs + [(b, a) for a, b in pairs])
    return from_cross, from_mate


def f32(*shape):
    return jax.ShapeDtypeStruct(shape, F32)


def body(object_field, probe_modes, prop_taps, measured, offsets, counts):
    tile = object_field.reshape(4, TILE, TILE)
    planes, strip, half = f32(4, TILE, TILE), f32(2, TILE, TILE), f32(4, HALF, TILE)
    tall, tall_strip = f32(4, 2 * TILE, TILE), f32(2, 2 * TILE, TILE)

    rims = exchange(*call(rows_kernel, (half, half), [VM], tile), ROW_AXES)
    object_tall, cross, mate = call(
        columns_kernel, (tall, tall_strip, tall_strip), [VM] * 3, tile, *rims
    )
    strips = exchange(cross, mate, COL_AXES)
    ops, probe, targets = call(
        operator_kernel,
        (jax.ShapeDtypeStruct((4, 512, 256), BF16), f32(8, TILE, TILE), strip), [VM, VM, VM],
        prop_taps, probe_modes.reshape(8, TILE, TILE), measured.reshape(2, TILE, TILE),
        scratch=[pltpu.VMEM((8, 2 * TILE), F32)],
    )
    probe_part, grad_tall, cross, mate = call(
        main_kernel,
        (f32(8, TILE, TILE), tall, tall_strip, tall_strip), [SM, SM] + [VM] * 6,
        offsets.reshape(-1), counts.reshape(1, 1), object_tall, *strips, probe, targets, ops,
        scratch=[
            pltpu.VMEM((4, 256, TILE), F32),
            pltpu.VMEM((4, 256, TILE), F32),
            pltpu.VMEM((2, 256, 512), BF16),
            pltpu.VMEM((2, 256, 512), BF16),
            pltpu.VMEM((2, 512, 256), BF16),
            pltpu.VMEM((2, 512, 256), BF16),
            pltpu.VMEM((2, 4, 2, TILE, TILE), F32),
            pltpu.VMEM((2, 4, 2, TILE, TILE), F32),
        ],
        flops=3_200_000_000, moved=4_000_000,
    )

    near = lax.axis_size(NEAR_AXES)
    far = lax.axis_size(FAR_AXES)
    rows = 8 * TILE // near
    shares = lax.all_to_all(probe_part.reshape(near, rows, TILE), NEAR_AXES, 0, 0, tiled=True)
    strips = exchange(cross, mate, COL_AXES)
    spread_share, part, cross, mate = call(
        near_kernel, (f32(far, rows, TILE), planes, half, half), [VM] * 4, shares, grad_tall, *strips
    )
    rims = exchange(cross, mate, ROW_AXES)
    shares = lax.all_to_all(spread_share, FAR_AXES, 0, 0, tiled=True)
    spread_share, result = call(
        functools.partial(far_kernel, 1.0 / math.sqrt(near * far)),
        (f32(near, rows, TILE), planes), [VM] * 4, shares, part, *rims,
    )
    gathered = lax.all_to_all(spread_share, NEAR_AXES, 0, 0, tiled=True)
    result, probe_grad = call(
        finish_kernel, (planes, f32(8 * TILE, TILE)), [VM] * 2,
        result, gathered.reshape(8 * TILE, TILE),
        scratch=[pltpu.SemaphoreType.DMA((8,))], out_specs=[FAR, FAR],
    )
    return result.reshape(object_field.shape), probe_grad.reshape(probe_modes.shape)


def solution(mesh):
    fine = Mesh(mesh.devices.reshape(2, 8, 2, 4, 2, 2), ROW_AXES + COL_AXES)
    return jax.shard_map(
        body,
        mesh=fine,
        in_specs=(
            P(None, None, ROW_AXES, COL_AXES),
            P(),
            P(),
            P(ROW_AXES, COL_AXES, None, None, None),
            P(ROW_AXES, COL_AXES, None, None),
            P(ROW_AXES, COL_AXES),
        ),
        out_specs=(P(None, None, ROW_AXES, COL_AXES), P()),
        check_vma=False,
    )
```

```python
import functools
import math

import jax
import jax.numpy as jnp
from jax import lax
from jax.experimental import pallas as pl
from jax.experimental.pallas import tpu as pltpu
from jax.sharding import Mesh
from jax.sharding import PartitionSpec as P

F32 = jnp.float32
BF16 = jnp.bfloat16
ROW_AXES = ("xl", "za", "zb")
COL_AXES = ("y", "xh", "core")
NEAR_AXES = ("xl", "zb", "y", "xh", "core")
FAR_AXES = ("za",)
VMEM_LIMIT = 40 * 1024 * 1024
TILE = 128
HALF = 64
VM = pl.BlockSpec(memory_space=pltpu.VMEM)
SM = pl.BlockSpec(memory_space=pltpu.SMEM)
FAR = pl.BlockSpec(memory_space=pltpu.HBM)


def call(kernel, out_shape, in_specs, *args, scratch=(), out_specs=None, flops=0, moved=0):
    out_shape = tuple(out_shape)
    return pl.pallas_call(
        kernel,
        out_shape=out_shape,
        in_specs=in_specs,
        out_specs=tuple(out_specs or [VM] * len(out_shape)),
        scratch_shapes=list(scratch),
        compiler_params=pltpu.CompilerParams(vmem_limit_bytes=VMEM_LIMIT),
        cost_estimate=pl.CostEstimate(flops=flops, bytes_accessed=moved, transcendentals=0),
    )(*args)


def low_lanes(shape):
    return lax.broadcasted_iota(jnp.int32, shape, len(shape) - 1) < HALF


def split(value):
    high = value.astype(BF16)
    return high, (value - high.astype(F32)).astype(BF16)


def even_column():
    return lax.axis_index("core") == 0


def even_row():
    return lax.axis_index("zb") == 0


def by_parity(even, first, second):
    return jnp.where(even, first, second), jnp.where(even, second, first)


def pack_columns(real, imag):
    low = low_lanes(real.shape)
    turned = pltpu.roll(imag, HALF, 1)
    return jnp.where(low, turned, real), jnp.where(low, real, turned)


def unpack_columns(from_left, from_right):
    low = low_lanes(from_left.shape)
    real = jnp.where(low, from_right, from_left)
    return real, pltpu.roll(jnp.where(low, from_left, from_right), HALF, 1)


def rows_kernel(tile, cross, mate):
    even = even_row()
    for p in range(4):
        mate[p], cross[p] = by_parity(even, tile[p, HALF:], tile[p, :HALF])


def columns_kernel(tile, from_cross, from_mate, tall, cross, mate):
    even = even_row()
    for p in range(4):
        below, above = by_parity(even, from_mate[p], from_cross[p])
        tall[p, :HALF] = above
        tall[p, HALF:HALF + TILE] = tile[p]
        tall[p, HALF + TILE:] = below
    even = even_column()
    for s in range(2):
        to_right, to_left = pack_columns(tall[s], tall[2 + s])
        mate[s], cross[s] = by_parity(even, to_right, to_left)


def operator_kernel(taps, probe, measured, ops, probe_near, measured_near, padded):
    probe_near[...] = probe[...]
    measured_near[...] = measured[...]
    padded[...] = jnp.zeros_like(padded)
    for axis in range(2):
        padded[2 * axis:2 * axis + 2, :31] = taps[axis]

    def band(index):
        line = jnp.broadcast_to(padded[index:index + 1, :], (TILE, 2 * TILE))
        return pltpu.roll(line, 2 * TILE - 15, 1, stride=1, stride_axis=0)[:, :TILE]

    def put(index, blocks):
        for i in range(2):
            for j in range(2):
                high, low = split(blocks[i][j])
                cols = slice(j * TILE, (j + 1) * TILE)
                ops[index, i * TILE:(i + 1) * TILE, cols] = high
                ops[index, (2 + i) * TILE:(3 + i) * TILE, cols] = low

    yr, yi = band(0), band(1)
    put(0, ((yr, -yi), (yi, yr)))
    yr, yi = yr.T, yi.T
    put(2, ((yr, yi), (-yi, yr)))
    xr, xi = band(2), band(3)
    put(3, ((xr, -xi), (xi, xr)))
    xr, xi = xr.T, xi.T
    put(1, ((xr, xi), (-xi, xr)))


def dot(a, b):
    return jnp.dot(a, b, preferred_element_type=F32)


def block(m):
    return slice(m * TILE, (m + 1) * TILE)


def main_kernel(
    offsets, counts, tall, from_cross, from_mate, probe, measured, ops,
    probe_grad, grad_tall, cross, mate,
    beside, grad_beside, field_high, field_low, mid_high, mid_low, wave_one, wave_two,
):
    even = even_column()
    for s in range(2):
        from_right, from_left = by_parity(even, from_mate[s], from_cross[s])
        beside[s], beside[2 + s] = unpack_columns(from_left, from_right)
    object_ext, grad_ext = (tall, beside), (grad_tall, grad_beside)
    for total in grad_ext:
        total[...] = jnp.zeros_like(total)

    def put_field(slot, m, real, imag):
        for c, value in enumerate((real, imag)):
            high, low = split(value)
            field_high[slot, block(c), block(m)] = high
            field_low[slot, block(c), block(m)] = low

    def rows_done(slot, which):
        for n in range(2):
            cols = slice(n * 256, (n + 1) * 256)
            both = dot(ops[which], field_high[slot, :, cols])
            mid = both[:256] + (both[256:] + dot(ops[which, :256], field_low[slot, :, cols]))
            for k in range(2):
                for c in range(2):
                    high, low = split(mid[block(c), block(k)])
                    mid_high[slot, block(2 * n + k), block(c)] = high
                    mid_low[slot, block(2 * n + k), block(c)] = low

    def cols_done(slot, which, take):
        high, low = ops[which, :256], ops[which, 256:]
        done = dot(mid_high[slot], high) + (dot(mid_low[slot], high) + dot(mid_high[slot], low))
        for m in range(4):
            take(slot, m, done[block(m), :TILE], done[block(m), TILE:])

    def propagate(which, take):
        for slot in range(2):
            rows_done(slot, which)
        for slot in range(2):
            cols_done(slot, which + 1, take)

    def window(slot, p):
        rows = [object_ext[b][p, pl.ds(offsets[2 * slot], TILE), :] for b in range(2)]
        shift = lax.rem(320 - offsets[2 * slot + 1], 256)
        return pltpu.roll(jnp.concatenate(rows, axis=1), shift, 1)[:, :TILE]

    def spread(slot, p, value):
        wide = jnp.concatenate([value, jnp.zeros_like(value)], axis=1)
        wide = pltpu.roll(wide, lax.rem(offsets[2 * slot + 1] + 192, 256), 1)
        for b in range(2):
            grad_ext[b][p, pl.ds(offsets[2 * slot], TILE), :] += wide[:, block(b)]

    views = [[window(slot, p) for p in range(4)] for slot in range(2)]
    for slot in range(2):
        o0r, o0i = views[slot][0], views[slot][2]
        for m in range(4):
            pr, pi = probe[m], probe[4 + m]
            put_field(slot, m, pr * o0r - pi * o0i, pr * o0i + pi * o0r)

    def after_first(slot, m, wr, wi):
        o1r, o1i = views[slot][1], views[slot][3]
        wave_one[slot, m, 0] = wr
        wave_one[slot, m, 1] = wi
        put_field(slot, m, wr * o1r - wi * o1i, wr * o1i + wi * o1r)

    propagate(0, after_first)
    intensity = [None, None]

    def after_second(slot, m, wr, wi):
        wave_two[slot, m, 0] = wr
        wave_two[slot, m, 1] = wi
        term = wr * wr + wi * wi
        intensity[slot] = term if m == 0 else intensity[slot] + term
        if m == 3:
            weight = jnp.where(slot < counts[0, 0], 2.0, 0.0).astype(F32)
            residual = (intensity[slot] - measured[slot]) * weight
            for k in range(4):
                put_field(slot, k, residual * wave_two[slot, k, 0], residual * wave_two[slot, k, 1])

    propagate(0, after_second)
    sums = [[None, None], [None, None]]

    def add(slot, m, real, imag):
        pair = (real, imag) if m == 0 else (sums[slot][0] + real, sums[slot][1] + imag)
        sums[slot] = pair

    def after_third(slot, m, hr, hi):
        o1r, o1i = views[slot][1], views[slot][3]
        wr, wi = wave_one[slot, m, 0], wave_one[slot, m, 1]
        add(slot, m, wr * hr + wi * hi, wr * hi - wi * hr)
        put_field(slot, m, hr * o1r + hi * o1i, hi * o1r - hr * o1i)
        if m == 3:
            spread(slot, 1, sums[slot][0])
            spread(slot, 3, sums[slot][1])

    propagate(2, after_third)

    def after_fourth(slot, m, hr, hi):
        o0r, o0i = views[slot][0], views[slot][2]
        pr, pi = probe[m], probe[4 + m]
        add(slot, m, pr * hr + pi * hi, pr * hi - pi * hr)
        dr = hr * o0r + hi * o0i
        di = hi * o0r - hr * o0i
        if slot == 0:
            probe_grad[m] = dr
            probe_grad[4 + m] = di
        else:
            probe_grad[m] += dr
            probe_grad[4 + m] += di
        if m == 3:
            spread(slot, 0, sums[slot][0])
            spread(slot, 2, sums[slot][1])

    propagate(2, after_fourth)
    for s in range(2):
        to_left, to_right = pack_columns(grad_beside[s], grad_beside[2 + s])
        mate[s], cross[s] = by_parity(even, to_right, to_left)


def spread_sum(scale, shares, spread_share):
    share = jnp.sum(shares[...], axis=0) * scale
    for i in range(spread_share.shape[0]):
        spread_share[i] = share


def near_kernel(shares, spread_share):
    spread_sum(1.0, shares, spread_share)


def far_kernel(scale, shares, grad_tall, from_cross, from_mate, spread_share, part, cross, mate):
    spread_sum(scale, shares, spread_share)
    even, even_down = even_column(), even_row()
    for s in range(2):
        from_right, from_left = by_parity(even, from_mate[s], from_cross[s])
        for p, sides in zip((s, 2 + s), unpack_columns(from_right, from_left)):
            total = grad_tall[p] + sides
            part[p] = total[HALF:HALF + TILE]
            mate[p], cross[p] = by_parity(even_down, total[HALF + TILE:], total[:HALF])


def finish_kernel(part, from_cross, from_mate, gathered, result_far, probe_far, result, sems):
    moves = []
    for i in range(4):
        rows = pl.ds(256 * i, 256)
        moves.append(pltpu.make_async_copy(gathered.at[rows], probe_far.at[rows], sems.at[i]))
        moves[i].start()
    even = even_row()
    for p in range(4):
        below, above = by_parity(even, from_mate[p], from_cross[p])
        result[p, :HALF] = part[p, :HALF] + above
        result[p, HALF:] = part[p, HALF:] + below
        moves.append(pltpu.make_async_copy(result.at[p], result_far.at[p], sems.at[4 + p]))
        moves[-1].start()
    for move in moves:
        move.wait()


def exchange(cross, mate, axes):
    count = lax.axis_size(axes)
    pairs = [(i, i + 1) for i in range(1, count - 1, 2)]
    from_cross = lax.ppermute(cross, axes, pairs + [(b, a) for a, b in pairs])
    pairs = [(i, i + 1) for i in range(0, count, 2)]
    from_mate = lax.ppermute(mate, axes, pairs + [(b, a) for a, b in pairs])
    return from_cross, from_mate


def f32(*shape):
    return jax.ShapeDtypeStruct(shape, F32)


def body(object_field, probe_modes, prop_taps, measured, offsets, counts):
    tile = object_field.reshape(4, TILE, TILE)
    planes, strip, half = f32(4, TILE, TILE), f32(2, TILE, TILE), f32(4, HALF, TILE)
    tall, tall_strip = f32(4, 2 * TILE, TILE), f32(2, 2 * TILE, TILE)

    rims = exchange(*call(rows_kernel, (half, half), [VM], tile), ROW_AXES)
    object_tall, cross, mate = call(
        columns_kernel, (tall, tall_strip, tall_strip), [VM] * 3, tile, *rims
    )
    strips = exchange(cross, mate, COL_AXES)
    ops, probe, targets = call(
        operator_kernel,
        (jax.ShapeDtypeStruct((4, 512, 256), BF16), f32(8, TILE, TILE), strip), [VM, VM, VM],
        prop_taps, probe_modes.reshape(8, TILE, TILE), measured.reshape(2, TILE, TILE),
        scratch=[pltpu.VMEM((8, 2 * TILE), F32)],
    )
    probe_part, grad_tall, cross, mate = call(
        main_kernel,
        (f32(8, TILE, TILE), tall, tall_strip, tall_strip), [SM, SM] + [VM] * 6,
        offsets.reshape(-1), counts.reshape(1, 1), object_tall, *strips, probe, targets, ops,
        scratch=[
            pltpu.VMEM((4, 256, TILE), F32),
            pltpu.VMEM((4, 256, TILE), F32),
            pltpu.VMEM((2, 256, 512), BF16),
            pltpu.VMEM((2, 256, 512), BF16),
            pltpu.VMEM((2, 512, 256), BF16),
            pltpu.VMEM((2, 512, 256), BF16),
            pltpu.VMEM((2, 4, 2, TILE, TILE), F32),
            pltpu.VMEM((2, 4, 2, TILE, TILE), F32),
        ],
        flops=3_200_000_000, moved=4_000_000,
    )

    near = lax.axis_size(NEAR_AXES)
    far = lax.axis_size(FAR_AXES)
    rows = 8 * TILE // near
    shares = lax.all_to_all(probe_part.reshape(near, rows, TILE), NEAR_AXES, 0, 0, tiled=True)
    (spread_share,) = call(near_kernel, (f32(far, rows, TILE),), [VM], shares)
    strips = exchange(cross, mate, COL_AXES)
    shares = lax.all_to_all(spread_share, FAR_AXES, 0, 0, tiled=True)
    spread_share, part, cross, mate = call(
        functools.partial(far_kernel, 1.0 / math.sqrt(near * far)),
        (f32(near, rows, TILE), planes, half, half), [VM] * 4, shares, grad_tall, *strips,
    )
    rims = exchange(cross, mate, ROW_AXES)
    gathered = lax.all_to_all(spread_share, NEAR_AXES, 0, 0, tiled=True)
    result, probe_grad = call(
        finish_kernel, (planes, f32(8 * TILE, TILE)), [VM] * 4,
        part, *rims, gathered.reshape(8 * TILE, TILE),
        scratch=[pltpu.VMEM((4, TILE, TILE), F32), pltpu.SemaphoreType.DMA((8,))],
        out_specs=[FAR, FAR],
    )
    return result.reshape(object_field.shape), probe_grad.reshape(probe_modes.shape)


def solution(mesh):
    fine = Mesh(mesh.devices.reshape(2, 8, 2, 4, 2, 2), ROW_AXES + COL_AXES)
    return jax.shard_map(
        body,
        mesh=fine,
        in_specs=(
            P(None, None, ROW_AXES, COL_AXES),
            P(),
            P(),
            P(ROW_AXES, COL_AXES, None, None, None),
            P(ROW_AXES, COL_AXES, None, None),
            P(ROW_AXES, COL_AXES),
        ),
        out_specs=(P(None, None, ROW_AXES, COL_AXES), P()),
        check_vma=False,
    )
```

```python
import functools
import math

import jax
import jax.numpy as jnp
from jax import lax
from jax.experimental import pallas as pl
from jax.experimental.pallas import tpu as pltpu
from jax.sharding import Mesh
from jax.sharding import PartitionSpec as P

F32 = jnp.float32
BF16 = jnp.bfloat16
ROW_AXES = ("xl", "za", "zb")
COL_AXES = ("y", "xh", "core")
NEAR_AXES = ("xl", "zb", "y", "xh", "core")
FAR_AXES = ("za",)
VMEM_LIMIT = 40 * 1024 * 1024
TILE = 128
HALF = 64
VM = pl.BlockSpec(memory_space=pltpu.VMEM)
SM = pl.BlockSpec(memory_space=pltpu.SMEM)
FAR = pl.BlockSpec(memory_space=pltpu.HBM)


def call(kernel, out_shape, in_specs, *args, scratch=(), out_specs=None, flops=0, moved=0):
    out_shape = tuple(out_shape)
    return pl.pallas_call(
        kernel,
        out_shape=out_shape,
        in_specs=in_specs,
        out_specs=tuple(out_specs or [VM] * len(out_shape)),
        scratch_shapes=list(scratch),
        compiler_params=pltpu.CompilerParams(vmem_limit_bytes=VMEM_LIMIT),
        cost_estimate=pl.CostEstimate(flops=flops, bytes_accessed=moved, transcendentals=0),
    )(*args)


def low_lanes(shape):
    return lax.broadcasted_iota(jnp.int32, shape, len(shape) - 1) < HALF


def split(value):
    high = value.astype(BF16)
    return high, (value - high.astype(F32)).astype(BF16)


def even_column():
    return lax.axis_index("core") == 0


def even_row():
    return lax.axis_index("zb") == 0


def by_parity(even, first, second):
    return jnp.where(even, first, second), jnp.where(even, second, first)


def pack_columns(real, imag):
    low = low_lanes(real.shape)
    turned = pltpu.roll(imag, HALF, 1)
    return jnp.where(low, turned, real), jnp.where(low, real, turned)


def unpack_columns(from_left, from_right):
    low = low_lanes(from_left.shape)
    real = jnp.where(low, from_right, from_left)
    return real, pltpu.roll(jnp.where(low, from_left, from_right), HALF, 1)


def rows_kernel(tile, cross, mate):
    even = even_row()
    for p in range(4):
        mate[p], cross[p] = by_parity(even, tile[p, HALF:], tile[p, :HALF])


def columns_kernel(tile, from_cross, from_mate, tall, cross, mate):
    even = even_row()
    for p in range(4):
        below, above = by_parity(even, from_mate[p], from_cross[p])
        tall[p, :HALF] = above
        tall[p, HALF:HALF + TILE] = tile[p]
        tall[p, HALF + TILE:] = below
    even = even_column()
    for s in range(2):
        to_right, to_left = pack_columns(tall[s], tall[2 + s])
        mate[s], cross[s] = by_parity(even, to_right, to_left)


def operator_kernel(taps, probe, measured, ops, probe_near, measured_near, padded):
    probe_near[...] = probe[...]
    measured_near[...] = measured[...]
    padded[...] = jnp.zeros_like(padded)
    for axis in range(2):
        padded[2 * axis:2 * axis + 2, :31] = taps[axis]

    def band(index):
        line = jnp.broadcast_to(padded[index:index + 1, :], (TILE, 2 * TILE))
        return pltpu.roll(line, 2 * TILE - 15, 1, stride=1, stride_axis=0)[:, :TILE]

    def put(index, blocks):
        for i in range(2):
            for j in range(2):
                high, low = split(blocks[i][j])
                cols = slice(j * TILE, (j + 1) * TILE)
                ops[index, i * TILE:(i + 1) * TILE, cols] = high
                ops[index, (2 + i) * TILE:(3 + i) * TILE, cols] = low

    yr, yi = band(0), band(1)
    put(0, ((yr, -yi), (yi, yr)))
    yr, yi = yr.T, yi.T
    put(2, ((yr, yi), (-yi, yr)))
    xr, xi = band(2), band(3)
    put(3, ((xr, -xi), (xi, xr)))
    xr, xi = xr.T, xi.T
    put(1, ((xr, xi), (-xi, xr)))


def dot(a, b):
    return jnp.dot(a, b, preferred_element_type=F32)


def block(m):
    return slice(m * TILE, (m + 1) * TILE)


def main_kernel(
    offsets, counts, tall, from_cross, from_mate, probe, measured, ops,
    probe_grad, grad_tall, cross, mate,
    beside, grad_beside, field_high, field_low, mid_high, mid_low, wave_one, wave_two,
):
    even = even_column()
    for s in range(2):
        from_right, from_left = by_parity(even, from_mate[s], from_cross[s])
        beside[s], beside[2 + s] = unpack_columns(from_left, from_right)
    object_ext, grad_ext = (tall, beside), (grad_tall, grad_beside)
    for total in grad_ext:
        total[...] = jnp.zeros_like(total)

    def put_field(slot, m, real, imag):
        for c, value in enumerate((real, imag)):
            high, low = split(value)
            field_high[slot, block(c), block(m)] = high
            field_low[slot, block(c), block(m)] = low

    def rows_done(slot, which):
        for n in range(2):
            cols = slice(n * 256, (n + 1) * 256)
            both = dot(ops[which], field_high[slot, :, cols])
            mid = both[:256] + (both[256:] + dot(ops[which, :256], field_low[slot, :, cols]))
            for k in range(2):
                for c in range(2):
                    high, low = split(mid[block(c), block(k)])
                    mid_high[slot, block(2 * n + k), block(c)] = high
                    mid_low[slot, block(2 * n + k), block(c)] = low

    def cols_done(slot, which, take):
        high, low = ops[which, :256], ops[which, 256:]
        done = dot(mid_high[slot], high) + (dot(mid_low[slot], high) + dot(mid_high[slot], low))
        for m in range(4):
            take(slot, m, done[block(m), :TILE], done[block(m), TILE:])

    def propagate(which, take):
        for slot in range(2):
            rows_done(slot, which)
        for slot in range(2):
            cols_done(slot, which + 1, take)

    def window(slot, p):
        rows = [object_ext[b][p, pl.ds(offsets[2 * slot], TILE), :] for b in range(2)]
        shift = lax.rem(320 - offsets[2 * slot + 1], 256)
        return pltpu.roll(jnp.concatenate(rows, axis=1), shift, 1)[:, :TILE]

    def spread(slot, p, value):
        wide = jnp.concatenate([value, jnp.zeros_like(value)], axis=1)
        wide = pltpu.roll(wide, lax.rem(offsets[2 * slot + 1] + 192, 256), 1)
        for b in range(2):
            grad_ext[b][p, pl.ds(offsets[2 * slot], TILE), :] += wide[:, block(b)]

    views = [[window(slot, p) for p in range(4)] for slot in range(2)]
    for slot in range(2):
        o0r, o0i = views[slot][0], views[slot][2]
        for m in range(4):
            pr, pi = probe[m], probe[4 + m]
            put_field(slot, m, pr * o0r - pi * o0i, pr * o0i + pi * o0r)

    def after_first(slot, m, wr, wi):
        o1r, o1i = views[slot][1], views[slot][3]
        wave_one[slot, m, 0] = wr
        wave_one[slot, m, 1] = wi
        put_field(slot, m, wr * o1r - wi * o1i, wr * o1i + wi * o1r)

    propagate(0, after_first)
    intensity = [None, None]

    def after_second(slot, m, wr, wi):
        wave_two[slot, m, 0] = wr
        wave_two[slot, m, 1] = wi
        term = wr * wr + wi * wi
        intensity[slot] = term if m == 0 else intensity[slot] + term
        if m == 3:
            weight = jnp.where(slot < counts[0, 0], 2.0, 0.0).astype(F32)
            residual = (intensity[slot] - measured[slot]) * weight
            for k in range(4):
                put_field(slot, k, residual * wave_two[slot, k, 0], residual * wave_two[slot, k, 1])

    propagate(0, after_second)
    sums = [[None, None], [None, None]]

    def add(slot, m, real, imag):
        pair = (real, imag) if m == 0 else (sums[slot][0] + real, sums[slot][1] + imag)
        sums[slot] = pair

    def after_third(slot, m, hr, hi):
        o1r, o1i = views[slot][1], views[slot][3]
        wr, wi = wave_one[slot, m, 0], wave_one[slot, m, 1]
        add(slot, m, wr * hr + wi * hi, wr * hi - wi * hr)
        put_field(slot, m, hr * o1r + hi * o1i, hi * o1r - hr * o1i)
        if m == 3:
            spread(slot, 1, sums[slot][0])
            spread(slot, 3, sums[slot][1])

    propagate(2, after_third)

    def after_fourth(slot, m, hr, hi):
        o0r, o0i = views[slot][0], views[slot][2]
        pr, pi = probe[m], probe[4 + m]
        add(slot, m, pr * hr + pi * hi, pr * hi - pi * hr)
        dr = hr * o0r + hi * o0i
        di = hi * o0r - hr * o0i
        if slot == 0:
            probe_grad[m] = dr
            probe_grad[4 + m] = di
        else:
            probe_grad[m] += dr
            probe_grad[4 + m] += di
        if m == 3:
            spread(slot, 0, sums[slot][0])
            spread(slot, 2, sums[slot][1])

    propagate(2, after_fourth)
    for s in range(2):
        to_left, to_right = pack_columns(grad_beside[s], grad_beside[2 + s])
        mate[s], cross[s] = by_parity(even, to_right, to_left)


def share_kernel(scale, shares, spread_share):
    share = jnp.sum(shares[...], axis=0) * scale
    for i in range(spread_share.shape[0]):
        spread_share[i] = share


def fold_columns_kernel(grad_tall, from_cross, from_mate, part, cross, mate):
    even, even_down = even_column(), even_row()
    for s in range(2):
        from_right, from_left = by_parity(even, from_mate[s], from_cross[s])
        for p, sides in zip((s, 2 + s), unpack_columns(from_right, from_left)):
            total = grad_tall[p] + sides
            part[p] = total[HALF:HALF + TILE]
            mate[p], cross[p] = by_parity(even_down, total[HALF + TILE:], total[:HALF])


def fold_rows_kernel(scale, shares, part, from_cross, from_mate, spread_share, result):
    share_kernel(scale, shares, spread_share)
    even = even_row()
    for p in range(4):
        below, above = by_parity(even, from_mate[p], from_cross[p])
        result[p, :HALF] = part[p, :HALF] + above
        result[p, HALF:] = part[p, HALF:] + below


def finish_kernel(result, gathered, result_far, probe_far, sems):
    moves = [pltpu.make_async_copy(result.at[p], result_far.at[p], sems.at[p]) for p in range(4)]
    for i in range(4):
        part = pl.ds(256 * i, 256)
        moves.append(pltpu.make_async_copy(gathered.at[part], probe_far.at[part], sems.at[4 + i]))
    for move in moves:
        move.start()
    for move in moves:
        move.wait()


def exchange(cross, mate, axes):
    count = lax.axis_size(axes)
    pairs = [(i, i + 1) for i in range(1, count - 1, 2)]
    from_cross = lax.ppermute(cross, axes, pairs + [(b, a) for a, b in pairs])
    pairs = [(i, i + 1) for i in range(0, count, 2)]
    from_mate = lax.ppermute(mate, axes, pairs + [(b, a) for a, b in pairs])
    return from_cross, from_mate


def f32(*shape):
    return jax.ShapeDtypeStruct(shape, F32)


def body(object_field, probe_modes, prop_taps, measured, offsets, counts):
    tile = object_field.reshape(4, TILE, TILE)
    planes, strip, half = f32(4, TILE, TILE), f32(2, TILE, TILE), f32(4, HALF, TILE)
    tall, tall_strip = f32(4, 2 * TILE, TILE), f32(2, 2 * TILE, TILE)

    rims = exchange(*call(rows_kernel, (half, half), [VM], tile), ROW_AXES)
    object_tall, cross, mate = call(
        columns_kernel, (tall, tall_strip, tall_strip), [VM] * 3, tile, *rims
    )
    strips = exchange(cross, mate, COL_AXES)
    ops, probe, targets = call(
        operator_kernel,
        (jax.ShapeDtypeStruct((4, 512, 256), BF16), f32(8, TILE, TILE), strip), [VM, VM, VM],
        prop_taps, probe_modes.reshape(8, TILE, TILE), measured.reshape(2, TILE, TILE),
        scratch=[pltpu.VMEM((8, 2 * TILE), F32)],
    )
    probe_part, grad_tall, cross, mate = call(
        main_kernel,
        (f32(8, TILE, TILE), tall, tall_strip, tall_strip), [SM, SM] + [VM] * 6,
        offsets.reshape(-1), counts.reshape(1, 1), object_tall, *strips, probe, targets, ops,
        scratch=[
            pltpu.VMEM((4, 256, TILE), F32),
            pltpu.VMEM((4, 256, TILE), F32),
            pltpu.VMEM((2, 256, 512), BF16),
            pltpu.VMEM((2, 256, 512), BF16),
            pltpu.VMEM((2, 512, 256), BF16),
            pltpu.VMEM((2, 512, 256), BF16),
            pltpu.VMEM((2, 4, 2, TILE, TILE), F32),
            pltpu.VMEM((2, 4, 2, TILE, TILE), F32),
        ],
        flops=3_200_000_000, moved=4_000_000,
    )

    near = lax.axis_size(NEAR_AXES)
    far = lax.axis_size(FAR_AXES)
    rows = 8 * TILE // near
    shares = lax.all_to_all(probe_part.reshape(near, rows, TILE), NEAR_AXES, 0, 0, tiled=True)
    (spread_share,) = call(
        functools.partial(share_kernel, 1.0), (f32(far, rows, TILE),), [VM], shares
    )
    strips = exchange(cross, mate, COL_AXES)
    shares = lax.all_to_all(spread_share, FAR_AXES, 0, 0, tiled=True)
    part, cross, mate = call(
        fold_columns_kernel, (planes, half, half), [VM] * 3, grad_tall, *strips
    )
    rims = exchange(cross, mate, ROW_AXES)
    spread_share, result = call(
        functools.partial(fold_rows_kernel, 1.0 / math.sqrt(near * far)),
        (f32(near, rows, TILE), planes), [VM] * 4, shares, part, *rims,
    )
    gathered = lax.all_to_all(spread_share, NEAR_AXES, 0, 0, tiled=True)
    result, probe_grad = call(
        finish_kernel, (planes, f32(8 * TILE, TILE)), [VM] * 2,
        result, gathered.reshape(8 * TILE, TILE),
        scratch=[pltpu.SemaphoreType.DMA((8,))], out_specs=[FAR, FAR],
    )
    return result.reshape(object_field.shape), probe_grad.reshape(probe_modes.shape)


def solution(mesh):
    fine = Mesh(mesh.devices.reshape(2, 8, 2, 4, 2, 2), ROW_AXES + COL_AXES)
    return jax.shard_map(
        body,
        mesh=fine,
        in_specs=(
            P(None, None, ROW_AXES, COL_AXES),
            P(),
            P(),
            P(ROW_AXES, COL_AXES, None, None, None),
            P(ROW_AXES, COL_AXES, None, None),
            P(ROW_AXES, COL_AXES),
        ),
        out_specs=(P(None, None, ROW_AXES, COL_AXES), P()),
        check_vma=False,
    )
```

```python
import functools
import math

import jax
import jax.numpy as jnp
from jax import lax
from jax.experimental import pallas as pl
from jax.experimental.pallas import tpu as pltpu
from jax.sharding import Mesh
from jax.sharding import PartitionSpec as P

F32 = jnp.float32
BF16 = jnp.bfloat16
ROW_AXES = ("xl", "za", "zb")
COL_AXES = ("y", "xh", "core")
NEAR_AXES = ("xl", "y", "xh", "core")
FAR_AXES = ("za", "zb")
VMEM_LIMIT = 40 * 1024 * 1024
TILE = 128
HALF = 64
VM = pl.BlockSpec(memory_space=pltpu.VMEM)
SM = pl.BlockSpec(memory_space=pltpu.SMEM)
FAR = pl.BlockSpec(memory_space=pltpu.HBM)


def call(kernel, out_shape, in_specs, *args, scratch=(), out_specs=None, flops=0, moved=0):
    out_shape = tuple(out_shape)
    return pl.pallas_call(
        kernel,
        out_shape=out_shape,
        in_specs=in_specs,
        out_specs=tuple(out_specs or [VM] * len(out_shape)),
        scratch_shapes=list(scratch),
        compiler_params=pltpu.CompilerParams(vmem_limit_bytes=VMEM_LIMIT),
        cost_estimate=pl.CostEstimate(flops=flops, bytes_accessed=moved, transcendentals=0),
    )(*args)


def low_lanes(shape):
    return lax.broadcasted_iota(jnp.int32, shape, len(shape) - 1) < HALF


def split(value):
    high = value.astype(BF16)
    return high, (value - high.astype(F32)).astype(BF16)


def even_column():
    return lax.axis_index("core") == 0


def even_row():
    return lax.axis_index("zb") == 0


def by_parity(even, first, second):
    return jnp.where(even, first, second), jnp.where(even, second, first)


def pack_columns(real, imag):
    low = low_lanes(real.shape)
    turned = pltpu.roll(imag, HALF, 1)
    return jnp.where(low, turned, real), jnp.where(low, real, turned)


def unpack_columns(from_left, from_right):
    low = low_lanes(from_left.shape)
    real = jnp.where(low, from_right, from_left)
    return real, pltpu.roll(jnp.where(low, from_left, from_right), HALF, 1)


def rows_kernel(tile, cross, mate):
    even = even_row()
    for p in range(4):
        mate[p], cross[p] = by_parity(even, tile[p, HALF:], tile[p, :HALF])


def columns_kernel(tile, from_cross, from_mate, tall, cross, mate):
    even = even_row()
    for p in range(4):
        below, above = by_parity(even, from_mate[p], from_cross[p])
        tall[p, :HALF] = above
        tall[p, HALF:HALF + TILE] = tile[p]
        tall[p, HALF + TILE:] = below
    even = even_column()
    for s in range(2):
        to_right, to_left = pack_columns(tall[s], tall[2 + s])
        mate[s], cross[s] = by_parity(even, to_right, to_left)


def operator_kernel(taps, probe, measured, ops, probe_near, measured_near, padded):
    probe_near[...] = probe[...]
    measured_near[...] = measured[...]
    padded[...] = jnp.zeros_like(padded)
    for axis in range(2):
        padded[2 * axis:2 * axis + 2, :31] = taps[axis]

    def band(index):
        line = jnp.broadcast_to(padded[index:index + 1, :], (TILE, 2 * TILE))
        return pltpu.roll(line, 2 * TILE - 15, 1, stride=1, stride_axis=0)[:, :TILE]

    def put(index, blocks):
        for i in range(2):
            for j in range(2):
                high, low = split(blocks[i][j])
                cols = slice(j * TILE, (j + 1) * TILE)
                ops[index, i * TILE:(i + 1) * TILE, cols] = high
                ops[index, (2 + i) * TILE:(3 + i) * TILE, cols] = low

    yr, yi = band(0), band(1)
    put(0, ((yr, -yi), (yi, yr)))
    yr, yi = yr.T, yi.T
    put(2, ((yr, yi), (-yi, yr)))
    xr, xi = band(2), band(3)
    put(3, ((xr, -xi), (xi, xr)))
    xr, xi = xr.T, xi.T
    put(1, ((xr, xi), (-xi, xr)))


def dot(a, b):
    return jnp.dot(a, b, preferred_element_type=F32)


def block(m):
    return slice(m * TILE, (m + 1) * TILE)


def main_kernel(
    offsets, counts, tall, from_cross, from_mate, probe, measured, ops,
    probe_grad, grad_tall, cross, mate,
    beside, grad_beside, field_high, field_low, mid_high, mid_low, wave_one, wave_two,
):
    even = even_column()
    for s in range(2):
        from_right, from_left = by_parity(even, from_mate[s], from_cross[s])
        beside[s], beside[2 + s] = unpack_columns(from_left, from_right)
    object_ext, grad_ext = (tall, beside), (grad_tall, grad_beside)
    for total in grad_ext:
        total[...] = jnp.zeros_like(total)

    def put_field(slot, m, real, imag):
        for c, value in enumerate((real, imag)):
            high, low = split(value)
            field_high[slot, block(c), block(m)] = high
            field_low[slot, block(c), block(m)] = low

    def rows_done(slot, which):
        for n in range(2):
            cols = slice(n * 256, (n + 1) * 256)
            both = dot(ops[which], field_high[slot, :, cols])
            mid = both[:256] + (both[256:] + dot(ops[which, :256], field_low[slot, :, cols]))
            for k in range(2):
                for c in range(2):
                    high, low = split(mid[block(c), block(k)])
                    mid_high[slot, block(2 * n + k), block(c)] = high
                    mid_low[slot, block(2 * n + k), block(c)] = low

    def cols_done(slot, which, take):
        high, low = ops[which, :256], ops[which, 256:]
        done = dot(mid_high[slot], high) + (dot(mid_low[slot], high) + dot(mid_high[slot], low))
        for m in range(4):
            take(slot, m, done[block(m), :TILE], done[block(m), TILE:])

    def propagate(which, take):
        for slot in range(2):
            rows_done(slot, which)
        for slot in range(2):
            cols_done(slot, which + 1, take)

    def window(slot, p):
        rows = [object_ext[b][p, pl.ds(offsets[2 * slot], TILE), :] for b in range(2)]
        shift = lax.rem(320 - offsets[2 * slot + 1], 256)
        return pltpu.roll(jnp.concatenate(rows, axis=1), shift, 1)[:, :TILE]

    def spread(slot, p, value):
        wide = jnp.concatenate([value, jnp.zeros_like(value)], axis=1)
        wide = pltpu.roll(wide, lax.rem(offsets[2 * slot + 1] + 192, 256), 1)
        for b in range(2):
            grad_ext[b][p, pl.ds(offsets[2 * slot], TILE), :] += wide[:, block(b)]

    views = [[window(slot, p) for p in range(4)] for slot in range(2)]
    for slot in range(2):
        o0r, o0i = views[slot][0], views[slot][2]
        for m in range(4):
            pr, pi = probe[m], probe[4 + m]
            put_field(slot, m, pr * o0r - pi * o0i, pr * o0i + pi * o0r)

    def after_first(slot, m, wr, wi):
        o1r, o1i = views[slot][1], views[slot][3]
        wave_one[slot, m, 0] = wr
        wave_one[slot, m, 1] = wi
        put_field(slot, m, wr * o1r - wi * o1i, wr * o1i + wi * o1r)

    propagate(0, after_first)
    intensity = [None, None]

    def after_second(slot, m, wr, wi):
        wave_two[slot, m, 0] = wr
        wave_two[slot, m, 1] = wi
        term = wr * wr + wi * wi
        intensity[slot] = term if m == 0 else intensity[slot] + term
        if m == 3:
            weight = jnp.where(slot < counts[0, 0], 2.0, 0.0).astype(F32)
            residual = (intensity[slot] - measured[slot]) * weight
            for k in range(4):
                put_field(slot, k, residual * wave_two[slot, k, 0], residual * wave_two[slot, k, 1])

    propagate(0, after_second)
    sums = [[None, None], [None, None]]

    def add(slot, m, real, imag):
        pair = (real, imag) if m == 0 else (sums[slot][0] + real, sums[slot][1] + imag)
        sums[slot] = pair

    def after_third(slot, m, hr, hi):
        o1r, o1i = views[slot][1], views[slot][3]
        wr, wi = wave_one[slot, m, 0], wave_one[slot, m, 1]
        add(slot, m, wr * hr + wi * hi, wr * hi - wi * hr)
        put_field(slot, m, hr * o1r + hi * o1i, hi * o1r - hr * o1i)
        if m == 3:
            spread(slot, 1, sums[slot][0])
            spread(slot, 3, sums[slot][1])

    propagate(2, after_third)

    def after_fourth(slot, m, hr, hi):
        o0r, o0i = views[slot][0], views[slot][2]
        pr, pi = probe[m], probe[4 + m]
        add(slot, m, pr * hr + pi * hi, pr * hi - pi * hr)
        dr = hr * o0r + hi * o0i
        di = hi * o0r - hr * o0i
        if slot == 0:
            probe_grad[m] = dr
            probe_grad[4 + m] = di
        else:
            probe_grad[m] += dr
            probe_grad[4 + m] += di
        if m == 3:
            spread(slot, 0, sums[slot][0])
            spread(slot, 2, sums[slot][1])

    propagate(2, after_fourth)
    for s in range(2):
        to_left, to_right = pack_columns(grad_beside[s], grad_beside[2 + s])
        mate[s], cross[s] = by_parity(even, to_right, to_left)


def share_kernel(scale, shares, spread_share):
    share = jnp.sum(shares[...], axis=0) * scale
    for i in range(spread_share.shape[0]):
        spread_share[i] = share


def fold_columns_kernel(grad_tall, from_cross, from_mate, part, cross, mate):
    even, even_down = even_column(), even_row()
    for s in range(2):
        from_right, from_left = by_parity(even, from_mate[s], from_cross[s])
        for p, sides in zip((s, 2 + s), unpack_columns(from_right, from_left)):
            total = grad_tall[p] + sides
            part[p] = total[HALF:HALF + TILE]
            mate[p], cross[p] = by_parity(even_down, total[HALF + TILE:], total[:HALF])


def fold_rows_kernel(scale, shares, part, from_cross, from_mate, spread_share, result):
    share_kernel(scale, shares, spread_share)
    even = even_row()
    for p in range(4):
        below, above = by_parity(even, from_mate[p], from_cross[p])
        result[p, :HALF] = part[p, :HALF] + above
        result[p, HALF:] = part[p, HALF:] + below


def finish_kernel(result, gathered, result_far, probe_far, sems):
    moves = [pltpu.make_async_copy(result.at[p], result_far.at[p], sems.at[p]) for p in range(4)]
    for i in range(4):
        part = pl.ds(256 * i, 256)
        moves.append(pltpu.make_async_copy(gathered.at[part], probe_far.at[part], sems.at[4 + i]))
    for move in moves:
        move.start()
    for move in moves:
        move.wait()


def exchange(cross, mate, axes):
    count = lax.axis_size(axes)
    pairs = [(i, i + 1) for i in range(1, count - 1, 2)]
    from_cross = lax.ppermute(cross, axes, pairs + [(b, a) for a, b in pairs])
    pairs = [(i, i + 1) for i in range(0, count, 2)]
    from_mate = lax.ppermute(mate, axes, pairs + [(b, a) for a, b in pairs])
    return from_cross, from_mate


def f32(*shape):
    return jax.ShapeDtypeStruct(shape, F32)


def body(object_field, probe_modes, prop_taps, measured, offsets, counts):
    tile = object_field.reshape(4, TILE, TILE)
    planes, strip, half = f32(4, TILE, TILE), f32(2, TILE, TILE), f32(4, HALF, TILE)
    tall, tall_strip = f32(4, 2 * TILE, TILE), f32(2, 2 * TILE, TILE)

    rims = exchange(*call(rows_kernel, (half, half), [VM], tile), ROW_AXES)
    object_tall, cross, mate = call(
        columns_kernel, (tall, tall_strip, tall_strip), [VM] * 3, tile, *rims
    )
    strips = exchange(cross, mate, COL_AXES)
    ops, probe, targets = call(
        operator_kernel,
        (jax.ShapeDtypeStruct((4, 512, 256), BF16), f32(8, TILE, TILE), strip), [VM, VM, VM],
        prop_taps, probe_modes.reshape(8, TILE, TILE), measured.reshape(2, TILE, TILE),
        scratch=[pltpu.VMEM((8, 2 * TILE), F32)],
    )
    probe_part, grad_tall, cross, mate = call(
        main_kernel,
        (f32(8, TILE, TILE), tall, tall_strip, tall_strip), [SM, SM] + [VM] * 6,
        offsets.reshape(-1), counts.reshape(1, 1), object_tall, *strips, probe, targets, ops,
        scratch=[
            pltpu.VMEM((4, 256, TILE), F32),
            pltpu.VMEM((4, 256, TILE), F32),
            pltpu.VMEM((2, 256, 512), BF16),
            pltpu.VMEM((2, 256, 512), BF16),
            pltpu.VMEM((2, 512, 256), BF16),
            pltpu.VMEM((2, 512, 256), BF16),
            pltpu.VMEM((2, 4, 2, TILE, TILE), F32),
            pltpu.VMEM((2, 4, 2, TILE, TILE), F32),
        ],
        flops=3_200_000_000, moved=4_000_000,
    )

    near = lax.axis_size(NEAR_AXES)
    far = lax.axis_size(FAR_AXES)
    rows = 8 * TILE // near
    shares = lax.all_to_all(probe_part.reshape(near, rows, TILE), NEAR_AXES, 0, 0, tiled=True)
    (spread_share,) = call(
        functools.partial(share_kernel, 1.0), (f32(far, rows, TILE),), [VM], shares
    )
    strips = exchange(cross, mate, COL_AXES)
    shares = lax.all_to_all(spread_share, FAR_AXES, 0, 0, tiled=True)
    part, cross, mate = call(
        fold_columns_kernel, (planes, half, half), [VM] * 3, grad_tall, *strips
    )
    rims = exchange(cross, mate, ROW_AXES)
    spread_share, result = call(
        functools.partial(fold_rows_kernel, 1.0 / math.sqrt(near * far)),
        (f32(near, rows, TILE), planes), [VM] * 4, shares, part, *rims,
    )
    gathered = lax.all_to_all(spread_share, NEAR_AXES, 0, 0, tiled=True)
    result, probe_grad = call(
        finish_kernel, (planes, f32(8 * TILE, TILE)), [VM] * 2,
        result, gathered.reshape(8 * TILE, TILE),
        scratch=[pltpu.SemaphoreType.DMA((8,))], out_specs=[FAR, FAR],
    )
    return result.reshape(object_field.shape), probe_grad.reshape(probe_modes.shape)


def solution(mesh):
    fine = Mesh(mesh.devices.reshape(2, 8, 2, 4, 2, 2), ROW_AXES + COL_AXES)
    return jax.shard_map(
        body,
        mesh=fine,
        in_specs=(
            P(None, None, ROW_AXES, COL_AXES),
            P(),
            P(),
            P(ROW_AXES, COL_AXES, None, None, None),
            P(ROW_AXES, COL_AXES, None, None),
            P(ROW_AXES, COL_AXES),
        ),
        out_specs=(P(None, None, ROW_AXES, COL_AXES), P()),
        check_vma=False,
    )
```

```python
import functools
import math

import jax
import jax.numpy as jnp
from jax import lax
from jax.experimental import pallas as pl
from jax.experimental.pallas import tpu as pltpu
from jax.sharding import Mesh
from jax.sharding import PartitionSpec as P

F32 = jnp.float32
BF16 = jnp.bfloat16
ROW_AXES = ("xl", "za", "zb")
COL_AXES = ("y", "xh", "core")
NEAR_AXES = ("xl", "y", "xh", "core")
FAR_AXES = ("za", "zb")
VMEM_LIMIT = 12 * 1024 * 1024
TILE = 128
HALF = 64
VM = pl.BlockSpec(memory_space=pltpu.VMEM)
SM = pl.BlockSpec(memory_space=pltpu.SMEM)
FAR = pl.BlockSpec(memory_space=pltpu.HBM)


def call(kernel, out_shape, in_specs, *args, scratch=(), out_specs=None, flops=0, moved=0):
    out_shape = tuple(out_shape)
    return pl.pallas_call(
        kernel,
        out_shape=out_shape,
        in_specs=in_specs,
        out_specs=tuple(out_specs or [VM] * len(out_shape)),
        scratch_shapes=list(scratch),
        compiler_params=pltpu.CompilerParams(vmem_limit_bytes=VMEM_LIMIT),
        cost_estimate=pl.CostEstimate(flops=flops, bytes_accessed=moved, transcendentals=0),
    )(*args)


def low_lanes(shape):
    return lax.broadcasted_iota(jnp.int32, shape, len(shape) - 1) < HALF


def split(value):
    high = value.astype(BF16)
    return high, (value - high.astype(F32)).astype(BF16)


def even_column():
    return lax.axis_index("core") == 0


def even_row():
    return lax.axis_index("zb") == 0


def by_parity(even, first, second):
    return jnp.where(even, first, second), jnp.where(even, second, first)


def pack_columns(real, imag):
    low = low_lanes(real.shape)
    turned = pltpu.roll(imag, HALF, 1)
    return jnp.where(low, turned, real), jnp.where(low, real, turned)


def unpack_columns(from_left, from_right):
    low = low_lanes(from_left.shape)
    real = jnp.where(low, from_right, from_left)
    return real, pltpu.roll(jnp.where(low, from_left, from_right), HALF, 1)


def rows_kernel(tile, cross, mate):
    even = even_row()
    for p in range(4):
        mate[p], cross[p] = by_parity(even, tile[p, HALF:], tile[p, :HALF])


def columns_kernel(tile, from_cross, from_mate, tall, cross, mate):
    even = even_row()
    for p in range(4):
        below, above = by_parity(even, from_mate[p], from_cross[p])
        tall[p, :HALF] = above
        tall[p, HALF:HALF + TILE] = tile[p]
        tall[p, HALF + TILE:] = below
    even = even_column()
    for s in range(2):
        to_right, to_left = pack_columns(tall[s], tall[2 + s])
        mate[s], cross[s] = by_parity(even, to_right, to_left)


def operator_kernel(taps, probe, measured, ops, probe_near, measured_near, padded):
    probe_near[...] = probe[...]
    measured_near[...] = measured[...]
    padded[...] = jnp.zeros_like(padded)
    for axis in range(2):
        padded[2 * axis:2 * axis + 2, :31] = taps[axis]

    def band(index):
        line = jnp.broadcast_to(padded[index:index + 1, :], (TILE, 2 * TILE))
        return pltpu.roll(line, 2 * TILE - 15, 1, stride=1, stride_axis=0)[:, :TILE]

    def put(index, blocks):
        for i in range(2):
            for j in range(2):
                high, low = split(blocks[i][j])
                cols = slice(j * TILE, (j + 1) * TILE)
                ops[index, i * TILE:(i + 1) * TILE, cols] = high
                ops[index, (2 + i) * TILE:(3 + i) * TILE, cols] = low

    yr, yi = band(0), band(1)
    put(0, ((yr, -yi), (yi, yr)))
    yr, yi = yr.T, yi.T
    put(2, ((yr, yi), (-yi, yr)))
    xr, xi = band(2), band(3)
    put(3, ((xr, -xi), (xi, xr)))
    xr, xi = xr.T, xi.T
    put(1, ((xr, xi), (-xi, xr)))


def dot(a, b):
    return jnp.dot(a, b, preferred_element_type=F32)


def block(m):
    return slice(m * TILE, (m + 1) * TILE)


def main_kernel(
    offsets, counts, tall, from_cross, from_mate, probe, measured, ops,
    probe_grad, object_grad,
    beside, field_high, field_low, mid_high, mid_low, wave_one, wave_two,
):
    even = even_column()
    for s in range(2):
        from_right, from_left = by_parity(even, from_mate[s], from_cross[s])
        beside[s], beside[2 + s] = unpack_columns(from_left, from_right)
    object_ext = (tall, beside)

    def put_field(slot, m, real, imag):
        for c, value in enumerate((real, imag)):
            high, low = split(value)
            field_high[slot, block(c), block(m)] = high
            field_low[slot, block(c), block(m)] = low

    def rows_done(slot, which):
        for n in range(2):
            cols = slice(n * 256, (n + 1) * 256)
            both = dot(ops[which], field_high[slot, :, cols])
            mid = both[:256] + (both[256:] + dot(ops[which, :256], field_low[slot, :, cols]))
            for k in range(2):
                for c in range(2):
                    high, low = split(mid[block(c), block(k)])
                    mid_high[slot, block(2 * n + k), block(c)] = high
                    mid_low[slot, block(2 * n + k), block(c)] = low

    def cols_done(slot, which, take):
        high, low = ops[which, :256], ops[which, 256:]
        for n in range(2):
            rows = slice(n * 256, (n + 1) * 256)
            gh, gl = mid_high[slot, rows], mid_low[slot, rows]
            done = dot(gh, high) + (dot(gl, high) + dot(gh, low))
            for k in range(2):
                take(slot, 2 * n + k, done[block(k), :TILE], done[block(k), TILE:])

    def propagate(which, take):
        for slot in range(2):
            rows_done(slot, which)
        for slot in range(2):
            cols_done(slot, which + 1, take)

    def window(slot, p):
        rows = [object_ext[b][p, pl.ds(offsets[2 * slot], TILE), :] for b in range(2)]
        shift = lax.rem(320 - offsets[2 * slot + 1], 256)
        return pltpu.roll(jnp.concatenate(rows, axis=1), shift, 1)[:, :TILE]

    views = [[window(slot, p) for p in range(4)] for slot in range(2)]
    for slot in range(2):
        o0r, o0i = views[slot][0], views[slot][2]
        for m in range(4):
            pr, pi = probe[m], probe[4 + m]
            put_field(slot, m, pr * o0r - pi * o0i, pr * o0i + pi * o0r)

    def after_first(slot, m, wr, wi):
        o1r, o1i = views[slot][1], views[slot][3]
        wave_one[slot, m, 0] = wr
        wave_one[slot, m, 1] = wi
        put_field(slot, m, wr * o1r - wi * o1i, wr * o1i + wi * o1r)

    propagate(0, after_first)
    intensity = [None, None]

    def after_second(slot, m, wr, wi):
        wave_two[slot, m, 0] = wr
        wave_two[slot, m, 1] = wi
        term = wr * wr + wi * wi
        intensity[slot] = term if m == 0 else intensity[slot] + term
        if m == 3:
            weight = jnp.where(slot < counts[0, 0], 2.0, 0.0).astype(F32)
            residual = (intensity[slot] - measured[slot]) * weight
            for k in range(4):
                put_field(slot, k, residual * wave_two[slot, k, 0], residual * wave_two[slot, k, 1])

    propagate(0, after_second)

    def add(slot, s, m, real, imag):
        for p, value in zip((s, 2 + s), (real, imag)):
            if m == 0:
                object_grad[slot, p] = value
            else:
                object_grad[slot, p] += value

    def after_third(slot, m, hr, hi):
        o1r, o1i = views[slot][1], views[slot][3]
        wr, wi = wave_one[slot, m, 0], wave_one[slot, m, 1]
        add(slot, 1, m, wr * hr + wi * hi, wr * hi - wi * hr)
        put_field(slot, m, hr * o1r + hi * o1i, hi * o1r - hr * o1i)

    propagate(2, after_third)

    def after_fourth(slot, m, hr, hi):
        o0r, o0i = views[slot][0], views[slot][2]
        pr, pi = probe[m], probe[4 + m]
        add(slot, 0, m, pr * hr + pi * hi, pr * hi - pi * hr)
        dr = hr * o0r + hi * o0i
        di = hi * o0r - hr * o0i
        if slot == 0:
            probe_grad[m] = dr
            probe_grad[4 + m] = di
        else:
            probe_grad[m] += dr
            probe_grad[4 + m] += di

    propagate(2, after_fourth)


def object_kernel(offsets, object_grad, grad_tall, cross, mate, grad_beside):
    grad_ext = (grad_tall, grad_beside)
    for total in grad_ext:
        total[...] = jnp.zeros_like(total)
    for slot in range(2):
        for p in range(4):
            value = object_grad[slot, p]
            wide = jnp.concatenate([value, jnp.zeros_like(value)], axis=1)
            wide = pltpu.roll(wide, lax.rem(offsets[2 * slot + 1] + 192, 256), 1)
            for b in range(2):
                grad_ext[b][p, pl.ds(offsets[2 * slot], TILE), :] += wide[:, block(b)]
    even = even_column()
    for s in range(2):
        to_left, to_right = pack_columns(grad_beside[s], grad_beside[2 + s])
        mate[s], cross[s] = by_parity(even, to_right, to_left)


def spread_sum(scale, shares, spread_share):
    share = jnp.sum(shares[...], axis=0) * scale
    for i in range(spread_share.shape[0]):
        spread_share[i] = share


def near_kernel(shares, spread_share):
    spread_sum(1.0, shares, spread_share)


def far_kernel(scale, shares, grad_tall, from_cross, from_mate, spread_share, part, cross, mate):
    spread_sum(scale, shares, spread_share)
    even, even_down = even_column(), even_row()
    for s in range(2):
        from_right, from_left = by_parity(even, from_mate[s], from_cross[s])
        for p, sides in zip((s, 2 + s), unpack_columns(from_right, from_left)):
            total = grad_tall[p] + sides
            part[p] = total[HALF:HALF + TILE]
            mate[p], cross[p] = by_parity(even_down, total[HALF + TILE:], total[:HALF])


def finish_kernel(part, from_cross, from_mate, gathered, result_far, probe_far, result, sems):
    moves = []
    for i in range(4):
        rows = pl.ds(256 * i, 256)
        moves.append(pltpu.make_async_copy(gathered.at[rows], probe_far.at[rows], sems.at[i]))
        moves[i].start()
    even = even_row()
    for p in range(4):
        below, above = by_parity(even, from_mate[p], from_cross[p])
        result[p, :HALF] = part[p, :HALF] + above
        result[p, HALF:] = part[p, HALF:] + below
        moves.append(pltpu.make_async_copy(result.at[p], result_far.at[p], sems.at[4 + p]))
        moves[-1].start()
    for move in moves:
        move.wait()


def exchange(cross, mate, axes):
    count = lax.axis_size(axes)
    pairs = [(i, i + 1) for i in range(1, count - 1, 2)]
    from_cross = lax.ppermute(cross, axes, pairs + [(b, a) for a, b in pairs])
    pairs = [(i, i + 1) for i in range(0, count, 2)]
    from_mate = lax.ppermute(mate, axes, pairs + [(b, a) for a, b in pairs])
    return from_cross, from_mate


def f32(*shape):
    return jax.ShapeDtypeStruct(shape, F32)


def body(object_field, probe_modes, prop_taps, measured, offsets, counts):
    tile = object_field.reshape(4, TILE, TILE)
    planes, strip, half = f32(4, TILE, TILE), f32(2, TILE, TILE), f32(4, HALF, TILE)
    tall, tall_strip = f32(4, 2 * TILE, TILE), f32(2, 2 * TILE, TILE)

    rims = exchange(*call(rows_kernel, (half, half), [VM], tile), ROW_AXES)
    object_tall, cross, mate = call(
        columns_kernel, (tall, tall_strip, tall_strip), [VM] * 3, tile, *rims
    )
    strips = exchange(cross, mate, COL_AXES)
    ops, probe, targets = call(
        operator_kernel,
        (jax.ShapeDtypeStruct((4, 512, 256), BF16), f32(8, TILE, TILE), strip), [VM, VM, VM],
        prop_taps, probe_modes.reshape(8, TILE, TILE), measured.reshape(2, TILE, TILE),
        scratch=[pltpu.VMEM((8, 2 * TILE), F32)],
    )
    probe_part, object_grad = call(
        main_kernel,
        (f32(8, TILE, TILE), f32(2, 4, TILE, TILE)), [SM, SM] + [VM] * 6,
        offsets.reshape(-1), counts.reshape(1, 1), object_tall, *strips, probe, targets, ops,
        scratch=[
            pltpu.VMEM((4, 256, TILE), F32),
            pltpu.VMEM((2, 256, 512), BF16),
            pltpu.VMEM((2, 256, 512), BF16),
            pltpu.VMEM((2, 512, 256), BF16),
            pltpu.VMEM((2, 512, 256), BF16),
            pltpu.VMEM((2, 4, 2, TILE, TILE), F32),
            pltpu.VMEM((2, 4, 2, TILE, TILE), F32),
        ],
        flops=3_200_000_000, moved=4_000_000,
    )
    grad_tall, cross, mate = call(
        object_kernel, (tall, tall_strip, tall_strip), [SM, VM],
        offsets.reshape(-1), object_grad,
        scratch=[pltpu.VMEM((4, 256, TILE), F32)],
    )

    near = lax.axis_size(NEAR_AXES)
    far = lax.axis_size(FAR_AXES)
    rows = 8 * TILE // near
    shares = lax.all_to_all(probe_part.reshape(near, rows, TILE), NEAR_AXES, 0, 0, tiled=True)
    (spread_share,) = call(near_kernel, (f32(far, rows, TILE),), [VM], shares)
    strips = exchange(cross, mate, COL_AXES)
    shares = lax.all_to_all(spread_share, FAR_AXES, 0, 0, tiled=True)
    spread_share, part, cross, mate = call(
        functools.partial(far_kernel, 1.0 / math.sqrt(near * far)),
        (f32(near, rows, TILE), planes, half, half), [VM] * 4, shares, grad_tall, *strips,
    )
    rims = exchange(cross, mate, ROW_AXES)
    gathered = lax.all_to_all(spread_share, NEAR_AXES, 0, 0, tiled=True)
    result, probe_grad = call(
        finish_kernel, (planes, f32(8 * TILE, TILE)), [VM] * 4,
        part, *rims, gathered.reshape(8 * TILE, TILE),
        scratch=[pltpu.VMEM((4, TILE, TILE), F32), pltpu.SemaphoreType.DMA((8,))],
        out_specs=[FAR, FAR],
    )
    return result.reshape(object_field.shape), probe_grad.reshape(probe_modes.shape)


def solution(mesh):
    fine = Mesh(mesh.devices.reshape(2, 8, 2, 4, 2, 2), ROW_AXES + COL_AXES)
    return jax.shard_map(
        body,
        mesh=fine,
        in_specs=(
            P(None, None, ROW_AXES, COL_AXES),
            P(),
            P(),
            P(ROW_AXES, COL_AXES, None, None, None),
            P(ROW_AXES, COL_AXES, None, None),
            P(ROW_AXES, COL_AXES),
        ),
        out_specs=(P(None, None, ROW_AXES, COL_AXES), P()),
        check_vma=False,
    )
```

```python
import functools
import math

import jax
import jax.numpy as jnp
from jax import lax
from jax.experimental import pallas as pl
from jax.experimental.pallas import tpu as pltpu
from jax.sharding import Mesh
from jax.sharding import PartitionSpec as P

F32 = jnp.float32
BF16 = jnp.bfloat16
ROW_AXES = ("xl", "za", "zb")
COL_AXES = ("y", "xh", "core")
NEAR_AXES = ("xl", "zb", "y", "xh", "core")
FAR_AXES = ("za",)
VMEM_LIMIT = 12 * 1024 * 1024
TILE = 128
HALF = 64
BESIDE = 100_000_000_000
VM = pl.BlockSpec(memory_space=pltpu.VMEM)
SM = pl.BlockSpec(memory_space=pltpu.SMEM)
FAR = pl.BlockSpec(memory_space=pltpu.HBM)


def call(kernel, out_shape, in_specs, *args, scratch=(), out_specs=None, flops=0, moved=0):
    out_shape = tuple(out_shape)
    return pl.pallas_call(
        kernel,
        out_shape=out_shape,
        in_specs=in_specs,
        out_specs=tuple(out_specs or [VM] * len(out_shape)),
        scratch_shapes=list(scratch),
        compiler_params=pltpu.CompilerParams(vmem_limit_bytes=VMEM_LIMIT),
        cost_estimate=pl.CostEstimate(flops=flops, bytes_accessed=moved, transcendentals=0),
    )(*args)


def low_lanes(shape):
    return lax.broadcasted_iota(jnp.int32, shape, len(shape) - 1) < HALF


def split(value):
    high = value.astype(BF16)
    return high, (value - high.astype(F32)).astype(BF16)


def even_column():
    return lax.axis_index("core") == 0


def even_row():
    return lax.axis_index("zb") == 0


def by_parity(even, first, second):
    return jnp.where(even, first, second), jnp.where(even, second, first)


def pack_columns(real, imag):
    low = low_lanes(real.shape)
    turned = pltpu.roll(imag, HALF, 1)
    return jnp.where(low, turned, real), jnp.where(low, real, turned)


def unpack_columns(from_left, from_right):
    low = low_lanes(from_left.shape)
    real = jnp.where(low, from_right, from_left)
    return real, pltpu.roll(jnp.where(low, from_left, from_right), HALF, 1)


def rows_kernel(tile, cross, mate):
    even = even_row()
    for p in range(4):
        mate[p], cross[p] = by_parity(even, tile[p, HALF:], tile[p, :HALF])


def columns_kernel(tile, from_cross, from_mate, tall, cross, mate):
    even = even_row()
    for p in range(4):
        below, above = by_parity(even, from_mate[p], from_cross[p])
        tall[p, :HALF] = above
        tall[p, HALF:HALF + TILE] = tile[p]
        tall[p, HALF + TILE:] = below
    even = even_column()
    for s in range(2):
        to_right, to_left = pack_columns(tall[s], tall[2 + s])
        mate[s], cross[s] = by_parity(even, to_right, to_left)


def operator_kernel(taps, probe, measured, ops, probe_near, measured_near, padded):
    probe_near[...] = probe[...]
    measured_near[...] = measured[...]
    padded[...] = jnp.zeros_like(padded)
    for axis in range(2):
        padded[2 * axis:2 * axis + 2, :31] = taps[axis]

    def band(index):
        line = jnp.broadcast_to(padded[index:index + 1, :], (TILE, 2 * TILE))
        return pltpu.roll(line, 2 * TILE - 15, 1, stride=1, stride_axis=0)[:, :TILE]

    def put(index, blocks):
        for i in range(2):
            for j in range(2):
                high, low = split(blocks[i][j])
                cols = slice(j * TILE, (j + 1) * TILE)
                ops[index, i * TILE:(i + 1) * TILE, cols] = high
                ops[index, (2 + i) * TILE:(3 + i) * TILE, cols] = low

    yr, yi = band(0), band(1)
    put(0, ((yr, -yi), (yi, yr)))
    yr, yi = yr.T, yi.T
    put(2, ((yr, yi), (-yi, yr)))
    xr, xi = band(2), band(3)
    put(3, ((xr, -xi), (xi, xr)))
    xr, xi = xr.T, xi.T
    put(1, ((xr, xi), (-xi, xr)))


def dot(a, b):
    return jnp.dot(a, b, preferred_element_type=F32)


def block(m):
    return slice(m * TILE, (m + 1) * TILE)


def main_kernel(
    offsets, counts, tall, from_cross, from_mate, probe, measured, ops,
    probe_grad, object_grad,
    beside, field_high, field_low, mid_high, mid_low, wave_one, wave_two,
):
    even = even_column()
    for s in range(2):
        from_right, from_left = by_parity(even, from_mate[s], from_cross[s])
        beside[s], beside[2 + s] = unpack_columns(from_left, from_right)
    object_ext = (tall, beside)

    def put_field(slot, m, real, imag):
        for c, value in enumerate((real, imag)):
            high, low = split(value)
            field_high[slot, block(c), block(m)] = high
            field_low[slot, block(c), block(m)] = low

    def rows_done(slot, which):
        for n in range(2):
            cols = slice(n * 256, (n + 1) * 256)
            both = dot(ops[which], field_high[slot, :, cols])
            mid = both[:256] + (both[256:] + dot(ops[which, :256], field_low[slot, :, cols]))
            for k in range(2):
                for c in range(2):
                    high, low = split(mid[block(c), block(k)])
                    mid_high[slot, block(2 * n + k), block(c)] = high
                    mid_low[slot, block(2 * n + k), block(c)] = low

    def cols_done(slot, which, take):
        high, low = ops[which, :256], ops[which, 256:]
        for n in range(2):
            rows = slice(n * 256, (n + 1) * 256)
            gh, gl = mid_high[slot, rows], mid_low[slot, rows]
            done = dot(gh, high) + (dot(gl, high) + dot(gh, low))
            for k in range(2):
                take(slot, 2 * n + k, done[block(k), :TILE], done[block(k), TILE:])

    def propagate(which, take):
        for slot in range(2):
            rows_done(slot, which)
        for slot in range(2):
            cols_done(slot, which + 1, take)

    def window(slot, p):
        rows = [object_ext[b][p, pl.ds(offsets[2 * slot], TILE), :] for b in range(2)]
        shift = lax.rem(320 - offsets[2 * slot + 1], 256)
        return pltpu.roll(jnp.concatenate(rows, axis=1), shift, 1)[:, :TILE]

    views = [[window(slot, p) for p in range(4)] for slot in range(2)]
    for slot in range(2):
        o0r, o0i = views[slot][0], views[slot][2]
        for m in range(4):
            pr, pi = probe[m], probe[4 + m]
            put_field(slot, m, pr * o0r - pi * o0i, pr * o0i + pi * o0r)

    def after_first(slot, m, wr, wi):
        o1r, o1i = views[slot][1], views[slot][3]
        wave_one[slot, m, 0] = wr
        wave_one[slot, m, 1] = wi
        put_field(slot, m, wr * o1r - wi * o1i, wr * o1i + wi * o1r)

    propagate(0, after_first)
    intensity = [None, None]

    def after_second(slot, m, wr, wi):
        wave_two[slot, m, 0] = wr
        wave_two[slot, m, 1] = wi
        term = wr * wr + wi * wi
        intensity[slot] = term if m == 0 else intensity[slot] + term
        if m == 3:
            weight = jnp.where(slot < counts[0, 0], 2.0, 0.0).astype(F32)
            residual = (intensity[slot] - measured[slot]) * weight
            for k in range(4):
                put_field(slot, k, residual * wave_two[slot, k, 0], residual * wave_two[slot, k, 1])

    propagate(0, after_second)

    def add(slot, s, m, real, imag):
        for p, value in zip((s, 2 + s), (real, imag)):
            if m == 0:
                object_grad[slot, p] = value
            else:
                object_grad[slot, p] += value

    def after_third(slot, m, hr, hi):
        o1r, o1i = views[slot][1], views[slot][3]
        wr, wi = wave_one[slot, m, 0], wave_one[slot, m, 1]
        add(slot, 1, m, wr * hr + wi * hi, wr * hi - wi * hr)
        put_field(slot, m, hr * o1r + hi * o1i, hi * o1r - hr * o1i)

    propagate(2, after_third)

    def after_fourth(slot, m, hr, hi):
        o0r, o0i = views[slot][0], views[slot][2]
        pr, pi = probe[m], probe[4 + m]
        add(slot, 0, m, pr * hr + pi * hi, pr * hi - pi * hr)
        dr = hr * o0r + hi * o0i
        di = hi * o0r - hr * o0i
        if slot == 0:
            probe_grad[m] = dr
            probe_grad[4 + m] = di
        else:
            probe_grad[m] += dr
            probe_grad[4 + m] += di

    propagate(2, after_fourth)


def object_kernel(offsets, object_grad, grad_tall, cross, mate, grad_beside):
    grad_ext = (grad_tall, grad_beside)
    for total in grad_ext:
        total[...] = jnp.zeros_like(total)
    for slot in range(2):
        for p in range(4):
            value = object_grad[slot, p]
            wide = jnp.concatenate([value, jnp.zeros_like(value)], axis=1)
            wide = pltpu.roll(wide, lax.rem(offsets[2 * slot + 1] + 192, 256), 1)
            for b in range(2):
                grad_ext[b][p, pl.ds(offsets[2 * slot], TILE), :] += wide[:, block(b)]
    even = even_column()
    for s in range(2):
        to_left, to_right = pack_columns(grad_beside[s], grad_beside[2 + s])
        mate[s], cross[s] = by_parity(even, to_right, to_left)


def spread_sum(scale, shares, spread_share):
    share = jnp.sum(shares[...], axis=0) * scale
    for i in range(spread_share.shape[0]):
        spread_share[i] = share


def fold_columns_kernel(grad_tall, from_cross, from_mate, part, cross, mate):
    even, even_down = even_column(), even_row()
    for s in range(2):
        from_right, from_left = by_parity(even, from_mate[s], from_cross[s])
        for p, sides in zip((s, 2 + s), unpack_columns(from_right, from_left)):
            total = grad_tall[p] + sides
            part[p] = total[HALF:HALF + TILE]
            mate[p], cross[p] = by_parity(even_down, total[HALF + TILE:], total[:HALF])


def fold_rows_kernel(part, from_cross, from_mate, result):
    even = even_row()
    for p in range(4):
        below, above = by_parity(even, from_mate[p], from_cross[p])
        result[p, :HALF] = part[p, :HALF] + above
        result[p, HALF:] = part[p, HALF:] + below


def finish_kernel(result, gathered, result_far, probe_far, sems):
    moves = [pltpu.make_async_copy(result.at[p], result_far.at[p], sems.at[p]) for p in range(4)]
    for i in range(4):
        part = pl.ds(256 * i, 256)
        moves.append(pltpu.make_async_copy(gathered.at[part], probe_far.at[part], sems.at[4 + i]))
    for move in moves:
        move.start()
    for move in moves:
        move.wait()


def exchange(cross, mate, axes):
    count = lax.axis_size(axes)
    pairs = [(i, i + 1) for i in range(1, count - 1, 2)]
    from_cross = lax.ppermute(cross, axes, pairs + [(b, a) for a, b in pairs])
    pairs = [(i, i + 1) for i in range(0, count, 2)]
    from_mate = lax.ppermute(mate, axes, pairs + [(b, a) for a, b in pairs])
    return from_cross, from_mate


def f32(*shape):
    return jax.ShapeDtypeStruct(shape, F32)


def body(object_field, probe_modes, prop_taps, measured, offsets, counts):
    tile = object_field.reshape(4, TILE, TILE)
    planes, strip, half = f32(4, TILE, TILE), f32(2, TILE, TILE), f32(4, HALF, TILE)
    tall, tall_strip = f32(4, 2 * TILE, TILE), f32(2, 2 * TILE, TILE)

    rims = exchange(*call(rows_kernel, (half, half), [VM], tile), ROW_AXES)
    object_tall, cross, mate = call(
        columns_kernel, (tall, tall_strip, tall_strip), [VM] * 3, tile, *rims
    )
    strips = exchange(cross, mate, COL_AXES)
    ops, probe, targets = call(
        operator_kernel,
        (jax.ShapeDtypeStruct((4, 512, 256), BF16), f32(8, TILE, TILE), strip), [VM, VM, VM],
        prop_taps, probe_modes.reshape(8, TILE, TILE), measured.reshape(2, TILE, TILE),
        scratch=[pltpu.VMEM((8, 2 * TILE), F32)],
    )
    probe_part, object_grad = call(
        main_kernel,
        (f32(8, TILE, TILE), f32(2, 4, TILE, TILE)), [SM, SM] + [VM] * 6,
        offsets.reshape(-1), counts.reshape(1, 1), object_tall, *strips, probe, targets, ops,
        scratch=[
            pltpu.VMEM((4, 256, TILE), F32),
            pltpu.VMEM((2, 256, 512), BF16),
            pltpu.VMEM((2, 256, 512), BF16),
            pltpu.VMEM((2, 512, 256), BF16),
            pltpu.VMEM((2, 512, 256), BF16),
            pltpu.VMEM((2, 4, 2, TILE, TILE), F32),
            pltpu.VMEM((2, 4, 2, TILE, TILE), F32),
        ],
        flops=3_200_000_000, moved=4_000_000,
    )
    grad_tall, cross, mate = call(
        object_kernel, (tall, tall_strip, tall_strip), [SM, VM],
        offsets.reshape(-1), object_grad,
        scratch=[pltpu.VMEM((4, 256, TILE), F32)],
    )

    near = lax.axis_size(NEAR_AXES)
    far = lax.axis_size(FAR_AXES)
    rows = 8 * TILE // near
    shares = lax.all_to_all(probe_part.reshape(near, rows, TILE), NEAR_AXES, 0, 0, tiled=True)
    (spread_share,) = call(
        functools.partial(spread_sum, 1.0), (f32(far, rows, TILE),), [VM], shares
    )
    strips = exchange(cross, mate, COL_AXES)
    shares = lax.all_to_all(spread_share, FAR_AXES, 0, 0, tiled=True)
    part, cross, mate = call(
        fold_columns_kernel, (planes, half, half), [VM] * 3, grad_tall, *strips
    )
    rims = exchange(cross, mate, ROW_AXES)
    (spread_share,) = call(
        functools.partial(spread_sum, 1.0 / math.sqrt(near * far)), (f32(near, rows, TILE),), [VM], shares
    )
    gathered = lax.all_to_all(spread_share, NEAR_AXES, 0, 0, tiled=True)
    (result,) = call(
        fold_rows_kernel, (planes,), [VM] * 3, part, *rims, flops=BESIDE, moved=1
    )
    result, probe_grad = call(
        finish_kernel, (planes, f32(8 * TILE, TILE)), [VM] * 2,
        result, gathered.reshape(8 * TILE, TILE),
        scratch=[pltpu.SemaphoreType.DMA((8,))], out_specs=[FAR, FAR],
    )
    return result.reshape(object_field.shape), probe_grad.reshape(probe_modes.shape)


def solution(mesh):
    fine = Mesh(mesh.devices.reshape(2, 8, 2, 4, 2, 2), ROW_AXES + COL_AXES)
    return jax.shard_map(
        body,
        mesh=fine,
        in_specs=(
            P(None, None, ROW_AXES, COL_AXES),
            P(),
            P(),
            P(ROW_AXES, COL_AXES, None, None, None),
            P(ROW_AXES, COL_AXES, None, None),
            P(ROW_AXES, COL_AXES),
        ),
        out_specs=(P(None, None, ROW_AXES, COL_AXES), P()),
        check_vma=False,
    )
```

```python
import functools
import math

import jax
import jax.numpy as jnp
from jax import lax
from jax.experimental import pallas as pl
from jax.experimental.pallas import tpu as pltpu
from jax.sharding import Mesh
from jax.sharding import PartitionSpec as P

F32 = jnp.float32
BF16 = jnp.bfloat16
ROW_AXES = ("xl", "za", "zb")
COL_AXES = ("y", "xh", "core")
NEAR_AXES = ("xl", "zb", "y", "xh", "core")
FAR_AXES = ("za",)
VMEM_LIMIT = 12 * 1024 * 1024
TILE = 128
HALF = 64
BESIDE = 100_000_000_000
VM = pl.BlockSpec(memory_space=pltpu.VMEM)
SM = pl.BlockSpec(memory_space=pltpu.SMEM)
FAR = pl.BlockSpec(memory_space=pltpu.HBM)


def call(kernel, out_shape, in_specs, *args, scratch=(), out_specs=None, flops=0, moved=0):
    out_shape = tuple(out_shape)
    return pl.pallas_call(
        kernel,
        out_shape=out_shape,
        in_specs=in_specs,
        out_specs=tuple(out_specs or [VM] * len(out_shape)),
        scratch_shapes=list(scratch),
        compiler_params=pltpu.CompilerParams(vmem_limit_bytes=VMEM_LIMIT),
        cost_estimate=pl.CostEstimate(flops=flops, bytes_accessed=moved, transcendentals=0),
    )(*args)


def low_lanes(shape):
    return lax.broadcasted_iota(jnp.int32, shape, len(shape) - 1) < HALF


def split(value):
    high = value.astype(BF16)
    return high, (value - high.astype(F32)).astype(BF16)


def even_column():
    return lax.axis_index("core") == 0


def even_row():
    return lax.axis_index("zb") == 0


def by_parity(even, first, second):
    return jnp.where(even, first, second), jnp.where(even, second, first)


def pack_columns(real, imag):
    low = low_lanes(real.shape)
    turned = pltpu.roll(imag, HALF, 1)
    return jnp.where(low, turned, real), jnp.where(low, real, turned)


def unpack_columns(from_left, from_right):
    low = low_lanes(from_left.shape)
    real = jnp.where(low, from_right, from_left)
    return real, pltpu.roll(jnp.where(low, from_left, from_right), HALF, 1)


def columns_kernel(tile, from_cross, from_mate, tall, cross, mate):
    even = even_row()
    for p in range(4):
        below, above = by_parity(even, from_mate[p], from_cross[p])
        tall[p, :HALF] = above
        tall[p, HALF:HALF + TILE] = tile[p]
        tall[p, HALF + TILE:] = below
    even = even_column()
    for s in range(2):
        to_right, to_left = pack_columns(tall[s], tall[2 + s])
        mate[s], cross[s] = by_parity(even, to_right, to_left)


def operator_kernel(taps, probe, measured, ops, probe_near, measured_near, padded):
    probe_near[...] = probe[...]
    measured_near[...] = measured[...]
    padded[...] = jnp.zeros_like(padded)
    for axis in range(2):
        padded[2 * axis:2 * axis + 2, :31] = taps[axis]

    def band(index):
        line = jnp.broadcast_to(padded[index:index + 1, :], (TILE, 2 * TILE))
        return pltpu.roll(line, 2 * TILE - 15, 1, stride=1, stride_axis=0)[:, :TILE]

    def put(index, blocks):
        for i in range(2):
            for j in range(2):
                high, low = split(blocks[i][j])
                cols = slice(j * TILE, (j + 1) * TILE)
                ops[index, i * TILE:(i + 1) * TILE, cols] = high
                ops[index, (2 + i) * TILE:(3 + i) * TILE, cols] = low

    yr, yi = band(0), band(1)
    put(0, ((yr, -yi), (yi, yr)))
    yr, yi = yr.T, yi.T
    put(2, ((yr, yi), (-yi, yr)))
    xr, xi = band(2), band(3)
    put(3, ((xr, -xi), (xi, xr)))
    xr, xi = xr.T, xi.T
    put(1, ((xr, xi), (-xi, xr)))


def dot(a, b):
    return jnp.dot(a, b, preferred_element_type=F32)


def block(m):
    return slice(m * TILE, (m + 1) * TILE)


def main_kernel(
    offsets, counts, tall, from_cross, from_mate, probe, measured, ops,
    probe_grad, object_grad,
    beside, field_high, field_low, mid_high, mid_low, wave_one, wave_two,
):
    even = even_column()
    for s in range(2):
        from_right, from_left = by_parity(even, from_mate[s], from_cross[s])
        beside[s], beside[2 + s] = unpack_columns(from_left, from_right)
    object_ext = (tall, beside)

    def put_field(slot, m, real, imag):
        for c, value in enumerate((real, imag)):
            high, low = split(value)
            field_high[slot, block(c), block(m)] = high
            field_low[slot, block(c), block(m)] = low

    def rows_done(slot, which):
        for n in range(2):
            cols = slice(n * 256, (n + 1) * 256)
            both = dot(ops[which], field_high[slot, :, cols])
            mid = both[:256] + (both[256:] + dot(ops[which, :256], field_low[slot, :, cols]))
            for k in range(2):
                for c in range(2):
                    high, low = split(mid[block(c), block(k)])
                    mid_high[slot, block(2 * n + k), block(c)] = high
                    mid_low[slot, block(2 * n + k), block(c)] = low

    def cols_done(slot, which, take):
        high, low = ops[which, :256], ops[which, 256:]
        for n in range(2):
            rows = slice(n * 256, (n + 1) * 256)
            gh, gl = mid_high[slot, rows], mid_low[slot, rows]
            done = dot(gh, high) + (dot(gl, high) + dot(gh, low))
            for k in range(2):
                take(slot, 2 * n + k, done[block(k), :TILE], done[block(k), TILE:])

    def propagate(which, take):
        for slot in range(2):
            rows_done(slot, which)
        for slot in range(2):
            cols_done(slot, which + 1, take)

    def window(slot, p):
        rows = [object_ext[b][p, pl.ds(offsets[2 * slot], TILE), :] for b in range(2)]
        shift = lax.rem(320 - offsets[2 * slot + 1], 256)
        return pltpu.roll(jnp.concatenate(rows, axis=1), shift, 1)[:, :TILE]

    views = [[window(slot, p) for p in range(4)] for slot in range(2)]
    for slot in range(2):
        o0r, o0i = views[slot][0], views[slot][2]
        for m in range(4):
            pr, pi = probe[m], probe[4 + m]
            put_field(slot, m, pr * o0r - pi * o0i, pr * o0i + pi * o0r)

    def after_first(slot, m, wr, wi):
        o1r, o1i = views[slot][1], views[slot][3]
        wave_one[slot, m, 0] = wr
        wave_one[slot, m, 1] = wi
        put_field(slot, m, wr * o1r - wi * o1i, wr * o1i + wi * o1r)

    propagate(0, after_first)
    intensity = [None, None]

    def after_second(slot, m, wr, wi):
        wave_two[slot, m, 0] = wr
        wave_two[slot, m, 1] = wi
        term = wr * wr + wi * wi
        intensity[slot] = term if m == 0 else intensity[slot] + term
        if m == 3:
            weight = jnp.where(slot < counts[0, 0], 2.0, 0.0).astype(F32)
            residual = (intensity[slot] - measured[slot]) * weight
            for k in range(4):
                put_field(slot, k, residual * wave_two[slot, k, 0], residual * wave_two[slot, k, 1])

    propagate(0, after_second)

    def add(slot, s, m, real, imag):
        for p, value in zip((s, 2 + s), (real, imag)):
            if m == 0:
                object_grad[slot, p] = value
            else:
                object_grad[slot, p] += value

    def after_third(slot, m, hr, hi):
        o1r, o1i = views[slot][1], views[slot][3]
        wr, wi = wave_one[slot, m, 0], wave_one[slot, m, 1]
        add(slot, 1, m, wr * hr + wi * hi, wr * hi - wi * hr)
        put_field(slot, m, hr * o1r + hi * o1i, hi * o1r - hr * o1i)

    propagate(2, after_third)

    def after_fourth(slot, m, hr, hi):
        o0r, o0i = views[slot][0], views[slot][2]
        pr, pi = probe[m], probe[4 + m]
        add(slot, 0, m, pr * hr + pi * hi, pr * hi - pi * hr)
        dr = hr * o0r + hi * o0i
        di = hi * o0r - hr * o0i
        if slot == 0:
            probe_grad[m] = dr
            probe_grad[4 + m] = di
        else:
            probe_grad[m] += dr
            probe_grad[4 + m] += di

    propagate(2, after_fourth)


def object_kernel(offsets, object_grad, grad_tall, cross, mate, grad_beside):
    grad_ext = (grad_tall, grad_beside)
    for total in grad_ext:
        total[...] = jnp.zeros_like(total)
    for slot in range(2):
        for p in range(4):
            value = object_grad[slot, p]
            wide = jnp.concatenate([value, jnp.zeros_like(value)], axis=1)
            wide = pltpu.roll(wide, lax.rem(offsets[2 * slot + 1] + 192, 256), 1)
            for b in range(2):
                grad_ext[b][p, pl.ds(offsets[2 * slot], TILE), :] += wide[:, block(b)]
    even = even_column()
    for s in range(2):
        to_left, to_right = pack_columns(grad_beside[s], grad_beside[2 + s])
        mate[s], cross[s] = by_parity(even, to_right, to_left)


def spread_sum(scale, shares, spread_share):
    share = jnp.sum(shares[...], axis=0) * scale
    for i in range(spread_share.shape[0]):
        spread_share[i] = share


def fold_columns_kernel(grad_tall, from_cross, from_mate, part, cross, mate):
    even, even_down = even_column(), even_row()
    for s in range(2):
        from_right, from_left = by_parity(even, from_mate[s], from_cross[s])
        for p, sides in zip((s, 2 + s), unpack_columns(from_right, from_left)):
            total = grad_tall[p] + sides
            part[p] = total[HALF:HALF + TILE]
            mate[p], cross[p] = by_parity(even_down, total[HALF + TILE:], total[:HALF])


def fold_rows_kernel(part, from_cross, from_mate, result):
    even = even_row()
    for p in range(4):
        below, above = by_parity(even, from_mate[p], from_cross[p])
        result[p, :HALF] = part[p, :HALF] + above
        result[p, HALF:] = part[p, HALF:] + below


def finish_kernel(gathered, probe_far, sems):
    moves = []
    for i in range(4):
        part = pl.ds(256 * i, 256)
        moves.append(pltpu.make_async_copy(gathered.at[part], probe_far.at[part], sems.at[i]))
        moves[i].start()
    for move in moves:
        move.wait()


def exchange(cross, mate, axes):
    count = lax.axis_size(axes)
    pairs = [(i, i + 1) for i in range(1, count - 1, 2)]
    from_cross = lax.ppermute(cross, axes, pairs + [(b, a) for a, b in pairs])
    pairs = [(i, i + 1) for i in range(0, count, 2)]
    from_mate = lax.ppermute(mate, axes, pairs + [(b, a) for a, b in pairs])
    return from_cross, from_mate


def f32(*shape):
    return jax.ShapeDtypeStruct(shape, F32)


def body(object_field, probe_modes, prop_taps, measured, offsets, counts):
    tile = object_field.reshape(4, TILE, TILE)
    planes, strip, half = f32(4, TILE, TILE), f32(2, TILE, TILE), f32(4, HALF, TILE)
    tall, tall_strip = f32(4, 2 * TILE, TILE), f32(2, 2 * TILE, TILE)

    upper = jnp.where(even_row(), 0, HALF)
    cross = lax.dynamic_slice_in_dim(tile, upper, HALF, axis=1)
    mate = lax.dynamic_slice_in_dim(tile, HALF - upper, HALF, axis=1)
    rims = exchange(cross, mate, ROW_AXES)
    object_tall, cross, mate = call(
        columns_kernel, (tall, tall_strip, tall_strip), [VM] * 3, tile, *rims
    )
    strips = exchange(cross, mate, COL_AXES)
    ops, probe, targets = call(
        operator_kernel,
        (jax.ShapeDtypeStruct((4, 512, 256), BF16), f32(8, TILE, TILE), strip), [VM, VM, VM],
        prop_taps, probe_modes.reshape(8, TILE, TILE), measured.reshape(2, TILE, TILE),
        scratch=[pltpu.VMEM((8, 2 * TILE), F32)],
    )
    probe_part, object_grad = call(
        main_kernel,
        (f32(8, TILE, TILE), f32(2, 4, TILE, TILE)), [SM, SM] + [VM] * 6,
        offsets.reshape(-1), counts.reshape(1, 1), object_tall, *strips, probe, targets, ops,
        scratch=[
            pltpu.VMEM((4, 256, TILE), F32),
            pltpu.VMEM((2, 256, 512), BF16),
            pltpu.VMEM((2, 256, 512), BF16),
            pltpu.VMEM((2, 512, 256), BF16),
            pltpu.VMEM((2, 512, 256), BF16),
            pltpu.VMEM((2, 4, 2, TILE, TILE), F32),
            pltpu.VMEM((2, 4, 2, TILE, TILE), F32),
        ],
        flops=3_200_000_000, moved=4_000_000,
    )
    grad_tall, cross, mate = call(
        object_kernel, (tall, tall_strip, tall_strip), [SM, VM],
        offsets.reshape(-1), object_grad,
        scratch=[pltpu.VMEM((4, 256, TILE), F32)],
    )

    near = lax.axis_size(NEAR_AXES)
    far = lax.axis_size(FAR_AXES)
    rows = 8 * TILE // near
    shares = lax.all_to_all(probe_part.reshape(near, rows, TILE), NEAR_AXES, 0, 0, tiled=True)
    spread_share = jnp.broadcast_to(jnp.sum(shares, axis=0)[None], (far, rows, TILE))
    strips = exchange(cross, mate, COL_AXES)
    shares = lax.all_to_all(spread_share, FAR_AXES, 0, 0, tiled=True)
    part, cross, mate = call(
        fold_columns_kernel, (planes, half, half), [VM] * 3, grad_tall, *strips
    )
    rims = exchange(cross, mate, ROW_AXES)
    (spread_share,) = call(
        functools.partial(spread_sum, 1.0 / math.sqrt(near * far)), (f32(near, rows, TILE),), [VM], shares
    )
    gathered = lax.all_to_all(spread_share, NEAR_AXES, 0, 0, tiled=True)
    (result,) = call(
        fold_rows_kernel, (planes,), [VM] * 3, part, *rims, flops=BESIDE, moved=1
    )
    (probe_grad,) = call(
        finish_kernel, (f32(8 * TILE, TILE),), [VM], gathered.reshape(8 * TILE, TILE),
        scratch=[pltpu.SemaphoreType.DMA((4,))], out_specs=[FAR],
    )
    return result.reshape(object_field.shape), probe_grad.reshape(probe_modes.shape)


def solution(mesh):
    fine = Mesh(mesh.devices.reshape(2, 8, 2, 4, 2, 2), ROW_AXES + COL_AXES)
    return jax.shard_map(
        body,
        mesh=fine,
        in_specs=(
            P(None, None, ROW_AXES, COL_AXES),
            P(),
            P(),
            P(ROW_AXES, COL_AXES, None, None, None),
            P(ROW_AXES, COL_AXES, None, None),
            P(ROW_AXES, COL_AXES),
        ),
        out_specs=(P(None, None, ROW_AXES, COL_AXES), P()),
        check_vma=False,
    )
```

```python
import functools
import math

import jax
import jax.numpy as jnp
from jax import lax
from jax.experimental import pallas as pl
from jax.experimental.pallas import tpu as pltpu
from jax.sharding import Mesh
from jax.sharding import PartitionSpec as P

F32 = jnp.float32
BF16 = jnp.bfloat16
ROW_AXES = ("xl", "za", "zb")
COL_AXES = ("y", "xh", "core")
NEAR_AXES = ("xl", "zb", "y", "xh")
ALL_NEAR_AXES = ("core",) + NEAR_AXES
FAR_AXES = ("za",)
VMEM_LIMIT = 12 * 1024 * 1024
TILE = 128
HALF = 64
BESIDE = 100_000_000_000
VM = pl.BlockSpec(memory_space=pltpu.VMEM)
SM = pl.BlockSpec(memory_space=pltpu.SMEM)
FAR = pl.BlockSpec(memory_space=pltpu.HBM)


def call(kernel, out_shape, in_specs, *args, scratch=(), out_specs=None, flops=0, moved=0):
    out_shape = tuple(out_shape)
    return pl.pallas_call(
        kernel,
        out_shape=out_shape,
        in_specs=in_specs,
        out_specs=tuple(out_specs or [VM] * len(out_shape)),
        scratch_shapes=list(scratch),
        compiler_params=pltpu.CompilerParams(vmem_limit_bytes=VMEM_LIMIT),
        cost_estimate=pl.CostEstimate(flops=flops, bytes_accessed=moved, transcendentals=0),
    )(*args)


def low_lanes(shape):
    return lax.broadcasted_iota(jnp.int32, shape, len(shape) - 1) < HALF


def split(value):
    high = value.astype(BF16)
    return high, (value - high.astype(F32)).astype(BF16)


def even_column():
    return lax.axis_index("core") == 0


def even_row():
    return lax.axis_index("zb") == 0


def by_parity(even, first, second):
    return jnp.where(even, first, second), jnp.where(even, second, first)


def pack_columns(real, imag):
    low = low_lanes(real.shape)
    turned = pltpu.roll(imag, HALF, 1)
    return jnp.where(low, turned, real), jnp.where(low, real, turned)


def unpack_columns(from_left, from_right):
    low = low_lanes(from_left.shape)
    real = jnp.where(low, from_right, from_left)
    return real, pltpu.roll(jnp.where(low, from_left, from_right), HALF, 1)


def columns_kernel(tile, from_cross, from_mate, tall, cross, mate):
    even = even_row()
    for p in range(4):
        below, above = by_parity(even, from_mate[p], from_cross[p])
        tall[p, :HALF] = above
        tall[p, HALF:HALF + TILE] = tile[p]
        tall[p, HALF + TILE:] = below
    even = even_column()
    for s in range(2):
        to_right, to_left = pack_columns(tall[s], tall[2 + s])
        mate[s], cross[s] = by_parity(even, to_right, to_left)


def operator_kernel(taps, probe, measured, ops, probe_near, measured_near, padded):
    probe_near[...] = probe[...]
    measured_near[...] = measured[...]
    padded[...] = jnp.zeros_like(padded)
    for axis in range(2):
        padded[2 * axis:2 * axis + 2, :31] = taps[axis]

    def band(index):
        line = jnp.broadcast_to(padded[index:index + 1, :], (TILE, 2 * TILE))
        return pltpu.roll(line, 2 * TILE - 15, 1, stride=1, stride_axis=0)[:, :TILE]

    def put(index, blocks):
        for i in range(2):
            for j in range(2):
                high, low = split(blocks[i][j])
                cols = slice(j * TILE, (j + 1) * TILE)
                ops[index, i * TILE:(i + 1) * TILE, cols] = high
                ops[index, (2 + i) * TILE:(3 + i) * TILE, cols] = low

    yr, yi = band(0), band(1)
    put(0, ((yr, -yi), (yi, yr)))
    yr, yi = yr.T, yi.T
    put(2, ((yr, yi), (-yi, yr)))
    xr, xi = band(2), band(3)
    put(3, ((xr, -xi), (xi, xr)))
    xr, xi = xr.T, xi.T
    put(1, ((xr, xi), (-xi, xr)))


def dot(a, b):
    return jnp.dot(a, b, preferred_element_type=F32)


def block(m):
    return slice(m * TILE, (m + 1) * TILE)


def main_kernel(
    offsets, counts, tall, from_cross, from_mate, probe, measured, ops,
    probe_keep, probe_send, object_grad,
    beside, field_high, field_low, mid_high, mid_low, wave_one, wave_two,
):
    even = even_column()
    for s in range(2):
        from_right, from_left = by_parity(even, from_mate[s], from_cross[s])
        beside[s], beside[2 + s] = unpack_columns(from_left, from_right)
    object_ext = (tall, beside)

    def put_field(slot, m, real, imag):
        for c, value in enumerate((real, imag)):
            high, low = split(value)
            field_high[slot, block(c), block(m)] = high
            field_low[slot, block(c), block(m)] = low

    def rows_done(slot, which):
        for n in range(2):
            cols = slice(n * 256, (n + 1) * 256)
            both = dot(ops[which], field_high[slot, :, cols])
            mid = both[:256] + (both[256:] + dot(ops[which, :256], field_low[slot, :, cols]))
            for k in range(2):
                for c in range(2):
                    high, low = split(mid[block(c), block(k)])
                    mid_high[slot, block(2 * n + k), block(c)] = high
                    mid_low[slot, block(2 * n + k), block(c)] = low

    def cols_done(slot, which, take):
        high, low = ops[which, :256], ops[which, 256:]
        for n in range(2):
            rows = slice(n * 256, (n + 1) * 256)
            gh, gl = mid_high[slot, rows], mid_low[slot, rows]
            done = dot(gh, high) + (dot(gl, high) + dot(gh, low))
            for k in range(2):
                take(slot, 2 * n + k, done[block(k), :TILE], done[block(k), TILE:])

    def propagate(which, take):
        for slot in range(2):
            rows_done(slot, which)
        for slot in range(2):
            cols_done(slot, which + 1, take)

    def window(slot, p):
        rows = [object_ext[b][p, pl.ds(offsets[2 * slot], TILE), :] for b in range(2)]
        shift = lax.rem(320 - offsets[2 * slot + 1], 256)
        return pltpu.roll(jnp.concatenate(rows, axis=1), shift, 1)[:, :TILE]

    views = [[window(slot, p) for p in range(4)] for slot in range(2)]
    for slot in range(2):
        o0r, o0i = views[slot][0], views[slot][2]
        for m in range(4):
            pr, pi = probe[m], probe[4 + m]
            put_field(slot, m, pr * o0r - pi * o0i, pr * o0i + pi * o0r)

    def after_first(slot, m, wr, wi):
        o1r, o1i = views[slot][1], views[slot][3]
        wave_one[slot, m, 0] = wr
        wave_one[slot, m, 1] = wi
        put_field(slot, m, wr * o1r - wi * o1i, wr * o1i + wi * o1r)

    propagate(0, after_first)
    intensity = [None, None]

    def after_second(slot, m, wr, wi):
        wave_two[slot, m, 0] = wr
        wave_two[slot, m, 1] = wi
        term = wr * wr + wi * wi
        intensity[slot] = term if m == 0 else intensity[slot] + term
        if m == 3:
            weight = jnp.where(slot < counts[0, 0], 2.0, 0.0).astype(F32)
            residual = (intensity[slot] - measured[slot]) * weight
            for k in range(4):
                put_field(slot, k, residual * wave_two[slot, k, 0], residual * wave_two[slot, k, 1])

    propagate(0, after_second)

    def add(slot, s, m, real, imag):
        for p, value in zip((s, 2 + s), (real, imag)):
            if m == 0:
                object_grad[slot, p] = value
            else:
                object_grad[slot, p] += value

    def after_third(slot, m, hr, hi):
        o1r, o1i = views[slot][1], views[slot][3]
        wr, wi = wave_one[slot, m, 0], wave_one[slot, m, 1]
        add(slot, 1, m, wr * hr + wi * hi, wr * hi - wi * hr)
        put_field(slot, m, hr * o1r + hi * o1i, hi * o1r - hr * o1i)

    propagate(2, after_third)

    def after_fourth(slot, m, hr, hi):
        o0r, o0i = views[slot][0], views[slot][2]
        pr, pi = probe[m], probe[4 + m]
        add(slot, 0, m, pr * hr + pi * hi, pr * hi - pi * hr)
        dr = hr * o0r + hi * o0i
        di = hi * o0r - hr * o0i
        keep, send = by_parity(even, dr, di)
        if slot == 0:
            probe_keep[m] = keep
            probe_send[m] = send
        else:
            probe_keep[m] += keep
            probe_send[m] += send

    propagate(2, after_fourth)


def object_kernel(offsets, object_grad, grad_tall, cross, mate, grad_beside):
    grad_ext = (grad_tall, grad_beside)
    for total in grad_ext:
        total[...] = jnp.zeros_like(total)
    for slot in range(2):
        for p in range(4):
            value = object_grad[slot, p]
            wide = jnp.concatenate([value, jnp.zeros_like(value)], axis=1)
            wide = pltpu.roll(wide, lax.rem(offsets[2 * slot + 1] + 192, 256), 1)
            for b in range(2):
                grad_ext[b][p, pl.ds(offsets[2 * slot], TILE), :] += wide[:, block(b)]
    even = even_column()
    for s in range(2):
        to_left, to_right = pack_columns(grad_beside[s], grad_beside[2 + s])
        mate[s], cross[s] = by_parity(even, to_right, to_left)


def spread_sum(scale, shares, spread_share):
    share = jnp.sum(shares[...], axis=0) * scale
    for i in range(spread_share.shape[0]):
        spread_share[i] = share


def fold_columns_kernel(grad_tall, from_cross, from_mate, part, cross, mate):
    even, even_down = even_column(), even_row()
    for s in range(2):
        from_right, from_left = by_parity(even, from_mate[s], from_cross[s])
        for p, sides in zip((s, 2 + s), unpack_columns(from_right, from_left)):
            total = grad_tall[p] + sides
            part[p] = total[HALF:HALF + TILE]
            mate[p], cross[p] = by_parity(even_down, total[HALF + TILE:], total[:HALF])


def fold_rows_kernel(part, from_cross, from_mate, result):
    even = even_row()
    for p in range(4):
        below, above = by_parity(even, from_mate[p], from_cross[p])
        result[p, :HALF] = part[p, :HALF] + above
        result[p, HALF:] = part[p, HALF:] + below


def finish_kernel(gathered, probe_far, sems):
    moves = []
    for i in range(4):
        part = pl.ds(256 * i, 256)
        moves.append(pltpu.make_async_copy(gathered.at[part], probe_far.at[part], sems.at[i]))
        moves[i].start()
    for move in moves:
        move.wait()


def exchange(cross, mate, axes):
    count = lax.axis_size(axes)
    pairs = [(i, i + 1) for i in range(1, count - 1, 2)]
    from_cross = lax.ppermute(cross, axes, pairs + [(b, a) for a, b in pairs])
    pairs = [(i, i + 1) for i in range(0, count, 2)]
    from_mate = lax.ppermute(mate, axes, pairs + [(b, a) for a, b in pairs])
    return from_cross, from_mate


def swap_cores(value):
    return lax.ppermute(value, "core", [(0, 1), (1, 0)])


def f32(*shape):
    return jax.ShapeDtypeStruct(shape, F32)


def body(object_field, probe_modes, prop_taps, measured, offsets, counts):
    tile = object_field.reshape(4, TILE, TILE)
    planes, strip, half = f32(4, TILE, TILE), f32(2, TILE, TILE), f32(4, HALF, TILE)
    tall, tall_strip = f32(4, 2 * TILE, TILE), f32(2, 2 * TILE, TILE)

    upper = jnp.where(even_row(), 0, HALF)
    cross = lax.dynamic_slice_in_dim(tile, upper, HALF, axis=1)
    mate = lax.dynamic_slice_in_dim(tile, HALF - upper, HALF, axis=1)
    rims = exchange(cross, mate, ROW_AXES)
    object_tall, cross, mate = call(
        columns_kernel, (tall, tall_strip, tall_strip), [VM] * 3, tile, *rims
    )
    strips = exchange(cross, mate, COL_AXES)
    ops, probe, targets = call(
        operator_kernel,
        (jax.ShapeDtypeStruct((4, 512, 256), BF16), f32(8, TILE, TILE), strip), [VM, VM, VM],
        prop_taps, probe_modes.reshape(8, TILE, TILE), measured.reshape(2, TILE, TILE),
        scratch=[pltpu.VMEM((8, 2 * TILE), F32)],
    )
    probe_keep, probe_send, object_grad = call(
        main_kernel,
        (planes, planes, f32(2, 4, TILE, TILE)), [SM, SM] + [VM] * 6,
        offsets.reshape(-1), counts.reshape(1, 1), object_tall, *strips, probe, targets, ops,
        scratch=[
            pltpu.VMEM((4, 256, TILE), F32),
            pltpu.VMEM((2, 256, 512), BF16),
            pltpu.VMEM((2, 256, 512), BF16),
            pltpu.VMEM((2, 512, 256), BF16),
            pltpu.VMEM((2, 512, 256), BF16),
            pltpu.VMEM((2, 4, 2, TILE, TILE), F32),
            pltpu.VMEM((2, 4, 2, TILE, TILE), F32),
        ],
        flops=3_200_000_000, moved=4_000_000,
    )
    grad_tall, cross, mate = call(
        object_kernel, (tall, tall_strip, tall_strip), [SM, VM],
        offsets.reshape(-1), object_grad,
        scratch=[pltpu.VMEM((4, 256, TILE), F32)],
    )

    near = lax.axis_size(NEAR_AXES)
    far = lax.axis_size(FAR_AXES)
    rows = 4 * TILE // near
    half_sum = probe_keep + swap_cores(probe_send)
    shares = lax.all_to_all(half_sum.reshape(near, rows, TILE), NEAR_AXES, 0, 0, tiled=True)
    spread_share = jnp.broadcast_to(jnp.sum(shares, axis=0)[None], (far, rows, TILE))
    strips = exchange(cross, mate, COL_AXES)
    shares = lax.all_to_all(spread_share, FAR_AXES, 0, 0, tiled=True)
    part, cross, mate = call(
        fold_columns_kernel, (planes, half, half), [VM] * 3, grad_tall, *strips
    )
    rims = exchange(cross, mate, ROW_AXES)
    (spread_share,) = call(
        functools.partial(spread_sum, 1.0 / math.sqrt(2 * near * far)), (f32(2 * near, rows, TILE),), [VM], shares
    )
    gathered = lax.all_to_all(spread_share, ALL_NEAR_AXES, 0, 0, tiled=True)
    (result,) = call(
        fold_rows_kernel, (planes,), [VM] * 3, part, *rims, flops=BESIDE, moved=1
    )
    (probe_grad,) = call(
        finish_kernel, (f32(8 * TILE, TILE),), [VM], gathered.reshape(8 * TILE, TILE),
        scratch=[pltpu.SemaphoreType.DMA((4,))], out_specs=[FAR],
    )
    return result.reshape(object_field.shape), probe_grad.reshape(probe_modes.shape)


def solution(mesh):
    fine = Mesh(mesh.devices.reshape(2, 8, 2, 4, 2, 2), ROW_AXES + COL_AXES)
    return jax.shard_map(
        body,
        mesh=fine,
        in_specs=(
            P(None, None, ROW_AXES, COL_AXES),
            P(),
            P(),
            P(ROW_AXES, COL_AXES, None, None, None),
            P(ROW_AXES, COL_AXES, None, None),
            P(ROW_AXES, COL_AXES),
        ),
        out_specs=(P(None, None, ROW_AXES, COL_AXES), P()),
        check_vma=False,
    )
```

```python
import functools
import math

import jax
import jax.numpy as jnp
from jax import lax
from jax.experimental import pallas as pl
from jax.experimental.pallas import tpu as pltpu
from jax.sharding import Mesh
from jax.sharding import PartitionSpec as P

F32 = jnp.float32
BF16 = jnp.bfloat16
ROW_AXES = ("xl", "za", "zb")
COL_AXES = ("y", "xh", "core")
NEAR_AXES = ("xl", "zb", "y", "xh", "core")
FAR_AXES = ("za",)
VMEM_LIMIT = 12 * 1024 * 1024
TILE = 128
HALF = 64
BESIDE = 100_000_000_000
VM = pl.BlockSpec(memory_space=pltpu.VMEM)
SM = pl.BlockSpec(memory_space=pltpu.SMEM)
FAR = pl.BlockSpec(memory_space=pltpu.HBM)


def call(kernel, out_shape, in_specs, *args, scratch=(), out_specs=None, flops=0, moved=0):
    out_shape = tuple(out_shape)
    return pl.pallas_call(
        kernel,
        out_shape=out_shape,
        in_specs=in_specs,
        out_specs=tuple(out_specs or [VM] * len(out_shape)),
        scratch_shapes=list(scratch),
        compiler_params=pltpu.CompilerParams(vmem_limit_bytes=VMEM_LIMIT),
        cost_estimate=pl.CostEstimate(flops=flops, bytes_accessed=moved, transcendentals=0),
    )(*args)


def low_lanes(shape):
    return lax.broadcasted_iota(jnp.int32, shape, len(shape) - 1) < HALF


def split(value):
    high = value.astype(BF16)
    return high, (value - high.astype(F32)).astype(BF16)


def even_column():
    return lax.axis_index("core") == 0


def even_row():
    return lax.axis_index("zb") == 0


def by_parity(even, first, second):
    return jnp.where(even, first, second), jnp.where(even, second, first)


def pack_columns(real, imag):
    low = low_lanes(real.shape)
    turned = pltpu.roll(imag, HALF, 1)
    return jnp.where(low, turned, real), jnp.where(low, real, turned)


def unpack_columns(from_left, from_right):
    low = low_lanes(from_left.shape)
    real = jnp.where(low, from_right, from_left)
    return real, pltpu.roll(jnp.where(low, from_left, from_right), HALF, 1)


def rows_kernel(tile, cross, mate, columns):
    even = even_row()
    for p in range(4):
        mate[p], cross[p] = by_parity(even, tile[p, HALF:], tile[p, :HALF])
    even = even_column()
    for s in range(2):
        to_right, to_left = pack_columns(tile[s], tile[2 + s])
        columns[s] = jnp.where(even, to_left, to_right)


def columns_kernel(tile, from_cross, from_mate, columns, tall, cross, mate, columns_near):
    columns_near[...] = columns[...]
    even = even_row()
    for p in range(4):
        below, above = by_parity(even, from_mate[p], from_cross[p])
        tall[p, :HALF] = above
        tall[p, HALF:HALF + TILE] = tile[p]
        tall[p, HALF + TILE:] = below
    even = even_column()
    for s in range(2):
        to_right, to_left = pack_columns(tall[s], tall[2 + s])
        to_mate, to_cross = by_parity(even, to_right, to_left)
        mate[s] = to_mate
        cross[s, :HALF] = to_cross[:HALF]
        cross[s, HALF:] = to_cross[HALF + TILE:]


def operator_kernel(taps, probe, measured, ops, probe_near, measured_near, padded):
    probe_near[...] = probe[...]
    measured_near[...] = measured[...]
    padded[...] = jnp.zeros_like(padded)
    for axis in range(2):
        padded[2 * axis:2 * axis + 2, :31] = taps[axis]

    def band(index):
        line = jnp.broadcast_to(padded[index:index + 1, :], (TILE, 2 * TILE))
        return pltpu.roll(line, 2 * TILE - 15, 1, stride=1, stride_axis=0)[:, :TILE]

    def put(index, blocks):
        for i in range(2):
            for j in range(2):
                high, low = split(blocks[i][j])
                cols = slice(j * TILE, (j + 1) * TILE)
                ops[index, i * TILE:(i + 1) * TILE, cols] = high
                ops[index, (2 + i) * TILE:(3 + i) * TILE, cols] = low

    yr, yi = band(0), band(1)
    put(0, ((yr, -yi), (yi, yr)))
    yr, yi = yr.T, yi.T
    put(2, ((yr, yi), (-yi, yr)))
    xr, xi = band(2), band(3)
    put(3, ((xr, -xi), (xi, xr)))
    xr, xi = xr.T, xi.T
    put(1, ((xr, xi), (-xi, xr)))


def dot(a, b):
    return jnp.dot(a, b, preferred_element_type=F32)


def block(m):
    return slice(m * TILE, (m + 1) * TILE)


def main_kernel(
    offsets, counts, tall, columns, corners, from_mate, probe, measured, ops,
    probe_far, object_grad,
    probe_grad, sems, beside, field_high, field_low, mid_high, mid_low, wave_one, wave_two,
):
    even = even_column()
    for s in range(2):
        from_cross = jnp.concatenate([corners[s, :HALF], columns[s], corners[s, HALF:]], axis=0)
        from_right, from_left = by_parity(even, from_mate[s], from_cross)
        beside[s], beside[2 + s] = unpack_columns(from_left, from_right)
    object_ext = (tall, beside)

    def put_field(slot, m, real, imag):
        for c, value in enumerate((real, imag)):
            high, low = split(value)
            field_high[slot, block(c), block(m)] = high
            field_low[slot, block(c), block(m)] = low

    def rows_done(slot, which):
        for n in range(2):
            cols = slice(n * 256, (n + 1) * 256)
            both = dot(ops[which], field_high[slot, :, cols])
            mid = both[:256] + (both[256:] + dot(ops[which, :256], field_low[slot, :, cols]))
            for k in range(2):
                for c in range(2):
                    high, low = split(mid[block(c), block(k)])
                    mid_high[slot, block(2 * n + k), block(c)] = high
                    mid_low[slot, block(2 * n + k), block(c)] = low

    def cols_done(slot, which, take):
        high, low = ops[which, :256], ops[which, 256:]
        for n in range(2):
            rows = slice(n * 256, (n + 1) * 256)
            gh, gl = mid_high[slot, rows], mid_low[slot, rows]
            done = dot(gh, high) + (dot(gl, high) + dot(gh, low))
            for k in range(2):
                take(slot, 2 * n + k, done[block(k), :TILE], done[block(k), TILE:])

    def propagate(which, take):
        for slot in range(2):
            rows_done(slot, which)
        for slot in range(2):
            cols_done(slot, which + 1, take)

    def window(slot, p):
        rows = [object_ext[b][p, pl.ds(offsets[2 * slot], TILE), :] for b in range(2)]
        shift = lax.rem(320 - offsets[2 * slot + 1], 256)
        return pltpu.roll(jnp.concatenate(rows, axis=1), shift, 1)[:, :TILE]

    views = [[window(slot, p) for p in range(4)] for slot in range(2)]
    for slot in range(2):
        o0r, o0i = views[slot][0], views[slot][2]
        for m in range(4):
            pr, pi = probe[m], probe[4 + m]
            put_field(slot, m, pr * o0r - pi * o0i, pr * o0i + pi * o0r)

    def after_first(slot, m, wr, wi):
        o1r, o1i = views[slot][1], views[slot][3]
        wave_one[slot, m, 0] = wr
        wave_one[slot, m, 1] = wi
        put_field(slot, m, wr * o1r - wi * o1i, wr * o1i + wi * o1r)

    propagate(0, after_first)
    intensity = [None, None]

    def after_second(slot, m, wr, wi):
        wave_two[slot, m, 0] = wr
        wave_two[slot, m, 1] = wi
        term = wr * wr + wi * wi
        intensity[slot] = term if m == 0 else intensity[slot] + term
        if m == 3:
            weight = jnp.where(slot < counts[0, 0], 2.0, 0.0).astype(F32)
            residual = (intensity[slot] - measured[slot]) * weight
            for k in range(4):
                put_field(slot, k, residual * wave_two[slot, k, 0], residual * wave_two[slot, k, 1])

    propagate(0, after_second)

    def add(slot, s, m, real, imag):
        for p, value in zip((s, 2 + s), (real, imag)):
            if m == 0:
                object_grad[slot, p] = value
            else:
                object_grad[slot, p] += value

    def after_third(slot, m, hr, hi):
        o1r, o1i = views[slot][1], views[slot][3]
        wr, wi = wave_one[slot, m, 0], wave_one[slot, m, 1]
        add(slot, 1, m, wr * hr + wi * hi, wr * hi - wi * hr)
        put_field(slot, m, hr * o1r + hi * o1i, hi * o1r - hr * o1i)

    propagate(2, after_third)

    def after_fourth(slot, m, hr, hi):
        o0r, o0i = views[slot][0], views[slot][2]
        pr, pi = probe[m], probe[4 + m]
        add(slot, 0, m, pr * hr + pi * hi, pr * hi - pi * hr)
        dr = hr * o0r + hi * o0i
        di = hi * o0r - hr * o0i
        if slot == 0:
            probe_grad[m] = dr
            probe_grad[4 + m] = di
        else:
            probe_grad[m] += dr
            probe_grad[4 + m] += di
            for part in (m, 4 + m):
                moves.append(pltpu.make_async_copy(probe_grad.at[part], probe_far.at[part], sems.at[part]))
                moves[-1].start()

    moves = []
    propagate(2, after_fourth)
    for move in moves:
        move.wait()


def object_kernel(offsets, object_grad, grad_tall, cross, mate, grad_beside):
    grad_ext = (grad_tall, grad_beside)
    for total in grad_ext:
        total[...] = jnp.zeros_like(total)
    for slot in range(2):
        for p in range(4):
            value = object_grad[slot, p]
            wide = jnp.concatenate([value, jnp.zeros_like(value)], axis=1)
            wide = pltpu.roll(wide, lax.rem(offsets[2 * slot + 1] + 192, 256), 1)
            for b in range(2):
                grad_ext[b][p, pl.ds(offsets[2 * slot], TILE), :] += wide[:, block(b)]
    even = even_column()
    for s in range(2):
        to_left, to_right = pack_columns(grad_beside[s], grad_beside[2 + s])
        mate[s], cross[s] = by_parity(even, to_right, to_left)


def spread_sum(scale, shares, spread_share):
    share = jnp.sum(shares[...], axis=0) * scale
    for i in range(spread_share.shape[0]):
        spread_share[i] = share


def fold_columns_kernel(grad_tall, from_cross, from_mate, part, cross, mate):
    even, even_down = even_column(), even_row()
    for s in range(2):
        from_right, from_left = by_parity(even, from_mate[s], from_cross[s])
        for p, sides in zip((s, 2 + s), unpack_columns(from_right, from_left)):
            total = grad_tall[p] + sides
            part[p] = total[HALF:HALF + TILE]
            mate[p], cross[p] = by_parity(even_down, total[HALF + TILE:], total[:HALF])


def fold_rows_kernel(part, from_cross, from_mate, result):
    even = even_row()
    for p in range(4):
        below, above = by_parity(even, from_mate[p], from_cross[p])
        result[p, :HALF] = part[p, :HALF] + above
        result[p, HALF:] = part[p, HALF:] + below


def finish_kernel(gathered, probe_far, sems):
    moves = []
    for i in range(4):
        part = pl.ds(256 * i, 256)
        moves.append(pltpu.make_async_copy(gathered.at[part], probe_far.at[part], sems.at[i]))
        moves[i].start()
    for move in moves:
        move.wait()


def to_cross(value, axes):
    pairs = [(i, i + 1) for i in range(1, lax.axis_size(axes) - 1, 2)]
    return lax.ppermute(value, axes, pairs + [(b, a) for a, b in pairs])


def to_mate(value, axes):
    pairs = [(i, i + 1) for i in range(0, lax.axis_size(axes), 2)]
    return lax.ppermute(value, axes, pairs + [(b, a) for a, b in pairs])


def exchange(cross, mate, axes):
    return to_cross(cross, axes), to_mate(mate, axes)


def f32(*shape):
    return jax.ShapeDtypeStruct(shape, F32)


def body(object_field, probe_modes, prop_taps, measured, offsets, counts):
    tile = object_field.reshape(4, TILE, TILE)
    planes, strip, half = f32(4, TILE, TILE), f32(2, TILE, TILE), f32(4, HALF, TILE)
    tall, tall_strip = f32(4, 2 * TILE, TILE), f32(2, 2 * TILE, TILE)

    cross, mate, columns = call(rows_kernel, (half, half, strip), [VM], tile)
    rims = exchange(cross, mate, ROW_AXES)
    columns = to_cross(columns, COL_AXES)
    object_tall, cross, mate, columns = call(
        columns_kernel, (tall, strip, tall_strip, strip), [VM] * 4, tile, *rims, columns
    )
    strips = exchange(cross, mate, COL_AXES)
    ops, probe, targets = call(
        operator_kernel,
        (jax.ShapeDtypeStruct((4, 512, 256), BF16), f32(8, TILE, TILE), strip), [VM, VM, VM],
        prop_taps, probe_modes.reshape(8, TILE, TILE), measured.reshape(2, TILE, TILE),
        scratch=[pltpu.VMEM((8, 2 * TILE), F32)],
    )
    probe_part, object_grad = call(
        main_kernel,
        (f32(8, TILE, TILE), f32(2, 4, TILE, TILE)), [SM, SM] + [VM] * 7,
        offsets.reshape(-1), counts.reshape(1, 1), object_tall, columns, *strips, probe, targets, ops,
        out_specs=[FAR, VM],
        scratch=[
            pltpu.VMEM((8, TILE, TILE), F32),
            pltpu.SemaphoreType.DMA((8,)),
            pltpu.VMEM((4, 256, TILE), F32),
            pltpu.VMEM((2, 256, 512), BF16),
            pltpu.VMEM((2, 256, 512), BF16),
            pltpu.VMEM((2, 512, 256), BF16),
            pltpu.VMEM((2, 512, 256), BF16),
            pltpu.VMEM((2, 4, 2, TILE, TILE), F32),
            pltpu.VMEM((2, 4, 2, TILE, TILE), F32),
        ],
        flops=3_200_000_000, moved=4_000_000,
    )
    grad_tall, cross, mate = call(
        object_kernel, (tall, tall_strip, tall_strip), [SM, VM],
        offsets.reshape(-1), object_grad,
        scratch=[pltpu.VMEM((4, 256, TILE), F32)],
    )

    near = lax.axis_size(NEAR_AXES)
    far = lax.axis_size(FAR_AXES)
    rows = 8 * TILE // near
    shares = lax.all_to_all(probe_part.reshape(near, rows, TILE), NEAR_AXES, 0, 0, tiled=True)
    spread_share = jnp.broadcast_to(jnp.sum(shares, axis=0)[None], (far, rows, TILE))
    strips = exchange(cross, mate, COL_AXES)
    shares = lax.all_to_all(spread_share, FAR_AXES, 0, 0, tiled=True)
    part, cross, mate = call(
        fold_columns_kernel, (planes, half, half), [VM] * 3, grad_tall, *strips
    )
    rims = exchange(cross, mate, ROW_AXES)
    (spread_share,) = call(
        functools.partial(spread_sum, 1.0 / math.sqrt(near * far)), (f32(near, rows, TILE),), [VM], shares
    )
    gathered = lax.all_to_all(spread_share, NEAR_AXES, 0, 0, tiled=True)
    (result,) = call(
        fold_rows_kernel, (planes,), [VM] * 3, part, *rims, flops=BESIDE, moved=1
    )
    (probe_grad,) = call(
        finish_kernel, (f32(8 * TILE, TILE),), [VM], gathered.reshape(8 * TILE, TILE),
        scratch=[pltpu.SemaphoreType.DMA((4,))], out_specs=[FAR],
    )
    return result.reshape(object_field.shape), probe_grad.reshape(probe_modes.shape)


def solution(mesh):
    fine = Mesh(mesh.devices.reshape(2, 8, 2, 4, 2, 2), ROW_AXES + COL_AXES)
    return jax.shard_map(
        body,
        mesh=fine,
        in_specs=(
            P(None, None, ROW_AXES, COL_AXES),
            P(),
            P(),
            P(ROW_AXES, COL_AXES, None, None, None),
            P(ROW_AXES, COL_AXES, None, None),
            P(ROW_AXES, COL_AXES),
        ),
        out_specs=(P(None, None, ROW_AXES, COL_AXES), P()),
        check_vma=False,
    )
```

```python
import functools
import math

import jax
import jax.numpy as jnp
from jax import lax
from jax.experimental import pallas as pl
from jax.experimental.pallas import tpu as pltpu
from jax.sharding import Mesh
from jax.sharding import PartitionSpec as P

F32 = jnp.float32
BF16 = jnp.bfloat16
ROW_AXES = ("xl", "za", "zb")
COL_AXES = ("y", "xh", "core")
NEAR_AXES = ("xl", "zb", "y", "xh", "core")
FAR_AXES = ("za",)
VMEM_LIMIT = 12 * 1024 * 1024
TILE = 128
HALF = 64
BESIDE = 100_000_000_000
VM = pl.BlockSpec(memory_space=pltpu.VMEM)
SM = pl.BlockSpec(memory_space=pltpu.SMEM)
FAR = pl.BlockSpec(memory_space=pltpu.HBM)


def call(kernel, out_shape, in_specs, *args, scratch=(), out_specs=None, flops=0, moved=0):
    out_shape = tuple(out_shape)
    return pl.pallas_call(
        kernel,
        out_shape=out_shape,
        in_specs=in_specs,
        out_specs=tuple(out_specs or [VM] * len(out_shape)),
        scratch_shapes=list(scratch),
        compiler_params=pltpu.CompilerParams(vmem_limit_bytes=VMEM_LIMIT),
        cost_estimate=pl.CostEstimate(flops=flops, bytes_accessed=moved, transcendentals=0),
    )(*args)


def low_lanes(shape):
    return lax.broadcasted_iota(jnp.int32, shape, len(shape) - 1) < HALF


def split(value):
    high = value.astype(BF16)
    return high, (value - high.astype(F32)).astype(BF16)


def even_column():
    return lax.axis_index("core") == 0


def above_first():
    return lax.axis_index("zb") == lax.axis_index("core")


def by_parity(even, first, second):
    return jnp.where(even, first, second), jnp.where(even, second, first)


def pack_columns(real, imag):
    low = low_lanes(real.shape)
    turned = pltpu.roll(imag, HALF, 1)
    return jnp.where(low, turned, real), jnp.where(low, real, turned)


def unpack_columns(from_left, from_right):
    low = low_lanes(from_left.shape)
    real = jnp.where(low, from_right, from_left)
    return real, pltpu.roll(jnp.where(low, from_left, from_right), HALF, 1)


def columns_kernel(tile, from_cross, from_mate, tall, cross, mate):
    first = above_first()
    for p in range(4):
        below, above = by_parity(first, from_mate[p], from_cross[p])
        tall[p, :HALF] = above
        tall[p, HALF:HALF + TILE] = tile[p]
        tall[p, HALF + TILE:] = below
    even = even_column()
    for s in range(2):
        to_right, to_left = pack_columns(tall[s], tall[2 + s])
        mate[s], cross[s] = by_parity(even, to_right, to_left)


def operator_kernel(taps, probe, measured, ops, probe_near, measured_near, padded):
    probe_near[...] = probe[...]
    measured_near[...] = measured[...]
    padded[...] = jnp.zeros_like(padded)
    for axis in range(2):
        padded[2 * axis:2 * axis + 2, :31] = taps[axis]

    def band(index):
        line = jnp.broadcast_to(padded[index:index + 1, :], (TILE, 2 * TILE))
        return pltpu.roll(line, 2 * TILE - 15, 1, stride=1, stride_axis=0)[:, :TILE]

    def put(index, blocks):
        for i in range(2):
            for j in range(2):
                high, low = split(blocks[i][j])
                cols = slice(j * TILE, (j + 1) * TILE)
                ops[index, i * TILE:(i + 1) * TILE, cols] = high
                ops[index, (2 + i) * TILE:(3 + i) * TILE, cols] = low

    yr, yi = band(0), band(1)
    put(0, ((yr, -yi), (yi, yr)))
    yr, yi = yr.T, yi.T
    put(2, ((yr, yi), (-yi, yr)))
    xr, xi = band(2), band(3)
    put(3, ((xr, -xi), (xi, xr)))
    xr, xi = xr.T, xi.T
    put(1, ((xr, xi), (-xi, xr)))


def dot(a, b):
    return jnp.dot(a, b, preferred_element_type=F32)


def block(m):
    return slice(m * TILE, (m + 1) * TILE)


def main_kernel(
    offsets, counts, tall, from_cross, from_mate, probe, measured, ops,
    probe_grad, object_grad,
    beside, field_high, field_low, mid_high, mid_low, wave_one, wave_two,
):
    even = even_column()
    for s in range(2):
        from_right, from_left = by_parity(even, from_mate[s], from_cross[s])
        beside[s], beside[2 + s] = unpack_columns(from_left, from_right)
    object_ext = (tall, beside)

    def put_field(slot, m, real, imag):
        for c, value in enumerate((real, imag)):
            high, low = split(value)
            field_high[slot, block(c), block(m)] = high
            field_low[slot, block(c), block(m)] = low

    def rows_done(slot, which):
        for n in range(2):
            cols = slice(n * 256, (n + 1) * 256)
            both = dot(ops[which], field_high[slot, :, cols])
            mid = both[:256] + (both[256:] + dot(ops[which, :256], field_low[slot, :, cols]))
            for k in range(2):
                for c in range(2):
                    high, low = split(mid[block(c), block(k)])
                    mid_high[slot, block(2 * n + k), block(c)] = high
                    mid_low[slot, block(2 * n + k), block(c)] = low

    def cols_done(slot, which, take):
        high, low = ops[which, :256], ops[which, 256:]
        for n in range(2):
            rows = slice(n * 256, (n + 1) * 256)
            gh, gl = mid_high[slot, rows], mid_low[slot, rows]
            done = dot(gh, high) + (dot(gl, high) + dot(gh, low))
            for k in range(2):
                take(slot, 2 * n + k, done[block(k), :TILE], done[block(k), TILE:])

    def propagate(which, take):
        for slot in range(2):
            rows_done(slot, which)
        for slot in range(2):
            cols_done(slot, which + 1, take)

    def window(slot, p):
        rows = [object_ext[b][p, pl.ds(offsets[2 * slot], TILE), :] for b in range(2)]
        shift = lax.rem(320 - offsets[2 * slot + 1], 256)
        return pltpu.roll(jnp.concatenate(rows, axis=1), shift, 1)[:, :TILE]

    views = [[window(slot, p) for p in range(4)] for slot in range(2)]
    for slot in range(2):
        o0r, o0i = views[slot][0], views[slot][2]
        for m in range(4):
            pr, pi = probe[m], probe[4 + m]
            put_field(slot, m, pr * o0r - pi * o0i, pr * o0i + pi * o0r)

    def after_first(slot, m, wr, wi):
        o1r, o1i = views[slot][1], views[slot][3]
        wave_one[slot, m, 0] = wr
        wave_one[slot, m, 1] = wi
        put_field(slot, m, wr * o1r - wi * o1i, wr * o1i + wi * o1r)

    propagate(0, after_first)
    intensity = [None, None]

    def after_second(slot, m, wr, wi):
        wave_two[slot, m, 0] = wr
        wave_two[slot, m, 1] = wi
        term = wr * wr + wi * wi
        intensity[slot] = term if m == 0 else intensity[slot] + term
        if m == 3:
            weight = jnp.where(slot < counts[0, 0], 2.0, 0.0).astype(F32)
            residual = (intensity[slot] - measured[slot]) * weight
            for k in range(4):
                put_field(slot, k, residual * wave_two[slot, k, 0], residual * wave_two[slot, k, 1])

    propagate(0, after_second)

    def add(slot, s, m, real, imag):
        for p, value in zip((s, 2 + s), (real, imag)):
            if m == 0:
                object_grad[slot, p] = value
            else:
                object_grad[slot, p] += value

    def after_third(slot, m, hr, hi):
        o1r, o1i = views[slot][1], views[slot][3]
        wr, wi = wave_one[slot, m, 0], wave_one[slot, m, 1]
        add(slot, 1, m, wr * hr + wi * hi, wr * hi - wi * hr)
        put_field(slot, m, hr * o1r + hi * o1i, hi * o1r - hr * o1i)

    propagate(2, after_third)

    def after_fourth(slot, m, hr, hi):
        o0r, o0i = views[slot][0], views[slot][2]
        pr, pi = probe[m], probe[4 + m]
        add(slot, 0, m, pr * hr + pi * hi, pr * hi - pi * hr)
        dr = hr * o0r + hi * o0i
        di = hi * o0r - hr * o0i
        if slot == 0:
            probe_grad[m] = dr
            probe_grad[4 + m] = di
        else:
            probe_grad[m] += dr
            probe_grad[4 + m] += di

    propagate(2, after_fourth)


def object_kernel(offsets, object_grad, grad_tall, cross, mate, grad_beside):
    grad_ext = (grad_tall, grad_beside)
    for total in grad_ext:
        total[...] = jnp.zeros_like(total)
    for slot in range(2):
        for p in range(4):
            value = object_grad[slot, p]
            wide = jnp.concatenate([value, jnp.zeros_like(value)], axis=1)
            wide = pltpu.roll(wide, lax.rem(offsets[2 * slot + 1] + 192, 256), 1)
            for b in range(2):
                grad_ext[b][p, pl.ds(offsets[2 * slot], TILE), :] += wide[:, block(b)]
    even = even_column()
    for s in range(2):
        to_left, to_right = pack_columns(grad_beside[s], grad_beside[2 + s])
        mate[s], cross[s] = by_parity(even, to_right, to_left)


def spread_sum(scale, shares, spread_share):
    share = jnp.sum(shares[...], axis=0) * scale
    for i in range(spread_share.shape[0]):
        spread_share[i] = share


def fold_columns_kernel(grad_tall, from_cross, from_mate, part, cross, mate):
    even, first = even_column(), above_first()
    for s in range(2):
        from_right, from_left = by_parity(even, from_mate[s], from_cross[s])
        for p, sides in zip((s, 2 + s), unpack_columns(from_right, from_left)):
            total = grad_tall[p] + sides
            part[p] = total[HALF:HALF + TILE]
            mate[p], cross[p] = by_parity(first, total[HALF + TILE:], total[:HALF])


def fold_rows_kernel(part, from_cross, from_mate, result):
    first = above_first()
    for p in range(4):
        below, above = by_parity(first, from_mate[p], from_cross[p])
        result[p, :HALF] = part[p, :HALF] + above
        result[p, HALF:] = part[p, HALF:] + below


def finish_kernel(gathered, probe_far, sems):
    moves = []
    for i in range(4):
        part = pl.ds(256 * i, 256)
        moves.append(pltpu.make_async_copy(gathered.at[part], probe_far.at[part], sems.at[i]))
        moves[i].start()
    for move in moves:
        move.wait()


def neighbours(count, start):
    pairs = [(i, i + 1) for i in range(start, count - 1, 2)]
    return pairs + [(b, a) for a, b in pairs]


def exchange_columns(cross, mate):
    count = lax.axis_size(COL_AXES)
    from_cross = lax.ppermute(cross, COL_AXES, neighbours(count, 1))
    return from_cross, lax.ppermute(mate, COL_AXES, neighbours(count, 0))


def exchange_rows(first, second):
    count = lax.axis_size(ROW_AXES)
    axes = ROW_AXES + ("core",)
    received = []
    for value, starts in ((first, (1, 0)), (second, (0, 1))):
        pairs = [(2 * a + c, 2 * b + c) for c in range(2) for a, b in neighbours(count, starts[c])]
        received.append(lax.ppermute(value, axes, pairs))
    return received


def f32(*shape):
    return jax.ShapeDtypeStruct(shape, F32)


def body(object_field, probe_modes, prop_taps, measured, offsets, counts):
    tile = object_field.reshape(4, TILE, TILE)
    planes, strip, half = f32(4, TILE, TILE), f32(2, TILE, TILE), f32(4, HALF, TILE)
    tall, tall_strip = f32(4, 2 * TILE, TILE), f32(2, 2 * TILE, TILE)

    upper = jnp.where(above_first(), 0, HALF)
    cross = lax.dynamic_slice_in_dim(tile, upper, HALF, axis=1)
    mate = lax.dynamic_slice_in_dim(tile, HALF - upper, HALF, axis=1)
    rims = exchange_rows(cross, mate)
    object_tall, cross, mate = call(
        columns_kernel, (tall, tall_strip, tall_strip), [VM] * 3, tile, *rims
    )
    strips = exchange_columns(cross, mate)
    ops, probe, targets = call(
        operator_kernel,
        (jax.ShapeDtypeStruct((4, 512, 256), BF16), f32(8, TILE, TILE), strip), [VM, VM, VM],
        prop_taps, probe_modes.reshape(8, TILE, TILE), measured.reshape(2, TILE, TILE),
        scratch=[pltpu.VMEM((8, 2 * TILE), F32)],
    )
    probe_part, object_grad = call(
        main_kernel,
        (f32(8, TILE, TILE), f32(2, 4, TILE, TILE)), [SM, SM] + [VM] * 6,
        offsets.reshape(-1), counts.reshape(1, 1), object_tall, *strips, probe, targets, ops,
        scratch=[
            pltpu.VMEM((4, 256, TILE), F32),
            pltpu.VMEM((2, 256, 512), BF16),
            pltpu.VMEM((2, 256, 512), BF16),
            pltpu.VMEM((2, 512, 256), BF16),
            pltpu.VMEM((2, 512, 256), BF16),
            pltpu.VMEM((2, 4, 2, TILE, TILE), F32),
            pltpu.VMEM((2, 4, 2, TILE, TILE), F32),
        ],
        flops=3_200_000_000, moved=4_000_000,
    )
    grad_tall, cross, mate = call(
        object_kernel, (tall, tall_strip, tall_strip), [SM, VM],
        offsets.reshape(-1), object_grad,
        scratch=[pltpu.VMEM((4, 256, TILE), F32)],
    )

    near = lax.axis_size(NEAR_AXES)
    far = lax.axis_size(FAR_AXES)
    rows = 8 * TILE // near
    shares = lax.all_to_all(probe_part.reshape(near, rows, TILE), NEAR_AXES, 0, 0, tiled=True)
    spread_share = jnp.broadcast_to(jnp.sum(shares, axis=0)[None], (far, rows, TILE))
    strips = exchange_columns(cross, mate)
    shares = lax.all_to_all(spread_share, FAR_AXES, 0, 0, tiled=True)
    part, cross, mate = call(
        fold_columns_kernel, (planes, half, half), [VM] * 3, grad_tall, *strips
    )
    rims = exchange_rows(cross, mate)
    (spread_share,) = call(
        functools.partial(spread_sum, 1.0 / math.sqrt(near * far)), (f32(near, rows, TILE),), [VM], shares
    )
    gathered = lax.all_to_all(spread_share, NEAR_AXES, 0, 0, tiled=True)
    (result,) = call(
        fold_rows_kernel, (planes,), [VM] * 3, part, *rims, flops=BESIDE, moved=1
    )
    (probe_grad,) = call(
        finish_kernel, (f32(8 * TILE, TILE),), [VM], gathered.reshape(8 * TILE, TILE),
        scratch=[pltpu.SemaphoreType.DMA((4,))], out_specs=[FAR],
    )
    return result.reshape(object_field.shape), probe_grad.reshape(probe_modes.shape)


def solution(mesh):
    fine = Mesh(mesh.devices.reshape(2, 8, 2, 4, 2, 2), ROW_AXES + COL_AXES)
    return jax.shard_map(
        body,
        mesh=fine,
        in_specs=(
            P(None, None, ROW_AXES, COL_AXES),
            P(),
            P(),
            P(ROW_AXES, COL_AXES, None, None, None),
            P(ROW_AXES, COL_AXES, None, None),
            P(ROW_AXES, COL_AXES),
        ),
        out_specs=(P(None, None, ROW_AXES, COL_AXES), P()),
        check_vma=False,
    )
```

```python
import functools
import math

import jax
import jax.numpy as jnp
from jax import lax
from jax.experimental import pallas as pl
from jax.experimental.pallas import tpu as pltpu
from jax.sharding import Mesh
from jax.sharding import PartitionSpec as P

F32 = jnp.float32
BF16 = jnp.bfloat16
ROW_AXES = ("xl", "za", "zb")
COL_AXES = ("y", "xh", "core")
NEAR_AXES = ("xl", "zb", "y", "xh", "core")
FAR_AXES = ("za",)
VMEM_LIMIT = 12 * 1024 * 1024
TILE = 128
HALF = 64
BESIDE = 100_000_000_000
VM = pl.BlockSpec(memory_space=pltpu.VMEM)
SM = pl.BlockSpec(memory_space=pltpu.SMEM)
FAR = pl.BlockSpec(memory_space=pltpu.HBM)


def call(kernel, out_shape, in_specs, *args, scratch=(), out_specs=None, flops=0, moved=0):
    out_shape = tuple(out_shape)
    return pl.pallas_call(
        kernel,
        out_shape=out_shape,
        in_specs=in_specs,
        out_specs=tuple(out_specs or [VM] * len(out_shape)),
        scratch_shapes=list(scratch),
        compiler_params=pltpu.CompilerParams(vmem_limit_bytes=VMEM_LIMIT),
        cost_estimate=pl.CostEstimate(flops=flops, bytes_accessed=moved, transcendentals=0),
    )(*args)


def low_lanes(shape):
    return lax.broadcasted_iota(jnp.int32, shape, len(shape) - 1) < HALF


def split(value):
    high = value.astype(BF16)
    return high, (value - high.astype(F32)).astype(BF16)


def even_column():
    return lax.axis_index("core") == 0


def above_first():
    return lax.axis_index("zb") == lax.axis_index("core")


def by_parity(even, first, second):
    return jnp.where(even, first, second), jnp.where(even, second, first)


def pack_columns(real, imag):
    low = low_lanes(real.shape)
    turned = pltpu.roll(imag, HALF, 1)
    return jnp.where(low, turned, real), jnp.where(low, real, turned)


def unpack_columns(from_left, from_right):
    low = low_lanes(from_left.shape)
    real = jnp.where(low, from_right, from_left)
    return real, pltpu.roll(jnp.where(low, from_left, from_right), HALF, 1)


def tall_kernel(tile, from_cross, from_mate, tall):
    first = above_first()
    for p in range(4):
        below, above = by_parity(first, from_mate[p], from_cross[p])
        tall[p, :HALF] = above
        tall[p, HALF:HALF + TILE] = tile[p]
        tall[p, HALF + TILE:] = below


def columns_kernel(tile, from_cross, from_mate, cross, mate):
    first, even = above_first(), even_column()
    for s in range(2):
        below = [None, None]
        above = [None, None]
        for c, p in enumerate((s, 2 + s)):
            below[c], above[c] = by_parity(first, from_mate[p], from_cross[p])
        for start, end, planes in (
            (0, HALF, above), (HALF, HALF + TILE, (tile[s], tile[2 + s])), (HALF + TILE, 2 * TILE, below)
        ):
            to_right, to_left = pack_columns(*planes)
            mate[s, start:end], cross[s, start:end] = by_parity(even, to_right, to_left)


def operator_kernel(taps, probe, measured, ops, probe_near, measured_near, padded):
    probe_near[...] = probe[...]
    measured_near[...] = measured[...]
    padded[...] = jnp.zeros_like(padded)
    for axis in range(2):
        padded[2 * axis:2 * axis + 2, :31] = taps[axis]

    def band(index):
        line = jnp.broadcast_to(padded[index:index + 1, :], (TILE, 2 * TILE))
        return pltpu.roll(line, 2 * TILE - 15, 1, stride=1, stride_axis=0)[:, :TILE]

    def put(index, blocks):
        for i in range(2):
            for j in range(2):
                high, low = split(blocks[i][j])
                cols = slice(j * TILE, (j + 1) * TILE)
                ops[index, i * TILE:(i + 1) * TILE, cols] = high
                ops[index, (2 + i) * TILE:(3 + i) * TILE, cols] = low

    yr, yi = band(0), band(1)
    put(0, ((yr, -yi), (yi, yr)))
    yr, yi = yr.T, yi.T
    put(2, ((yr, yi), (-yi, yr)))
    xr, xi = band(2), band(3)
    put(3, ((xr, -xi), (xi, xr)))
    xr, xi = xr.T, xi.T
    put(1, ((xr, xi), (-xi, xr)))


def dot(a, b):
    return jnp.dot(a, b, preferred_element_type=F32)


def block(m):
    return slice(m * TILE, (m + 1) * TILE)


def main_kernel(
    offsets, counts, tall, from_cross, from_mate, probe, measured, ops,
    probe_far, object_grad,
    probe_grad, sems, beside, field_high, field_low, mid_high, mid_low, wave_one, wave_two,
    slope_one, slope_zero,
):
    even = even_column()
    for s in range(2):
        from_right, from_left = by_parity(even, from_mate[s], from_cross[s])
        beside[s], beside[2 + s] = unpack_columns(from_left, from_right)
    object_ext = (tall, beside)

    def put_field(slot, m, real, imag):
        for c, value in enumerate((real, imag)):
            high, low = split(value)
            field_high[slot, block(c), block(m)] = high
            field_low[slot, block(c), block(m)] = low

    def rows_done(slot, which):
        for n in range(2):
            cols = slice(n * 256, (n + 1) * 256)
            both = dot(ops[which], field_high[slot, :, cols])
            mid = both[:256] + (both[256:] + dot(ops[which, :256], field_low[slot, :, cols]))
            for k in range(2):
                for c in range(2):
                    high, low = split(mid[block(c), block(k)])
                    mid_high[slot, block(2 * n + k), block(c)] = high
                    mid_low[slot, block(2 * n + k), block(c)] = low

    def cols_done(slot, which, take):
        high, low = ops[which, :256], ops[which, 256:]
        for n in range(2):
            rows = slice(n * 256, (n + 1) * 256)
            gh, gl = mid_high[slot, rows], mid_low[slot, rows]
            done = dot(gh, high) + (dot(gl, high) + dot(gh, low))
            for k in range(2):
                take(slot, 2 * n + k, done[block(k), :TILE], done[block(k), TILE:])

    def propagate(which, take):
        for slot in range(2):
            rows_done(slot, which)
        for slot in range(2):
            cols_done(slot, which + 1, take)

    def window(slot, p):
        rows = [object_ext[b][p, pl.ds(offsets[2 * slot], TILE), :] for b in range(2)]
        shift = lax.rem(320 - offsets[2 * slot + 1], 256)
        return pltpu.roll(jnp.concatenate(rows, axis=1), shift, 1)[:, :TILE]

    views = [[window(slot, p) for p in range(4)] for slot in range(2)]
    for slot in range(2):
        o0r, o0i = views[slot][0], views[slot][2]
        for m in range(4):
            pr, pi = probe[m], probe[4 + m]
            put_field(slot, m, pr * o0r - pi * o0i, pr * o0i + pi * o0r)

    def after_first(slot, m, wr, wi):
        o1r, o1i = views[slot][1], views[slot][3]
        wave_one[slot, m, 0] = wr
        wave_one[slot, m, 1] = wi
        put_field(slot, m, wr * o1r - wi * o1i, wr * o1i + wi * o1r)

    propagate(0, after_first)
    intensity = [None, None]

    def after_second(slot, m, wr, wi):
        wave_two[slot, m, 0] = wr
        wave_two[slot, m, 1] = wi
        term = wr * wr + wi * wi
        intensity[slot] = term if m == 0 else intensity[slot] + term
        if m == 3:
            weight = jnp.where(slot < counts[0, 0], 2.0, 0.0).astype(F32)
            residual = (intensity[slot] - measured[slot]) * weight
            for k in range(4):
                put_field(slot, k, residual * wave_two[slot, k, 0], residual * wave_two[slot, k, 1])

    propagate(0, after_second)

    def after_third(slot, m, hr, hi):
        o1r, o1i = views[slot][1], views[slot][3]
        slope_one[slot, m, 0] = hr
        slope_one[slot, m, 1] = hi
        put_field(slot, m, hr * o1r + hi * o1i, hi * o1r - hr * o1i)

    propagate(2, after_third)

    def after_fourth(slot, m, hr, hi):
        o0r, o0i = views[slot][0], views[slot][2]
        slope_zero[slot, m, 0] = hr
        slope_zero[slot, m, 1] = hi
        dr = hr * o0r + hi * o0i
        di = hi * o0r - hr * o0i
        if slot == 0:
            probe_grad[m] = dr
            probe_grad[4 + m] = di
        else:
            probe_grad[m] += dr
            probe_grad[4 + m] += di

    propagate(2, after_fourth)
    moves = []
    for i in range(4):
        planes = pl.ds(2 * i, 2)
        moves.append(pltpu.make_async_copy(probe_grad.at[planes], probe_far.at[planes], sems.at[i]))
        moves[i].start()
    for slot in range(2):
        for s, slope in enumerate((slope_zero, slope_one)):
            real = imag = None
            for m in range(4):
                hr, hi = slope[slot, m, 0], slope[slot, m, 1]
                if s == 0:
                    wr, wi = probe[m], probe[4 + m]
                else:
                    wr, wi = wave_one[slot, m, 0], wave_one[slot, m, 1]
                terms = wr * hr + wi * hi, wr * hi - wi * hr
                real, imag = terms if m == 0 else (real + terms[0], imag + terms[1])
            object_grad[slot, s] = real
            object_grad[slot, 2 + s] = imag
    for move in moves:
        move.wait()


def object_kernel(offsets, object_grad, grad_tall, cross, mate, grad_beside):
    grad_ext = (grad_tall, grad_beside)
    for total in grad_ext:
        total[...] = jnp.zeros_like(total)
    for slot in range(2):
        for p in range(4):
            value = object_grad[slot, p]
            wide = jnp.concatenate([value, jnp.zeros_like(value)], axis=1)
            wide = pltpu.roll(wide, lax.rem(offsets[2 * slot + 1] + 192, 256), 1)
            for b in range(2):
                grad_ext[b][p, pl.ds(offsets[2 * slot], TILE), :] += wide[:, block(b)]
    even = even_column()
    for s in range(2):
        to_left, to_right = pack_columns(grad_beside[s], grad_beside[2 + s])
        mate[s], cross[s] = by_parity(even, to_right, to_left)


def spread_sum(scale, shares, spread_share):
    share = jnp.sum(shares[...], axis=0) * scale
    for i in range(spread_share.shape[0]):
        spread_share[i] = share


def fold_columns_kernel(grad_tall, from_cross, from_mate, part, cross, mate):
    even, first = even_column(), above_first()
    for s in range(2):
        from_right, from_left = by_parity(even, from_mate[s], from_cross[s])
        for p, sides in zip((s, 2 + s), unpack_columns(from_right, from_left)):
            total = grad_tall[p] + sides
            part[p] = total[HALF:HALF + TILE]
            mate[p], cross[p] = by_parity(first, total[HALF + TILE:], total[:HALF])


def fold_rows_kernel(part, from_cross, from_mate, result):
    first = above_first()
    for p in range(4):
        below, above = by_parity(first, from_mate[p], from_cross[p])
        result[p, :HALF] = part[p, :HALF] + above
        result[p, HALF:] = part[p, HALF:] + below


def finish_kernel(gathered, probe_far, sems):
    moves = []
    for i in range(4):
        part = pl.ds(256 * i, 256)
        moves.append(pltpu.make_async_copy(gathered.at[part], probe_far.at[part], sems.at[i]))
        moves[i].start()
    for move in moves:
        move.wait()


def neighbours(count, start):
    pairs = [(i, i + 1) for i in range(start, count - 1, 2)]
    return pairs + [(b, a) for a, b in pairs]


def exchange_columns(cross, mate):
    count = lax.axis_size(COL_AXES)
    from_cross = lax.ppermute(cross, COL_AXES, neighbours(count, 1))
    return from_cross, lax.ppermute(mate, COL_AXES, neighbours(count, 0))


def exchange_rows(first, second):
    count = lax.axis_size(ROW_AXES)
    axes = ROW_AXES + ("core",)
    received = []
    for value, starts in ((first, (1, 0)), (second, (0, 1))):
        pairs = [(2 * a + c, 2 * b + c) for c in range(2) for a, b in neighbours(count, starts[c])]
        received.append(lax.ppermute(value, axes, pairs))
    return received


def f32(*shape):
    return jax.ShapeDtypeStruct(shape, F32)


def body(object_field, probe_modes, prop_taps, measured, offsets, counts):
    tile = object_field.reshape(4, TILE, TILE)
    planes, strip, half = f32(4, TILE, TILE), f32(2, TILE, TILE), f32(4, HALF, TILE)
    tall, tall_strip = f32(4, 2 * TILE, TILE), f32(2, 2 * TILE, TILE)

    upper = jnp.where(above_first(), 0, HALF)
    cross = lax.dynamic_slice_in_dim(tile, upper, HALF, axis=1)
    mate = lax.dynamic_slice_in_dim(tile, HALF - upper, HALF, axis=1)
    rims = exchange_rows(cross, mate)
    cross, mate = call(columns_kernel, (tall_strip, tall_strip), [VM] * 3, tile, *rims)
    (object_tall,) = call(tall_kernel, (tall,), [VM] * 3, tile, *rims)
    strips = exchange_columns(cross, mate)
    ops, probe, targets = call(
        operator_kernel,
        (jax.ShapeDtypeStruct((4, 512, 256), BF16), f32(8, TILE, TILE), strip), [VM, VM, VM],
        prop_taps, probe_modes.reshape(8, TILE, TILE), measured.reshape(2, TILE, TILE),
        scratch=[pltpu.VMEM((8, 2 * TILE), F32)],
    )
    probe_part, object_grad = call(
        main_kernel,
        (f32(8, TILE, TILE), f32(2, 4, TILE, TILE)), [SM, SM] + [VM] * 6,
        offsets.reshape(-1), counts.reshape(1, 1), object_tall, *strips, probe, targets, ops,
        out_specs=[FAR, VM],
        scratch=[
            pltpu.VMEM((8, TILE, TILE), F32),
            pltpu.SemaphoreType.DMA((4,)),
            pltpu.VMEM((4, 256, TILE), F32),
            pltpu.VMEM((2, 256, 512), BF16),
            pltpu.VMEM((2, 256, 512), BF16),
            pltpu.VMEM((2, 512, 256), BF16),
            pltpu.VMEM((2, 512, 256), BF16),
            *[pltpu.VMEM((2, 4, 2, TILE, TILE), F32)] * 4,
        ],
        flops=3_200_000_000, moved=4_000_000,
    )
    grad_tall, cross, mate = call(
        object_kernel, (tall, tall_strip, tall_strip), [SM, VM],
        offsets.reshape(-1), object_grad,
        scratch=[pltpu.VMEM((4, 256, TILE), F32)],
    )

    near = lax.axis_size(NEAR_AXES)
    far = lax.axis_size(FAR_AXES)
    rows = 8 * TILE // near
    shares = lax.all_to_all(probe_part.reshape(near, rows, TILE), NEAR_AXES, 0, 0, tiled=True)
    spread_share = jnp.broadcast_to(jnp.sum(shares, axis=0)[None], (far, rows, TILE))
    strips = exchange_columns(cross, mate)
    shares = lax.all_to_all(spread_share, FAR_AXES, 0, 0, tiled=True)
    part, cross, mate = call(
        fold_columns_kernel, (planes, half, half), [VM] * 3, grad_tall, *strips
    )
    rims = exchange_rows(cross, mate)
    (spread_share,) = call(
        functools.partial(spread_sum, 1.0 / math.sqrt(near * far)), (f32(near, rows, TILE),), [VM], shares
    )
    gathered = lax.all_to_all(spread_share, NEAR_AXES, 0, 0, tiled=True)
    (result,) = call(
        fold_rows_kernel, (planes,), [VM] * 3, part, *rims, flops=BESIDE, moved=1
    )
    (probe_grad,) = call(
        finish_kernel, (f32(8 * TILE, TILE),), [VM], gathered.reshape(8 * TILE, TILE),
        scratch=[pltpu.SemaphoreType.DMA((4,))], out_specs=[FAR],
    )
    return result.reshape(object_field.shape), probe_grad.reshape(probe_modes.shape)


def solution(mesh):
    fine = Mesh(mesh.devices.reshape(2, 8, 2, 4, 2, 2), ROW_AXES + COL_AXES)
    return jax.shard_map(
        body,
        mesh=fine,
        in_specs=(
            P(None, None, ROW_AXES, COL_AXES),
            P(),
            P(),
            P(ROW_AXES, COL_AXES, None, None, None),
            P(ROW_AXES, COL_AXES, None, None),
            P(ROW_AXES, COL_AXES),
        ),
        out_specs=(P(None, None, ROW_AXES, COL_AXES), P()),
        check_vma=False,
    )
```

```python
import functools
import math

import jax
import jax.numpy as jnp
from jax import lax
from jax.experimental import pallas as pl
from jax.experimental.pallas import tpu as pltpu
from jax.sharding import Mesh
from jax.sharding import PartitionSpec as P

F32 = jnp.float32
BF16 = jnp.bfloat16
ROW_AXES = ("xl", "za", "zb")
COL_AXES = ("y", "xh", "core")
PLANE_AXES = ("xl", "y", "xh", "core")
NEAR_AXES = PLANE_AXES + ("zb",)
FAR_AXES = ("za", "zb")
VMEM_LIMIT = 12 * 1024 * 1024
TILE = 128
HALF = 64
BESIDE = 100_000_000_000
VM = pl.BlockSpec(memory_space=pltpu.VMEM)
SM = pl.BlockSpec(memory_space=pltpu.SMEM)
FAR = pl.BlockSpec(memory_space=pltpu.HBM)


def call(kernel, out_shape, in_specs, *args, scratch=(), out_specs=None, flops=0, moved=0):
    out_shape = tuple(out_shape)
    return pl.pallas_call(
        kernel,
        out_shape=out_shape,
        in_specs=in_specs,
        out_specs=tuple(out_specs or [VM] * len(out_shape)),
        scratch_shapes=list(scratch),
        compiler_params=pltpu.CompilerParams(vmem_limit_bytes=VMEM_LIMIT),
        cost_estimate=pl.CostEstimate(flops=flops, bytes_accessed=moved, transcendentals=0),
    )(*args)


def low_lanes(shape):
    return lax.broadcasted_iota(jnp.int32, shape, len(shape) - 1) < HALF


def split(value):
    high = value.astype(BF16)
    return high, (value - high.astype(F32)).astype(BF16)


def even_column():
    return lax.axis_index("core") == 0


def above_first():
    return lax.axis_index("zb") == lax.axis_index("core")


def by_parity(even, first, second):
    return jnp.where(even, first, second), jnp.where(even, second, first)


def pack_columns(real, imag):
    low = low_lanes(real.shape)
    turned = pltpu.roll(imag, HALF, 1)
    return jnp.where(low, turned, real), jnp.where(low, real, turned)


def unpack_columns(from_left, from_right):
    low = low_lanes(from_left.shape)
    real = jnp.where(low, from_right, from_left)
    return real, pltpu.roll(jnp.where(low, from_left, from_right), HALF, 1)


def columns_kernel(tile, from_cross, from_mate, tall, cross, mate):
    first = above_first()
    for p in range(4):
        below, above = by_parity(first, from_mate[p], from_cross[p])
        tall[p, :HALF] = above
        tall[p, HALF:HALF + TILE] = tile[p]
        tall[p, HALF + TILE:] = below
    even = even_column()
    for s in range(2):
        to_right, to_left = pack_columns(tall[s], tall[2 + s])
        mate[s], cross[s] = by_parity(even, to_right, to_left)


def operator_kernel(taps, probe, measured, ops, probe_near, measured_near, padded):
    probe_near[...] = probe[...]
    measured_near[...] = measured[...]
    padded[...] = jnp.zeros_like(padded)
    for axis in range(2):
        padded[2 * axis:2 * axis + 2, :31] = taps[axis]

    def band(index):
        line = jnp.broadcast_to(padded[index:index + 1, :], (TILE, 2 * TILE))
        return pltpu.roll(line, 2 * TILE - 15, 1, stride=1, stride_axis=0)[:, :TILE]

    def put(index, blocks):
        for i in range(2):
            for j in range(2):
                high, low = split(blocks[i][j])
                cols = slice(j * TILE, (j + 1) * TILE)
                ops[index, i * TILE:(i + 1) * TILE, cols] = high
                ops[index, (2 + i) * TILE:(3 + i) * TILE, cols] = low

    yr, yi = band(0), band(1)
    put(0, ((yr, -yi), (yi, yr)))
    yr, yi = yr.T, yi.T
    put(2, ((yr, yi), (-yi, yr)))
    xr, xi = band(2), band(3)
    put(3, ((xr, -xi), (xi, xr)))
    xr, xi = xr.T, xi.T
    put(1, ((xr, xi), (-xi, xr)))


def dot(a, b):
    return jnp.dot(a, b, preferred_element_type=F32)


def block(m):
    return slice(m * TILE, (m + 1) * TILE)


def main_kernel(
    offsets, counts, tall, from_cross, from_mate, probe, measured, ops,
    probe_grad, object_grad,
    beside, field_high, field_low, mid_high, mid_low, wave_one, wave_two,
):
    even = even_column()
    for s in range(2):
        from_right, from_left = by_parity(even, from_mate[s], from_cross[s])
        beside[s], beside[2 + s] = unpack_columns(from_left, from_right)
    object_ext = (tall, beside)

    def put_field(slot, m, real, imag):
        for c, value in enumerate((real, imag)):
            high, low = split(value)
            field_high[slot, block(c), block(m)] = high
            field_low[slot, block(c), block(m)] = low

    def rows_done(slot, which):
        for n in range(2):
            cols = slice(n * 256, (n + 1) * 256)
            both = dot(ops[which], field_high[slot, :, cols])
            mid = both[:256] + (both[256:] + dot(ops[which, :256], field_low[slot, :, cols]))
            for k in range(2):
                for c in range(2):
                    high, low = split(mid[block(c), block(k)])
                    mid_high[slot, block(2 * n + k), block(c)] = high
                    mid_low[slot, block(2 * n + k), block(c)] = low

    def cols_done(slot, which, take):
        high, low = ops[which, :256], ops[which, 256:]
        for n in range(2):
            rows = slice(n * 256, (n + 1) * 256)
            gh, gl = mid_high[slot, rows], mid_low[slot, rows]
            done = dot(gh, high) + (dot(gl, high) + dot(gh, low))
            for k in range(2):
                take(slot, 2 * n + k, done[block(k), :TILE], done[block(k), TILE:])

    def propagate(which, take):
        for slot in range(2):
            rows_done(slot, which)
        for slot in range(2):
            cols_done(slot, which + 1, take)

    def window(slot, p):
        rows = [object_ext[b][p, pl.ds(offsets[2 * slot], TILE), :] for b in range(2)]
        shift = lax.rem(320 - offsets[2 * slot + 1], 256)
        return pltpu.roll(jnp.concatenate(rows, axis=1), shift, 1)[:, :TILE]

    views = [[window(slot, p) for p in range(4)] for slot in range(2)]
    for slot in range(2):
        o0r, o0i = views[slot][0], views[slot][2]
        for m in range(4):
            pr, pi = probe[m], probe[4 + m]
            put_field(slot, m, pr * o0r - pi * o0i, pr * o0i + pi * o0r)

    def after_first(slot, m, wr, wi):
        o1r, o1i = views[slot][1], views[slot][3]
        wave_one[slot, m, 0] = wr
        wave_one[slot, m, 1] = wi
        put_field(slot, m, wr * o1r - wi * o1i, wr * o1i + wi * o1r)

    propagate(0, after_first)
    intensity = [None, None]

    def after_second(slot, m, wr, wi):
        wave_two[slot, m, 0] = wr
        wave_two[slot, m, 1] = wi
        term = wr * wr + wi * wi
        intensity[slot] = term if m == 0 else intensity[slot] + term
        if m == 3:
            weight = jnp.where(slot < counts[0, 0], 2.0, 0.0).astype(F32)
            residual = (intensity[slot] - measured[slot]) * weight
            for k in range(4):
                put_field(slot, k, residual * wave_two[slot, k, 0], residual * wave_two[slot, k, 1])

    propagate(0, after_second)

    def add(slot, s, m, real, imag):
        for p, value in zip((s, 2 + s), (real, imag)):
            if m == 0:
                object_grad[slot, p] = value
            else:
                object_grad[slot, p] += value

    def after_third(slot, m, hr, hi):
        o1r, o1i = views[slot][1], views[slot][3]
        wr, wi = wave_one[slot, m, 0], wave_one[slot, m, 1]
        add(slot, 1, m, wr * hr + wi * hi, wr * hi - wi * hr)
        put_field(slot, m, hr * o1r + hi * o1i, hi * o1r - hr * o1i)

    propagate(2, after_third)

    def after_fourth(slot, m, hr, hi):
        o0r, o0i = views[slot][0], views[slot][2]
        pr, pi = probe[m], probe[4 + m]
        add(slot, 0, m, pr * hr + pi * hi, pr * hi - pi * hr)
        dr = hr * o0r + hi * o0i
        di = hi * o0r - hr * o0i
        if slot == 0:
            probe_grad[m] = dr
            probe_grad[4 + m] = di
        else:
            probe_grad[m] += dr
            probe_grad[4 + m] += di

    propagate(2, after_fourth)


def object_kernel(offsets, object_grad, grad_tall, cross, mate, grad_beside):
    grad_ext = (grad_tall, grad_beside)
    for total in grad_ext:
        total[...] = jnp.zeros_like(total)
    for slot in range(2):
        for p in range(4):
            value = object_grad[slot, p]
            wide = jnp.concatenate([value, jnp.zeros_like(value)], axis=1)
            wide = pltpu.roll(wide, lax.rem(offsets[2 * slot + 1] + 192, 256), 1)
            for b in range(2):
                grad_ext[b][p, pl.ds(offsets[2 * slot], TILE), :] += wide[:, block(b)]
    even = even_column()
    for s in range(2):
        to_left, to_right = pack_columns(grad_beside[s], grad_beside[2 + s])
        mate[s], cross[s] = by_parity(even, to_right, to_left)


def spread_sum(scale, shares, spread_share):
    count, rows = shares.shape[:2]
    for member in range(2):
        share = shares[member]
        for i in range(member + 2, count, 2):
            share += shares[i]
        share *= scale
        for i in range(spread_share.shape[0]):
            spread_share[i, member * rows:(member + 1) * rows] = share


def fold_columns_kernel(grad_tall, from_cross, from_mate, part, cross, mate):
    even, first = even_column(), above_first()
    for s in range(2):
        from_right, from_left = by_parity(even, from_mate[s], from_cross[s])
        for p, sides in zip((s, 2 + s), unpack_columns(from_right, from_left)):
            total = grad_tall[p] + sides
            part[p] = total[HALF:HALF + TILE]
            mate[p], cross[p] = by_parity(first, total[HALF + TILE:], total[:HALF])


def fold_rows_kernel(part, from_cross, from_mate, result):
    first = above_first()
    for p in range(4):
        below, above = by_parity(first, from_mate[p], from_cross[p])
        result[p, :HALF] = part[p, :HALF] + above
        result[p, HALF:] = part[p, HALF:] + below


def finish_kernel(gathered, probe_far, sems):
    moves = []
    for i in range(4):
        part = pl.ds(256 * i, 256)
        moves.append(pltpu.make_async_copy(gathered.at[part], probe_far.at[part], sems.at[i]))
        moves[i].start()
    for move in moves:
        move.wait()


def neighbours(count, start):
    pairs = [(i, i + 1) for i in range(start, count - 1, 2)]
    return pairs + [(b, a) for a, b in pairs]


def exchange_columns(cross, mate):
    count = lax.axis_size(COL_AXES)
    from_cross = lax.ppermute(cross, COL_AXES, neighbours(count, 1))
    return from_cross, lax.ppermute(mate, COL_AXES, neighbours(count, 0))


def exchange_rows(first, second):
    count = lax.axis_size(ROW_AXES)
    axes = ROW_AXES + ("core",)
    received = []
    for value, starts in ((first, (1, 0)), (second, (0, 1))):
        pairs = [(2 * a + c, 2 * b + c) for c in range(2) for a, b in neighbours(count, starts[c])]
        received.append(lax.ppermute(value, axes, pairs))
    return received


def f32(*shape):
    return jax.ShapeDtypeStruct(shape, F32)


def body(object_field, probe_modes, prop_taps, measured, offsets, counts):
    tile = object_field.reshape(4, TILE, TILE)
    planes, strip, half = f32(4, TILE, TILE), f32(2, TILE, TILE), f32(4, HALF, TILE)
    tall, tall_strip = f32(4, 2 * TILE, TILE), f32(2, 2 * TILE, TILE)

    upper = jnp.where(above_first(), 0, HALF)
    cross = lax.dynamic_slice_in_dim(tile, upper, HALF, axis=1)
    mate = lax.dynamic_slice_in_dim(tile, HALF - upper, HALF, axis=1)
    rims = exchange_rows(cross, mate)
    object_tall, cross, mate = call(
        columns_kernel, (tall, tall_strip, tall_strip), [VM] * 3, tile, *rims
    )
    strips = exchange_columns(cross, mate)
    ops, probe, targets = call(
        operator_kernel,
        (jax.ShapeDtypeStruct((4, 512, 256), BF16), f32(8, TILE, TILE), strip), [VM, VM, VM],
        prop_taps, probe_modes.reshape(8, TILE, TILE), measured.reshape(2, TILE, TILE),
        scratch=[pltpu.VMEM((8, 2 * TILE), F32)],
    )
    probe_part, object_grad = call(
        main_kernel,
        (f32(8, TILE, TILE), f32(2, 4, TILE, TILE)), [SM, SM] + [VM] * 6,
        offsets.reshape(-1), counts.reshape(1, 1), object_tall, *strips, probe, targets, ops,
        scratch=[
            pltpu.VMEM((4, 256, TILE), F32),
            pltpu.VMEM((2, 256, 512), BF16),
            pltpu.VMEM((2, 256, 512), BF16),
            pltpu.VMEM((2, 512, 256), BF16),
            pltpu.VMEM((2, 512, 256), BF16),
            pltpu.VMEM((2, 4, 2, TILE, TILE), F32),
            pltpu.VMEM((2, 4, 2, TILE, TILE), F32),
        ],
        flops=3_200_000_000, moved=4_000_000,
    )
    grad_tall, cross, mate = call(
        object_kernel, (tall, tall_strip, tall_strip), [SM, VM],
        offsets.reshape(-1), object_grad,
        scratch=[pltpu.VMEM((4, 256, TILE), F32)],
    )

    near = lax.axis_size(NEAR_AXES)
    far, plane = lax.axis_size(FAR_AXES), lax.axis_size(PLANE_AXES)
    rows = 8 * TILE // near
    shares = lax.all_to_all(probe_part.reshape(near, rows, TILE), NEAR_AXES, 0, 0, tiled=True)
    spread_share = jnp.broadcast_to(jnp.sum(shares, axis=0)[None], (far, rows, TILE))
    strips = exchange_columns(cross, mate)
    shares = lax.all_to_all(spread_share, FAR_AXES, 0, 0, tiled=True)
    part, cross, mate = call(
        fold_columns_kernel, (planes, half, half), [VM] * 3, grad_tall, *strips, flops=BESIDE, moved=1
    )
    rims = exchange_rows(cross, mate)
    (spread_share,) = call(
        functools.partial(spread_sum, 1.0 / math.sqrt(plane * far)), (f32(plane, 2 * rows, TILE),), [VM], shares
    )
    gathered = lax.all_to_all(spread_share, PLANE_AXES, 0, 0, tiled=True)
    (result,) = call(
        fold_rows_kernel, (planes,), [VM] * 3, part, *rims, flops=BESIDE, moved=1
    )
    (probe_grad,) = call(
        finish_kernel, (f32(8 * TILE, TILE),), [VM], gathered.reshape(8 * TILE, TILE),
        scratch=[pltpu.SemaphoreType.DMA((4,))], out_specs=[FAR],
    )
    return result.reshape(object_field.shape), probe_grad.reshape(probe_modes.shape)


def solution(mesh):
    fine = Mesh(mesh.devices.reshape(2, 8, 2, 4, 2, 2), ROW_AXES + COL_AXES)
    return jax.shard_map(
        body,
        mesh=fine,
        in_specs=(
            P(None, None, ROW_AXES, COL_AXES),
            P(),
            P(),
            P(ROW_AXES, COL_AXES, None, None, None),
            P(ROW_AXES, COL_AXES, None, None),
            P(ROW_AXES, COL_AXES),
        ),
        out_specs=(P(None, None, ROW_AXES, COL_AXES), P()),
        check_vma=False,
    )
```

```python
import functools
import math

import jax
import jax.numpy as jnp
from jax import lax
from jax.experimental import pallas as pl
from jax.experimental.pallas import tpu as pltpu
from jax.sharding import Mesh
from jax.sharding import PartitionSpec as P

F32 = jnp.float32
BF16 = jnp.bfloat16
ROW_AXES = ("xl", "za", "zb")
COL_AXES = ("y", "xh", "core")
NEAR_AXES = ("xl", "zb", "y", "xh", "core")
FAR_AXES = ("za",)
VMEM_LIMIT = 12 * 1024 * 1024
TILE = 128
HALF = 64
BESIDE = 100_000_000_000
VM = pl.BlockSpec(memory_space=pltpu.VMEM)
SM = pl.BlockSpec(memory_space=pltpu.SMEM)
FAR = pl.BlockSpec(memory_space=pltpu.HBM)


def call(kernel, out_shape, in_specs, *args, scratch=(), out_specs=None, flops=0, moved=0):
    out_shape = tuple(out_shape)
    return pl.pallas_call(
        kernel,
        out_shape=out_shape,
        in_specs=in_specs,
        out_specs=tuple(out_specs or [VM] * len(out_shape)),
        scratch_shapes=list(scratch),
        compiler_params=pltpu.CompilerParams(vmem_limit_bytes=VMEM_LIMIT),
        cost_estimate=pl.CostEstimate(flops=flops, bytes_accessed=moved, transcendentals=0),
    )(*args)


def low_lanes(shape):
    return lax.broadcasted_iota(jnp.int32, shape, len(shape) - 1) < HALF


def split(value):
    high = value.astype(BF16)
    return high, (value - high.astype(F32)).astype(BF16)


def even_column():
    return lax.axis_index("core") == 0


def even_row():
    return lax.axis_index("zb") == 0


def by_parity(even, first, second):
    return jnp.where(even, first, second), jnp.where(even, second, first)


def pack_columns(real, imag):
    low = low_lanes(real.shape)
    turned = pltpu.roll(imag, HALF, 1)
    return jnp.where(low, turned, real), jnp.where(low, real, turned)


def unpack_columns(from_left, from_right):
    low = low_lanes(from_left.shape)
    real = jnp.where(low, from_right, from_left)
    return real, pltpu.roll(jnp.where(low, from_left, from_right), HALF, 1)


def rows_kernel(tile, cross, mate):
    even = even_row()
    for p in range(4):
        mate[p], cross[p] = by_parity(even, tile[p, HALF:], tile[p, :HALF])


def columns_kernel(tile, from_cross, from_mate, tall, cross, mate):
    even = even_row()
    for p in range(4):
        below, above = by_parity(even, from_mate[p], from_cross[p])
        tall[p, :HALF] = above
        tall[p, HALF:HALF + TILE] = tile[p]
        tall[p, HALF + TILE:] = below
    even = even_column()
    for s in range(2):
        to_right, to_left = pack_columns(tall[s], tall[2 + s])
        mate[s], cross[s] = by_parity(even, to_right, to_left)


def operator_kernel(taps, probe, measured, ops, probe_near, measured_near, padded):
    probe_near[...] = probe[...]
    measured_near[...] = measured[...]
    padded[...] = jnp.zeros_like(padded)
    for axis in range(2):
        padded[2 * axis:2 * axis + 2, :31] = taps[axis]

    def band(index):
        line = jnp.broadcast_to(padded[index:index + 1, :], (TILE, 2 * TILE))
        return pltpu.roll(line, 2 * TILE - 15, 1, stride=1, stride_axis=0)[:, :TILE]

    def put(index, blocks):
        for i in range(2):
            for j in range(2):
                high, low = split(blocks[i][j])
                cols = slice(j * TILE, (j + 1) * TILE)
                ops[index, i * TILE:(i + 1) * TILE, cols] = high
                ops[index, (2 + i) * TILE:(3 + i) * TILE, cols] = low

    yr, yi = band(0), band(1)
    put(0, ((yr, -yi), (yi, yr)))
    yr, yi = yr.T, yi.T
    put(2, ((yr, yi), (-yi, yr)))
    xr, xi = band(2), band(3)
    put(3, ((xr, -xi), (xi, xr)))
    xr, xi = xr.T, xi.T
    put(1, ((xr, xi), (-xi, xr)))


def dot(a, b):
    return jnp.dot(a, b, preferred_element_type=F32)


def block(m):
    return slice(m * TILE, (m + 1) * TILE)


def main_kernel(
    offsets, counts, tall, from_cross, from_mate, probe, measured, ops,
    probe_grad, object_grad,
    beside, field_high, field_low, mid_high, mid_low, wave_one, wave_two,
):
    even = even_column()
    for s in range(2):
        from_right, from_left = by_parity(even, from_mate[s], from_cross[s])
        beside[s], beside[2 + s] = unpack_columns(from_left, from_right)
    object_ext = (tall, beside)

    def put_field(slot, m, real, imag):
        for c, value in enumerate((real, imag)):
            high, low = split(value)
            field_high[slot, block(c), block(m)] = high
            field_low[slot, block(c), block(m)] = low

    def rows_done(slot, which):
        for n in range(2):
            cols = slice(n * 256, (n + 1) * 256)
            both = dot(ops[which], field_high[slot, :, cols])
            mid = both[:256] + (both[256:] + dot(ops[which, :256], field_low[slot, :, cols]))
            for k in range(2):
                for c in range(2):
                    high, low = split(mid[block(c), block(k)])
                    mid_high[slot, block(2 * n + k), block(c)] = high
                    mid_low[slot, block(2 * n + k), block(c)] = low

    def cols_done(slot, which, take):
        high, low = ops[which, :256], ops[which, 256:]
        for n in range(2):
            rows = slice(n * 256, (n + 1) * 256)
            gh, gl = mid_high[slot, rows], mid_low[slot, rows]
            done = dot(gh, high) + (dot(gl, high) + dot(gh, low))
            for k in range(2):
                take(slot, 2 * n + k, done[block(k), :TILE], done[block(k), TILE:])

    def propagate(which, take):
        for slot in range(2):
            rows_done(slot, which)
        for slot in range(2):
            cols_done(slot, which + 1, take)

    def window(slot, p):
        rows = [object_ext[b][p, pl.ds(offsets[2 * slot], TILE), :] for b in range(2)]
        shift = lax.rem(320 - offsets[2 * slot + 1], 256)
        return pltpu.roll(jnp.concatenate(rows, axis=1), shift, 1)[:, :TILE]

    views = [[window(slot, p) for p in range(4)] for slot in range(2)]
    for slot in range(2):
        o0r, o0i = views[slot][0], views[slot][2]
        for m in range(4):
            pr, pi = probe[m], probe[4 + m]
            put_field(slot, m, pr * o0r - pi * o0i, pr * o0i + pi * o0r)

    def after_first(slot, m, wr, wi):
        o1r, o1i = views[slot][1], views[slot][3]
        wave_one[slot, m, 0] = wr
        wave_one[slot, m, 1] = wi
        put_field(slot, m, wr * o1r - wi * o1i, wr * o1i + wi * o1r)

    propagate(0, after_first)
    intensity = [None, None]

    def after_second(slot, m, wr, wi):
        wave_two[slot, m, 0] = wr
        wave_two[slot, m, 1] = wi
        term = wr * wr + wi * wi
        intensity[slot] = term if m == 0 else intensity[slot] + term
        if m == 3:
            weight = jnp.where(slot < counts[0, 0], 2.0, 0.0).astype(F32)
            residual = (intensity[slot] - measured[slot]) * weight
            for k in range(4):
                put_field(slot, k, residual * wave_two[slot, k, 0], residual * wave_two[slot, k, 1])

    propagate(0, after_second)

    def add(slot, s, m, real, imag):
        for p, value in zip((s, 2 + s), (real, imag)):
            if m == 0:
                object_grad[slot, p] = value
            else:
                object_grad[slot, p] += value

    def after_third(slot, m, hr, hi):
        o1r, o1i = views[slot][1], views[slot][3]
        wr, wi = wave_one[slot, m, 0], wave_one[slot, m, 1]
        add(slot, 1, m, wr * hr + wi * hi, wr * hi - wi * hr)
        put_field(slot, m, hr * o1r + hi * o1i, hi * o1r - hr * o1i)

    propagate(2, after_third)

    def after_fourth(slot, m, hr, hi):
        o0r, o0i = views[slot][0], views[slot][2]
        pr, pi = probe[m], probe[4 + m]
        add(slot, 0, m, pr * hr + pi * hi, pr * hi - pi * hr)
        dr = hr * o0r + hi * o0i
        di = hi * o0r - hr * o0i
        if slot == 0:
            probe_grad[m] = dr
            probe_grad[4 + m] = di
        else:
            probe_grad[m] += dr
            probe_grad[4 + m] += di

    propagate(2, after_fourth)


def object_kernel(offsets, object_grad, grad_tall, cross, mate, grad_beside):
    grad_ext = (grad_tall, grad_beside)
    for total in grad_ext:
        total[...] = jnp.zeros_like(total)
    for slot in range(2):
        for p in range(4):
            value = object_grad[slot, p]
            wide = jnp.concatenate([value, jnp.zeros_like(value)], axis=1)
            wide = pltpu.roll(wide, lax.rem(offsets[2 * slot + 1] + 192, 256), 1)
            for b in range(2):
                grad_ext[b][p, pl.ds(offsets[2 * slot], TILE), :] += wide[:, block(b)]
    even = even_column()
    for s in range(2):
        to_left, to_right = pack_columns(grad_beside[s], grad_beside[2 + s])
        mate[s], cross[s] = by_parity(even, to_right, to_left)


def spread_sum(scale, shares, spread_share):
    share = jnp.sum(shares[...], axis=0) * scale
    for i in range(spread_share.shape[0]):
        spread_share[i] = share


def fold_columns_kernel(grad_tall, from_cross, from_mate, part, cross, mate):
    even, even_down = even_column(), even_row()
    for s in range(2):
        from_right, from_left = by_parity(even, from_mate[s], from_cross[s])
        for p, sides in zip((s, 2 + s), unpack_columns(from_right, from_left)):
            total = grad_tall[p] + sides
            part[p] = total[HALF:HALF + TILE]
            mate[p], cross[p] = by_parity(even_down, total[HALF + TILE:], total[:HALF])


def fold_rows_kernel(part, from_cross, from_mate, result):
    even = even_row()
    for p in range(4):
        below, above = by_parity(even, from_mate[p], from_cross[p])
        result[p, :HALF] = part[p, :HALF] + above
        result[p, HALF:] = part[p, HALF:] + below


def finish_kernel(gathered, probe_far, sems):
    moves = []
    for i in range(4):
        part = pl.ds(256 * i, 256)
        moves.append(pltpu.make_async_copy(gathered.at[part], probe_far.at[part], sems.at[i]))
        moves[i].start()
    for move in moves:
        move.wait()


def exchange(cross, mate, axes):
    count = lax.axis_size(axes)
    pairs = [(i, i + 1) for i in range(1, count - 1, 2)]
    from_cross = lax.ppermute(cross, axes, pairs + [(b, a) for a, b in pairs])
    pairs = [(i, i + 1) for i in range(0, count, 2)]
    from_mate = lax.ppermute(mate, axes, pairs + [(b, a) for a, b in pairs])
    return from_cross, from_mate


def f32(*shape):
    return jax.ShapeDtypeStruct(shape, F32)


def body(object_field, probe_modes, prop_taps, measured, offsets, counts):
    tile = object_field.reshape(4, TILE, TILE)
    planes, strip, half = f32(4, TILE, TILE), f32(2, TILE, TILE), f32(4, HALF, TILE)
    tall, tall_strip = f32(4, 2 * TILE, TILE), f32(2, 2 * TILE, TILE)

    rims = exchange(*call(rows_kernel, (half, half), [VM], tile), ROW_AXES)
    object_tall, cross, mate = call(
        columns_kernel, (tall, tall_strip, tall_strip), [VM] * 3, tile, *rims
    )
    strips = exchange(cross, mate, COL_AXES)
    ops, probe, targets = call(
        operator_kernel,
        (jax.ShapeDtypeStruct((4, 512, 256), BF16), f32(8, TILE, TILE), strip), [VM, VM, VM],
        prop_taps, probe_modes.reshape(8, TILE, TILE), measured.reshape(2, TILE, TILE),
        scratch=[pltpu.VMEM((8, 2 * TILE), F32)],
    )
    probe_part, object_grad = call(
        main_kernel,
        (f32(8, TILE, TILE), f32(2, 4, TILE, TILE)), [SM, SM] + [VM] * 6,
        offsets.reshape(-1), counts.reshape(1, 1), object_tall, *strips, probe, targets, ops,
        scratch=[
            pltpu.VMEM((4, 256, TILE), F32),
            pltpu.VMEM((2, 256, 512), BF16),
            pltpu.VMEM((2, 256, 512), BF16),
            pltpu.VMEM((2, 512, 256), BF16),
            pltpu.VMEM((2, 512, 256), BF16),
            pltpu.VMEM((2, 4, 2, TILE, TILE), F32),
            pltpu.VMEM((2, 4, 2, TILE, TILE), F32),
        ],
        flops=3_200_000_000, moved=4_000_000,
    )
    grad_tall, cross, mate = call(
        object_kernel, (tall, tall_strip, tall_strip), [SM, VM],
        offsets.reshape(-1), object_grad,
        scratch=[pltpu.VMEM((4, 256, TILE), F32)],
    )

    near = lax.axis_size(NEAR_AXES)
    far = lax.axis_size(FAR_AXES)
    rows = 8 * TILE // near
    shares = lax.all_to_all(probe_part.reshape(near, rows, TILE), NEAR_AXES, 0, 0, tiled=True)
    spread_share = jnp.broadcast_to(jnp.sum(shares, axis=0)[None], (far, rows, TILE))
    strips = exchange(cross, mate, COL_AXES)
    shares = lax.all_to_all(spread_share, FAR_AXES, 0, 0, tiled=True)
    part, cross, mate = call(
        fold_columns_kernel, (planes, half, half), [VM] * 3, grad_tall, *strips
    )
    rims = exchange(cross, mate, ROW_AXES)
    (spread_share,) = call(
        functools.partial(spread_sum, 1.0 / math.sqrt(near * far)), (f32(near, rows, TILE),), [VM], shares
    )
    gathered = lax.all_to_all(spread_share, NEAR_AXES, 0, 0, tiled=True)
    (result,) = call(
        fold_rows_kernel, (planes,), [VM] * 3, part, *rims, flops=BESIDE, moved=1
    )
    (probe_grad,) = call(
        finish_kernel, (f32(8 * TILE, TILE),), [VM], gathered.reshape(8 * TILE, TILE),
        scratch=[pltpu.SemaphoreType.DMA((4,))], out_specs=[FAR],
    )
    return result.reshape(object_field.shape), probe_grad.reshape(probe_modes.shape)


def solution(mesh):
    fine = Mesh(mesh.devices.reshape(2, 8, 2, 4, 2, 2), ROW_AXES + COL_AXES)
    return jax.shard_map(
        body,
        mesh=fine,
        in_specs=(
            P(None, None, ROW_AXES, COL_AXES),
            P(),
            P(),
            P(ROW_AXES, COL_AXES, None, None, None),
            P(ROW_AXES, COL_AXES, None, None),
            P(ROW_AXES, COL_AXES),
        ),
        out_specs=(P(None, None, ROW_AXES, COL_AXES), P()),
        check_vma=False,
    )
```

```python
import functools
import math

import jax
import jax.numpy as jnp
from jax import lax
from jax.experimental import pallas as pl
from jax.experimental.pallas import tpu as pltpu
from jax.sharding import Mesh
from jax.sharding import PartitionSpec as P

F32 = jnp.float32
BF16 = jnp.bfloat16
ROW_AXES = ("xl", "za", "zb")
COL_AXES = ("y", "xh", "core")
NEAR_AXES = ("xl", "zb", "y", "xh", "core")
FAR_AXES = ("za",)
VMEM_LIMIT = 12 * 1024 * 1024
TILE = 128
HALF = 64
BESIDE = 100_000_000_000
VM = pl.BlockSpec(memory_space=pltpu.VMEM)
SM = pl.BlockSpec(memory_space=pltpu.SMEM)
FAR = pl.BlockSpec(memory_space=pltpu.HBM)


def call(kernel, out_shape, in_specs, *args, scratch=(), out_specs=None, flops=0, moved=0):
    out_shape = tuple(out_shape)
    return pl.pallas_call(
        kernel,
        out_shape=out_shape,
        in_specs=in_specs,
        out_specs=tuple(out_specs or [VM] * len(out_shape)),
        scratch_shapes=list(scratch),
        compiler_params=pltpu.CompilerParams(vmem_limit_bytes=VMEM_LIMIT),
        cost_estimate=pl.CostEstimate(flops=flops, bytes_accessed=moved, transcendentals=0),
    )(*args)


def low_lanes(shape):
    return lax.broadcasted_iota(jnp.int32, shape, len(shape) - 1) < HALF


def split(value):
    high = value.astype(BF16)
    return high, (value - high.astype(F32)).astype(BF16)


def even_column():
    return lax.axis_index("core") == 0


def even_row():
    return lax.axis_index("zb") == 0


def by_parity(even, first, second):
    return jnp.where(even, first, second), jnp.where(even, second, first)


def pack_columns(real, imag):
    low = low_lanes(real.shape)
    turned = pltpu.roll(imag, HALF, 1)
    return jnp.where(low, turned, real), jnp.where(low, real, turned)


def unpack_columns(from_left, from_right):
    low = low_lanes(from_left.shape)
    real = jnp.where(low, from_right, from_left)
    return real, pltpu.roll(jnp.where(low, from_left, from_right), HALF, 1)


def rows_kernel(tile, cross, mate):
    even = even_row()
    for p in range(4):
        mate[p], cross[p] = by_parity(even, tile[p, HALF:], tile[p, :HALF])


def tall_kernel(tile, from_cross, from_mate, tall):
    even = even_row()
    for p in range(4):
        below, above = by_parity(even, from_mate[p], from_cross[p])
        tall[p, :HALF] = above
        tall[p, HALF:HALF + TILE] = tile[p]
        tall[p, HALF + TILE:] = below


def columns_kernel(tile, from_cross, from_mate, cross, mate):
    down, even = even_row(), even_column()
    for s in range(2):
        ends = [by_parity(down, from_mate[p], from_cross[p]) for p in (s, 2 + s)]
        for start, end, planes in (
            (0, HALF, (ends[0][1], ends[1][1])),
            (HALF, HALF + TILE, (tile[s], tile[2 + s])),
            (HALF + TILE, 2 * TILE, (ends[0][0], ends[1][0])),
        ):
            to_right, to_left = pack_columns(*planes)
            mate[s, start:end], cross[s, start:end] = by_parity(even, to_right, to_left)


def operator_kernel(taps, probe, measured, ops, probe_near, measured_near, padded):
    probe_near[...] = probe[...]
    measured_near[...] = measured[...]
    padded[...] = jnp.zeros_like(padded)
    for axis in range(2):
        padded[2 * axis:2 * axis + 2, :31] = taps[axis]

    def band(index):
        line = jnp.broadcast_to(padded[index:index + 1, :], (TILE, 2 * TILE))
        return pltpu.roll(line, 2 * TILE - 15, 1, stride=1, stride_axis=0)[:, :TILE]

    def put(index, blocks):
        for i in range(2):
            for j in range(2):
                high, low = split(blocks[i][j])
                cols = slice(j * TILE, (j + 1) * TILE)
                ops[index, i * TILE:(i + 1) * TILE, cols] = high
                ops[index, (2 + i) * TILE:(3 + i) * TILE, cols] = low

    yr, yi = band(0), band(1)
    put(0, ((yr, -yi), (yi, yr)))
    yr, yi = yr.T, yi.T
    put(2, ((yr, yi), (-yi, yr)))
    xr, xi = band(2), band(3)
    put(3, ((xr, -xi), (xi, xr)))
    xr, xi = xr.T, xi.T
    put(1, ((xr, xi), (-xi, xr)))


def dot(a, b):
    return jnp.dot(a, b, preferred_element_type=F32)


def block(m):
    return slice(m * TILE, (m + 1) * TILE)


def main_kernel(
    offsets, counts, tall, from_cross, from_mate, probe, measured, ops,
    probe_grad, object_grad,
    beside, field_high, field_low, mid_high, mid_low, wave_one, wave_two,
):
    even = even_column()
    for s in range(2):
        from_right, from_left = by_parity(even, from_mate[s], from_cross[s])
        beside[s], beside[2 + s] = unpack_columns(from_left, from_right)
    object_ext = (tall, beside)

    def put_field(slot, m, real, imag):
        for c, value in enumerate((real, imag)):
            high, low = split(value)
            field_high[slot, block(c), block(m)] = high
            field_low[slot, block(c), block(m)] = low

    def rows_done(slot, which):
        for n in range(2):
            cols = slice(n * 256, (n + 1) * 256)
            both = dot(ops[which], field_high[slot, :, cols])
            mid = both[:256] + (both[256:] + dot(ops[which, :256], field_low[slot, :, cols]))
            for k in range(2):
                for c in range(2):
                    high, low = split(mid[block(c), block(k)])
                    mid_high[slot, block(2 * n + k), block(c)] = high
                    mid_low[slot, block(2 * n + k), block(c)] = low

    def cols_done(slot, which, take):
        high, low = ops[which, :256], ops[which, 256:]
        for n in range(2):
            rows = slice(n * 256, (n + 1) * 256)
            gh, gl = mid_high[slot, rows], mid_low[slot, rows]
            done = dot(gh, high) + (dot(gl, high) + dot(gh, low))
            for k in range(2):
                take(slot, 2 * n + k, done[block(k), :TILE], done[block(k), TILE:])

    def propagate(which, take):
        for slot in range(2):
            rows_done(slot, which)
        for slot in range(2):
            cols_done(slot, which + 1, take)

    def window(slot, p):
        rows = [object_ext[b][p, pl.ds(offsets[2 * slot], TILE), :] for b in range(2)]
        shift = lax.rem(320 - offsets[2 * slot + 1], 256)
        return pltpu.roll(jnp.concatenate(rows, axis=1), shift, 1)[:, :TILE]

    views = [[window(slot, p) for p in range(4)] for slot in range(2)]
    for slot in range(2):
        o0r, o0i = views[slot][0], views[slot][2]
        for m in range(4):
            pr, pi = probe[m], probe[4 + m]
            put_field(slot, m, pr * o0r - pi * o0i, pr * o0i + pi * o0r)

    def after_first(slot, m, wr, wi):
        o1r, o1i = views[slot][1], views[slot][3]
        wave_one[slot, m, 0] = wr
        wave_one[slot, m, 1] = wi
        put_field(slot, m, wr * o1r - wi * o1i, wr * o1i + wi * o1r)

    propagate(0, after_first)
    intensity = [None, None]

    def after_second(slot, m, wr, wi):
        wave_two[slot, m, 0] = wr
        wave_two[slot, m, 1] = wi
        term = wr * wr + wi * wi
        intensity[slot] = term if m == 0 else intensity[slot] + term
        if m == 3:
            weight = jnp.where(slot < counts[0, 0], 2.0, 0.0).astype(F32)
            residual = (intensity[slot] - measured[slot]) * weight
            for k in range(4):
                put_field(slot, k, residual * wave_two[slot, k, 0], residual * wave_two[slot, k, 1])

    propagate(0, after_second)

    def add(slot, s, m, real, imag):
        for p, value in zip((s, 2 + s), (real, imag)):
            if m == 0:
                object_grad[slot, p] = value
            else:
                object_grad[slot, p] += value

    def after_third(slot, m, hr, hi):
        o1r, o1i = views[slot][1], views[slot][3]
        wr, wi = wave_one[slot, m, 0], wave_one[slot, m, 1]
        add(slot, 1, m, wr * hr + wi * hi, wr * hi - wi * hr)
        put_field(slot, m, hr * o1r + hi * o1i, hi * o1r - hr * o1i)

    propagate(2, after_third)

    def after_fourth(slot, m, hr, hi):
        o0r, o0i = views[slot][0], views[slot][2]
        pr, pi = probe[m], probe[4 + m]
        add(slot, 0, m, pr * hr + pi * hi, pr * hi - pi * hr)
        dr = hr * o0r + hi * o0i
        di = hi * o0r - hr * o0i
        if slot == 0:
            probe_grad[m] = dr
            probe_grad[4 + m] = di
        else:
            probe_grad[m] += dr
            probe_grad[4 + m] += di

    propagate(2, after_fourth)


def object_kernel(offsets, object_grad, grad_tall, cross, mate, grad_beside):
    grad_ext = (grad_tall, grad_beside)
    for total in grad_ext:
        total[...] = jnp.zeros_like(total)
    for slot in range(2):
        for p in range(4):
            value = object_grad[slot, p]
            wide = jnp.concatenate([value, jnp.zeros_like(value)], axis=1)
            wide = pltpu.roll(wide, lax.rem(offsets[2 * slot + 1] + 192, 256), 1)
            for b in range(2):
                grad_ext[b][p, pl.ds(offsets[2 * slot], TILE), :] += wide[:, block(b)]
    even = even_column()
    for s in range(2):
        to_left, to_right = pack_columns(grad_beside[s], grad_beside[2 + s])
        mate[s], cross[s] = by_parity(even, to_right, to_left)


def spread_sum(scale, shares, spread_share):
    share = jnp.sum(shares[...], axis=0) * scale
    for i in range(spread_share.shape[0]):
        spread_share[i] = share


def fold_columns_kernel(grad_tall, from_cross, from_mate, part, cross, mate):
    even, even_down = even_column(), even_row()
    for s in range(2):
        from_right, from_left = by_parity(even, from_mate[s], from_cross[s])
        for p, sides in zip((s, 2 + s), unpack_columns(from_right, from_left)):
            total = grad_tall[p] + sides
            part[p] = total[HALF:HALF + TILE]
            mate[p], cross[p] = by_parity(even_down, total[HALF + TILE:], total[:HALF])


def fold_rows_kernel(part, from_cross, from_mate, result):
    even = even_row()
    for p in range(4):
        below, above = by_parity(even, from_mate[p], from_cross[p])
        result[p, :HALF] = part[p, :HALF] + above
        result[p, HALF:] = part[p, HALF:] + below


def finish_kernel(result, gathered, result_far, probe_far, sems):
    moves = [pltpu.make_async_copy(result.at[p], result_far.at[p], sems.at[p]) for p in range(4)]
    for i in range(4):
        part = pl.ds(256 * i, 256)
        moves.append(pltpu.make_async_copy(gathered.at[part], probe_far.at[part], sems.at[4 + i]))
    for move in moves:
        move.start()
    for move in moves:
        move.wait()


def exchange(cross, mate, axes):
    count = lax.axis_size(axes)
    pairs = [(i, i + 1) for i in range(1, count - 1, 2)]
    from_cross = lax.ppermute(cross, axes, pairs + [(b, a) for a, b in pairs])
    pairs = [(i, i + 1) for i in range(0, count, 2)]
    from_mate = lax.ppermute(mate, axes, pairs + [(b, a) for a, b in pairs])
    return from_cross, from_mate


def f32(*shape):
    return jax.ShapeDtypeStruct(shape, F32)


def body(object_field, probe_modes, prop_taps, measured, offsets, counts):
    tile = object_field.reshape(4, TILE, TILE)
    planes, strip, half = f32(4, TILE, TILE), f32(2, TILE, TILE), f32(4, HALF, TILE)
    tall, tall_strip = f32(4, 2 * TILE, TILE), f32(2, 2 * TILE, TILE)

    rims = exchange(*call(rows_kernel, (half, half), [VM], tile), ROW_AXES)
    cross, mate = call(columns_kernel, (tall_strip, tall_strip), [VM] * 3, tile, *rims)
    (object_tall,) = call(tall_kernel, (tall,), [VM] * 3, tile, *rims)
    strips = exchange(cross, mate, COL_AXES)
    ops, probe, targets = call(
        operator_kernel,
        (jax.ShapeDtypeStruct((4, 512, 256), BF16), f32(8, TILE, TILE), strip), [VM, VM, VM],
        prop_taps, probe_modes.reshape(8, TILE, TILE), measured.reshape(2, TILE, TILE),
        scratch=[pltpu.VMEM((8, 2 * TILE), F32)],
    )
    probe_part, object_grad = call(
        main_kernel,
        (f32(8, TILE, TILE), f32(2, 4, TILE, TILE)), [SM, SM] + [VM] * 6,
        offsets.reshape(-1), counts.reshape(1, 1), object_tall, *strips, probe, targets, ops,
        scratch=[
            pltpu.VMEM((4, 256, TILE), F32),
            pltpu.VMEM((2, 256, 512), BF16),
            pltpu.VMEM((2, 256, 512), BF16),
            pltpu.VMEM((2, 512, 256), BF16),
            pltpu.VMEM((2, 512, 256), BF16),
            pltpu.VMEM((2, 4, 2, TILE, TILE), F32),
            pltpu.VMEM((2, 4, 2, TILE, TILE), F32),
        ],
        flops=3_200_000_000, moved=4_000_000,
    )
    grad_tall, cross, mate = call(
        object_kernel, (tall, tall_strip, tall_strip), [SM, VM],
        offsets.reshape(-1), object_grad,
        scratch=[pltpu.VMEM((4, 256, TILE), F32)],
    )

    near = lax.axis_size(NEAR_AXES)
    far = lax.axis_size(FAR_AXES)
    rows = 8 * TILE // near
    shares = lax.all_to_all(probe_part.reshape(near, rows, TILE), NEAR_AXES, 0, 0, tiled=True)
    (spread_share,) = call(
        functools.partial(spread_sum, 1.0), (f32(far, rows, TILE),), [VM], shares
    )
    strips = exchange(cross, mate, COL_AXES)
    shares = lax.all_to_all(spread_share, FAR_AXES, 0, 0, tiled=True)
    part, cross, mate = call(
        fold_columns_kernel, (planes, half, half), [VM] * 3, grad_tall, *strips
    )
    rims = exchange(cross, mate, ROW_AXES)
    (spread_share,) = call(
        functools.partial(spread_sum, 1.0 / math.sqrt(near * far)), (f32(near, rows, TILE),), [VM], shares
    )
    gathered = lax.all_to_all(spread_share, NEAR_AXES, 0, 0, tiled=True)
    (result,) = call(
        fold_rows_kernel, (planes,), [VM] * 3, part, *rims, flops=BESIDE, moved=1
    )
    result, probe_grad = call(
        finish_kernel, (planes, f32(8 * TILE, TILE)), [VM] * 2,
        result, gathered.reshape(8 * TILE, TILE),
        scratch=[pltpu.SemaphoreType.DMA((8,))], out_specs=[FAR, FAR],
    )
    return result.reshape(object_field.shape), probe_grad.reshape(probe_modes.shape)


def solution(mesh):
    fine = Mesh(mesh.devices.reshape(2, 8, 2, 4, 2, 2), ROW_AXES + COL_AXES)
    return jax.shard_map(
        body,
        mesh=fine,
        in_specs=(
            P(None, None, ROW_AXES, COL_AXES),
            P(),
            P(),
            P(ROW_AXES, COL_AXES, None, None, None),
            P(ROW_AXES, COL_AXES, None, None),
            P(ROW_AXES, COL_AXES),
        ),
        out_specs=(P(None, None, ROW_AXES, COL_AXES), P()),
        check_vma=False,
    )
```
